128 devices in a mesh: det: 2 (over z_hi), grp: 2 (over core), tm: 32 (over y, z_lo, x).
Axes of the slice: x: 4, y: 4, z: 4 (z_hi: 2, z_lo: 2; z = z_hi * 2 + z_lo), core: 2. Of those that a mesh axis runs over, the one named last changes fastest.
Arguments:
- strain: float32 [2, 2, 128, 4096], P('det', None, 'tm'), may hold values from -6 to 6
- bank: float32 [16, 2, 128, 4096], P('grp', None, 'tm'), may hold values from -64 to 64
- assignment: int32 [16], replicated, may hold values from 0 to 15, each once
- slides: int32 [4], replicated, may hold values from 0 to 524287
- bounds: int32 [7], replicated, may hold values from 49152 to 475136, as said below
- antenna: float32 [2, 2], replicated, may hold values from 0.2 to 1
Outputs:
- chi_squared: float32 [2, 16, 128, 4096], P('det', 'grp', 'tm')
- network: float32 [16, 4, 128, 4096], P('grp', 'det', 'tm')
The draws below stay inside these ranges and needn't reach their ends.
Inputs may be any that keep to these rules, and one draw needn't show every extreme that they name: `assignment`: each template index appears once. `bounds`: strictly rising; bound j lies within 16384 of (j + 1) * 65536.
All inputs are finite; a program needn't handle non-finite values.
Results may differ from the reference program's by a relative error of at most 0.0003.
Values sent between devices are 32-bit elements; how exact they have to be, the bound alone decides.
A program may use at most 128 MiB of HBM per device.

```python
import math
import jax
import jax.numpy as jnp
from jax import lax

FOLD = 128
BANDS = 8
SLIDES = 4
DETECTORS = 2
TEMPL = 16
BINS = 524288
COLS = 4096
RADIX = 512
SPLIT = 8
N_DET = 2


def draw_bank(key, part):
    key = jax.random.fold_in(key, 11)
    shape = (TEMPL, 2, FOLD, COLS)
    rows = lax.broadcasted_iota(jnp.int32, shape, 2)
    cols = lax.broadcasted_iota(jnp.int32, shape, 3)
    place = (cols + COLS * rows).astype(jnp.float32) / BINS
    envelope = (place + 0.05) ** (-0.6)
    noise = jax.random.normal(key, shape, jnp.float32)
    return envelope * noise


def draw_bounds(key, part):
    key = jax.random.fold_in(key, 23)
    width = BINS // BANDS
    reach = width // 4
    offsets = jax.random.randint(key, (BANDS - 1,), -reach, reach + 1)
    return (jnp.arange(1, BANDS, dtype=jnp.int32) * width + offsets).astype(jnp.int32)


def touch_ends(values, key, low, largest):
    shape = values.shape
    spot = [jax.random.randint(jax.random.fold_in(key, axis), (), 0, shape[axis]) for axis in range(len(shape))]
    values = values.at[tuple(spot)].set(low)
    longest = shape.index(max(shape))
    spot[longest] = (spot[longest] + 1) % shape[longest]
    return values.at[tuple(spot)].set(largest)


def shard_levels(rng, shape, shards, least, top_value):
    gain = 1.0
    for dim, blocks in shards:
        heights = jax.random.uniform(jax.random.fold_in(jax.random.fold_in(rng, 6), dim), (blocks,), jnp.float32, least / len(shards), top_value / len(shards))
        gain = gain * jnp.repeat(jnp.exp(heights), shape[dim] // blocks).reshape((-1,) + (1,) * (len(shape) - 1 - dim))
    return gain


def centred(key, dims, deviation, most, split=(), kind=jnp.bfloat16):
    level = shard_levels(key, dims, split, -0.22, 0.18) if split else 1.0
    drawn = jax.random.normal(key, dims, jnp.float32) * deviation * level
    return jnp.minimum(jnp.maximum(drawn, -most), most).astype(kind)


def setup_inputs(seed: int = 0) -> dict:
    splits = jax.random.split(jax.random.key(seed), 7)
    return {
        "strain": centred(splits[0], (DETECTORS, 2, FOLD, COLS), 1.0, 6.0, ((0, 2), (2, 32)), jnp.float32),
        "bank": draw_bank(jax.random.fold_in(splits[6], 71), 0),
        "assignment": jax.random.permutation(splits[2], TEMPL).astype(jnp.int32),
        "slides": touch_ends(jax.random.randint(splits[3], (SLIDES,), 0, BINS), jax.random.fold_in(splits[3], 1), 0, BINS - 1).astype(jnp.int32),
        "bounds": draw_bounds(jax.random.fold_in(splits[6], 71), 0),
        "antenna": jnp.clip(jax.random.uniform(splits[5], (DETECTORS, 2), jnp.float32, 0.2, 1.0), 0.2, 1.0),
    }


def slide_phase(index, shift, total):
    first = shift % total
    second = first * 128 % total
    third = second * 128 % total
    lowest = index % 128
    middle = index // 128 % 128
    upper = index // 16384
    summed = lowest * first % total + middle * second % total + upper * third % total
    return (summed % total).astype(jnp.float32) * (2.0 * math.pi / total)

def fold_order(series):
    lead = series.shape[:-1]
    grid = series.reshape(lead + (COLS, FOLD))
    grid = jnp.swapaxes(grid, -1, -2)
    grid = grid.reshape(lead + (FOLD, RADIX, SPLIT))
    grid = jnp.swapaxes(grid, -1, -2)
    return grid.reshape(lead + (FOLD, COLS))

def inverse(spectrum):
    return jnp.fft.ifft(spectrum, axis=-1) * BINS

def reference(strain, bank, assignment, slides, bounds, antenna):
    spectra = (strain[:, 0] + 1j * strain[:, 1]).reshape(N_DET, BINS)
    chosen = bank[assignment]
    positions = jnp.arange(BINS, dtype=jnp.int32)
    band_index = lax.optimization_barrier(jnp.sum((positions[None, :] >= bounds[:, None]).astype(jnp.int32), axis=0))
    levels = jnp.arange(BANDS, dtype=jnp.int32)
    masks = (band_index[None, :] == levels[:, None]).astype(jnp.float32)
    angle = slide_phase(positions[None, :], slides[:, None], BINS)
    rotate = jnp.cos(angle) + 1j * jnp.sin(angle)
    weight_one = antenna[0, 0] + 1j * antenna[0, 1]
    weight_two = antenna[1, 0] + 1j * antenna[1, 1]
    response = jnp.sum(antenna * antenna)

    def one_template(template):
        wave = (template[0] + 1j * template[1]).reshape(BINS)
        power = (template[0] * template[0] + template[1] * template[1]).reshape(BINS)
        band_power = lax.optimization_barrier(jnp.sum(masks * power[None, :], axis=1))
        total = jnp.sum(band_power)
        share = band_power / total
        scale = 1.0 / jnp.sqrt(total)
        product = spectra * jnp.conj(wave)[None, :]
        bands = inverse(product[:, None, :] * masks[None]) * scale
        whole = lax.optimization_barrier(jnp.sum(bands, axis=1))
        gap = bands - share[None, :, None] * whole[:, None, :]
        chi = lax.optimization_barrier(jnp.sum((gap.real * gap.real + gap.imag * gap.imag) / share[None, :, None], axis=1)) / (2 * BANDS - 2)
        network_input = weight_one * product[0][None, :] + weight_two * product[1][None, :] * rotate
        series = inverse(network_input)
        net = (series.real * series.real + series.imag * series.imag) * (scale * scale) / response
        return (fold_order(chi), fold_order(net))
    chi_all, net_all = lax.map(one_template, chosen)
    return (jnp.swapaxes(chi_all, 0, 1), net_all)
```

```python
import math

import jax
import jax.numpy as jnp
import numpy as np
from jax import lax
from jax.experimental import pallas as pl
from jax.experimental.pallas import tpu as pltpu

FOLD = 128
COLS = 4096
BINS = FOLD * COLS
BANDS = 8
CHUNK = 512
STEPS = COLS // CHUNK
LANES = 128
OUT_ROWS = 32
SPACED = True


def rows_of(part):
    tau = np.arange(OUT_ROWS)
    return 4 * tau + part if SPACED else 32 * part + tau


def halves(table):
    high = np.asarray(table, np.float32).astype(jnp.bfloat16)
    low = (np.asarray(table, np.float64) - high.astype(np.float64)).astype(np.float32)
    return high, low.astype(jnp.bfloat16)


def pack_columns(real, imag):
    m = real.shape[0]
    xp = np if isinstance(real, np.ndarray) else jnp
    parts = xp.stack([real.reshape(m, 32, 4), imag.reshape(m, 32, 4)], axis=2)
    return parts.reshape(m, 256)


def stacked_rows(cos, sin, xp=np):
    top = pack_columns(cos, -sin)
    bottom = pack_columns(sin, cos)
    return xp.concatenate([top, bottom], axis=0)


def constant_tables():
    b = np.arange(FOLD)
    even, odd, twiddle = [], [], []
    for part in range(4):
        e = rows_of(part)
        angle = 2 * np.pi * ((e[:, None] * b[None, :]) % FOLD) / FOLD
        cos, sin = np.cos(angle), np.sin(angle)
        for parity, group in ((0, even), (1, odd)):
            blocks = []
            for band in range(parity, BANDS, 2):
                inside = (b >= 16 * band - 8) & (b < 16 * band + 24)
                blocks.append(stacked_rows(cos * inside, sin * inside))
            group.append(np.concatenate(blocks, axis=0))
        a = np.arange(COLS)
        angle = 2 * np.pi * (e[:, None] * a[None, :]) / BINS
        twiddle.append(np.stack([np.cos(angle), np.sin(angle)]))
    even = halves(np.stack(even))
    odd = halves(np.stack(odd))
    bands = np.stack([even[0], even[1], odd[0], odd[1]], axis=1)
    twiddle = np.stack(twiddle).astype(np.float32)
    a1 = np.arange(LANES)
    q2 = np.arange(32)
    angle = 2 * np.pi * (a1[None, :] * q2[:, None]) / COLS
    inner = np.stack([np.cos(angle), np.sin(angle)]).astype(np.float32)
    angle = 2 * np.pi * ((a1[:, None] * a1[None, :]) % LANES) / LANES
    cos, sin = np.cos(angle), np.sin(angle)
    last = np.stack(halves(np.block([[cos, sin], [-sin, cos]])))
    place = np.zeros((512, 512), np.float32)
    u1, u2 = np.meshgrid(np.arange(128), np.arange(4), indexing="ij")
    place[(u2 * 128 + u1).ravel(), (u2 + 4 * u1).ravel()] = 1.0
    return bands, twiddle, inner, last, place.astype(jnp.bfloat16)


def split_two(x):
    high = x.astype(jnp.bfloat16)
    low = (x - high.astype(jnp.float32)).astype(jnp.bfloat16)
    return high, low


def mm(a, b):
    return jnp.dot(a, b, preferred_element_type=jnp.float32)


ROOT = math.sqrt(0.5)


def eight(x):
    def add(p, q):
        return (p[0] + q[0], p[1] + q[1])

    def sub(p, q):
        return (p[0] - q[0], p[1] - q[1])

    def turn(p):
        return (-p[1], p[0])

    def addi(p, q):
        return (p[0] - q[1], p[1] + q[0])

    def subi(p, q):
        return (p[0] + q[1], p[1] - q[0])

    def four(z):
        s02, d02 = add(z[0], z[2]), sub(z[0], z[2])
        s13, d13 = add(z[1], z[3]), sub(z[1], z[3])
        return [add(s02, s13), addi(d02, d13), sub(s02, s13), subi(d02, d13)]

    ev = four([x[0], x[2], x[4], x[6]])
    od = four([x[1], x[3], x[5], x[7]])
    o1 = ((od[1][0] - od[1][1]) * ROOT, (od[1][0] + od[1][1]) * ROOT)
    o3 = ((od[3][0] + od[3][1]) * ROOT, (od[3][1] - od[3][0]) * ROOT)
    return [
        add(ev[0], od[0]),
        add(ev[1], o1),
        addi(ev[2], od[2]),
        sub(ev[3], o3),
        sub(ev[0], od[0]),
        sub(ev[1], o1),
        subi(ev[2], od[2]),
        add(ev[3], o3),
    ]


def four_point(z):
    s0 = (z[0][0] + z[2][0], z[0][1] + z[2][1])
    d0 = (z[0][0] - z[2][0], z[0][1] - z[2][1])
    s1 = (z[1][0] + z[3][0], z[1][1] + z[3][1])
    d1 = (z[1][0] - z[3][0], z[1][1] - z[3][1])
    return [
        (s0[0] + s1[0], s0[1] + s1[1]),
        (d0[0] - d1[1], d0[1] + d1[0]),
        (s0[0] - s1[0], s0[1] - s1[1]),
        (d0[0] + d1[1], d0[1] - d1[0]),
    ]


def times(x, c, s):
    return (x[0] * c - x[1] * s, x[0] * s + x[1] * c)


def swap_halves(x):
    rows, width = x.shape
    return pltpu.roll(x.reshape(rows // 8, 8, width), 4, 1).reshape(rows, width)


def kernel(
    where_ref, bounds_ref, tmpl_ref, own_ref, oth_ref, bands_ref, net_ref, twiddle_ref, ramp_ref,
    inner_ref, last_ref, place_ref, response_ref, out_ref,
    series, net_oth, xe, xo, xn, power, zbuf, bbuf, vbuf,
):
    step = pl.program_id(0)
    start = step * CHUNK

    @pl.when(step == 0)
    def _():
        power[...] = jnp.zeros_like(power)

    sub = lax.broadcasted_iota(jnp.int32, (16, CHUNK), 0)
    lane = lax.broadcasted_iota(jnp.int32, (16, CHUNK), 1)
    top = (sub & 7) < 4
    place_in = ((sub >> 3) * 4 + (sub & 3)) * COLS + lane + start
    for group in range(16):
        rows = slice(16 * group, 16 * group + 16)
        wave = tmpl_ref[rows, :]
        rolled = swap_halves(wave)
        wave_re = jnp.where(top, wave, rolled)
        wave_im = jnp.where(top, rolled, -wave)
        own = own_ref[0, rows, :]
        own = own * wave_re + swap_halves(own) * wave_im
        oth = oth_ref[0, rows, :]
        oth = oth * wave_re + swap_halves(oth) * wave_im
        bound = (group - 1) // 2
        upper = (place_in + 8 * group * COLS) >= bounds_ref[bound + 1]
        even = upper if bound % 2 else jnp.logical_not(upper)
        squares = wave * wave
        low_sum = jnp.where(upper, 0.0, squares)
        fold = lambda v: sum(
            v[r : r + 8, c : c + LANES] for r in (0, 8) for c in range(0, CHUNK, LANES)
        )
        power[2 * group] += fold(low_sum)
        power[2 * group + 1] += fold(squares)
        high = own.astype(jnp.bfloat16).astype(jnp.float32)
        low = own - high
        xe[0, rows, :] = jnp.where(even, high, 0.0).astype(jnp.bfloat16)
        xe[1, rows, :] = jnp.where(even, low, 0.0).astype(jnp.bfloat16)
        xo[0, rows, :] = jnp.where(even, 0.0, high).astype(jnp.bfloat16)
        xo[1, rows, :] = jnp.where(even, 0.0, low).astype(jnp.bfloat16)
        high, low = split_two(oth)
        xn[0, rows, :] = high
        xn[1, rows, :] = low
    cols = pl.ds(pl.multiple_of(start, CHUNK), CHUNK)

    def three(high, low, x):
        return mm(high, x[0]) + mm(low, x[0]) + mm(high, x[1])

    series[0:256, cols] = three(bands_ref[0, 0], bands_ref[0, 1], xe)
    series[256:512, cols] = three(bands_ref[0, 2], bands_ref[0, 3], xo)
    series[512:640, cols] = three(net_ref[0, 0], net_ref[0, 1], xe) + three(net_ref[0, 0], net_ref[0, 1], xo)
    net_oth[:, cols] = three(net_ref[1, 0], net_ref[1, 1], xn)

    @pl.when(step == STEPS - 1)
    def _():
        total = jnp.zeros((1, 1), jnp.float32)
        powers = []
        for band in range(BANDS):
            acc = jnp.zeros((8, LANES), jnp.float32)
            for group in range(16):
                bound = (group - 1) // 2
                if bound == band:
                    acc += power[2 * group]
                if bound + 1 == band:
                    acc += power[2 * group + 1] - power[2 * group]
            value = jnp.sum(jnp.sum(acc, axis=0, keepdims=True), axis=1, keepdims=True)
            powers.append(value)
            total = total + value
        shares = [value / total for value in powers]
        inverse = [(1.0 / (2 * BANDS - 2)) / (total * share) for share in shares]
        net_scale = 1.0 / (total * response_ref[0])

        def block(eb, carry):
            first = pl.multiple_of(eb * 8, 8)
            erows = pl.ds(first, 8)

            def load(item, a2):
                columns = slice(a2 * LANES, (a2 + 1) * LANES)
                if item < 8:
                    base = (item // 2) * 64 + (item % 2) * 256
                    re = series[pl.ds(base + first, 8), columns]
                    im = series[pl.ds(base + 32 + first, 8), columns]
                else:
                    slide = item - 8
                    base = 512 + 64 * slide
                    own = (series[pl.ds(base + first, 8), columns], series[pl.ds(base + 32 + first, 8), columns])
                    base = 64 * slide
                    oth = (net_oth[pl.ds(base + first, 8), columns], net_oth[pl.ds(base + 32 + first, 8), columns])
                    own = times(own, ramp_ref[slide, 0:1, columns], ramp_ref[slide, 1:2, columns])
                    oth = times(oth, ramp_ref[slide, 2:3, columns], ramp_ref[slide, 3:4, columns])
                    re, im = own[0] + oth[0], own[1] + oth[1]
                return times((re, im), twiddle_ref[0, 0, erows, columns], twiddle_ref[0, 1, erows, columns])

            for item in range(10):
                slot = item % 2
                halfway = []
                for r2 in range(4):
                    values = eight([load(item, 4 * s + r2) for s in range(8)])
                    turned = []
                    for v in range(8):
                        if r2 * v == 0:
                            turned.append(values[v])
                        else:
                            angle = 2 * math.pi * r2 * v / 32
                            turned.append(times(values[v], math.cos(angle), math.sin(angle)))
                    halfway.append(turned)
                for v in range(8):
                    done = four_point([halfway[r2][v] for r2 in range(4)])
                    for u2 in range(4):
                        q2 = v + 8 * u2
                        z = times(done[u2], inner_ref[0, q2 : q2 + 1, :], inner_ref[1, q2 : q2 + 1, :])
                        zbuf[slot, q2 * 8 : q2 * 8 + 8, 0:LANES] = z[0]
                        zbuf[slot, q2 * 8 : q2 * 8 + 8, LANES : 2 * LANES] = z[1]
                high, low = split_two(zbuf[slot])
                bbuf[item] = mm(high, last_ref[0]) + mm(low, last_ref[0]) + mm(high, last_ref[1])
            for q2 in range(32):
                rows = slice(q2 * 8, q2 * 8 + 8)
                v, u2 = q2 % 8, q2 // 8
                at = (slice(v * 8, v * 8 + 8), slice(u2 * LANES, (u2 + 1) * LANES))
                re = [bbuf[band, rows, 0:LANES] for band in range(BANDS)]
                im = [bbuf[band, rows, LANES : 2 * LANES] for band in range(BANDS)]
                whole_re, whole_im = sum(re), sum(im)
                chi = jnp.zeros((8, LANES), jnp.float32)
                for band in range(BANDS):
                    gap_re = re[band] - shares[band] * whole_re
                    gap_im = im[band] - shares[band] * whole_im
                    chi = chi + (gap_re * gap_re + gap_im * gap_im) * inverse[band]
                vbuf[0, at[0], at[1]] = chi
                for slide in range(2):
                    re = bbuf[8 + slide, rows, 0:LANES]
                    im = bbuf[8 + slide, rows, LANES : 2 * LANES]
                    vbuf[1 + slide, at[0], at[1]] = (re * re + im * im) * net_scale
            for kind in range(3):
                high, low = split_two(vbuf[kind])
                done = mm(high, place_ref[...]) + mm(low, place_ref[...])
                for v in range(8):
                    out_ref[kind, erows, v * 512 : (v + 1) * 512] = done[v * 8 : v * 8 + 8, :]
            return carry

        lax.fori_loop(0, OUT_ROWS // 8, block, 0)


def filter_rows(part, det, tmpl, strain, bounds, net_tables, ramp, response):
    bands, twiddle, inner, last, place = constant_tables()
    where = jnp.stack([part, det]).astype(jnp.int32)
    edges = jnp.concatenate([jnp.zeros((1,), jnp.int32), bounds, jnp.full((1,), BINS, jnp.int32)])
    one = pl.Buffered(1)
    spec = pltpu.PrefetchScalarGridSpec(
        num_scalar_prefetch=2,
        grid=(STEPS,),
        in_specs=[
            pl.BlockSpec((256, CHUNK), lambda i, w, e: (0, i)),
            pl.BlockSpec((1, 256, CHUNK), lambda i, w, e: (w[1], 0, i)),
            pl.BlockSpec((1, 256, CHUNK), lambda i, w, e: (1 - w[1], 0, i)),
            pl.BlockSpec((1, 4, 256, 256), lambda i, w, e: (w[0], 0, 0, 0), pipeline_mode=one),
            pl.BlockSpec((2, 2, 128, 256), lambda i, w, e: (0, 0, 0, 0), pipeline_mode=one),
            pl.BlockSpec((1, 2, OUT_ROWS, COLS), lambda i, w, e: (w[0], 0, 0, 0), pipeline_mode=one),
            pl.BlockSpec((2, 4, COLS), lambda i, w, e: (0, 0, 0), pipeline_mode=one),
            pl.BlockSpec((2, 32, LANES), lambda i, w, e: (0, 0, 0), pipeline_mode=one),
            pl.BlockSpec((2, 256, 256), lambda i, w, e: (0, 0, 0), pipeline_mode=one),
            pl.BlockSpec((512, 512), lambda i, w, e: (0, 0), pipeline_mode=one),
            pl.BlockSpec(memory_space=pltpu.SMEM),
        ],
        out_specs=pl.BlockSpec((3, OUT_ROWS, COLS), lambda i, w, e: (0, 0, 0), pipeline_mode=one),
        scratch_shapes=[
            pltpu.VMEM((640, COLS), jnp.float32),
            pltpu.VMEM((128, COLS), jnp.float32),
            pltpu.VMEM((2, 256, CHUNK), jnp.bfloat16),
            pltpu.VMEM((2, 256, CHUNK), jnp.bfloat16),
            pltpu.VMEM((2, 256, CHUNK), jnp.bfloat16),
            pltpu.VMEM((32, 8, LANES), jnp.float32),
            pltpu.VMEM((2, 256, 256), jnp.float32),
            pltpu.VMEM((10, 256, 256), jnp.float32),
            pltpu.VMEM((3, 64, 512), jnp.float32),
        ],
    )
    return pl.pallas_call(
        kernel,
        grid_spec=spec,
        out_shape=jax.ShapeDtypeStruct((3, OUT_ROWS, COLS), jnp.float32),
        compiler_params=pltpu.CompilerParams(vmem_limit_bytes=48 * 2**20),
        cost_estimate=pl.CostEstimate(flops=20 * 10**9, bytes_accessed=20 * 10**6, transcendentals=0),
    )(
        where, edges, tmpl, strain, strain, jnp.asarray(bands), net_tables, jnp.asarray(twiddle), ramp,
        jnp.asarray(inner), jnp.asarray(last), jnp.asarray(place), response,
    )


def dynamic_tables(part, det, slides_mine, antenna):
    tau = jnp.arange(OUT_ROWS, dtype=jnp.int32)
    e = 4 * tau + part if SPACED else 32 * part + tau
    b = jnp.arange(FOLD, dtype=jnp.int32)
    a = jnp.arange(COLS, dtype=jnp.int32)

    def unit(index, total):
        angle = (index % total).astype(jnp.float32) * (2.0 * math.pi / total)
        return jnp.cos(angle), jnp.sin(angle)

    tables, ramps = [], []
    for which in (det, 1 - det):
        moving = which == 1
        weight_re, weight_im = antenna[which, 0], antenna[which, 1]
        rows, cols = [], []
        for slide in range(2):
            shift = jnp.where(moving, slides_mine[slide], 0)
            cos, sin = unit((e[:, None] + shift % FOLD) * b[None, :], FOLD)
            re = weight_re * cos - weight_im * sin
            im = weight_re * sin + weight_im * cos
            rows.append(stacked_rows(re, im, jnp))
            cols.append(jnp.stack(unit(a * shift, BINS)))
        table = jnp.concatenate(rows, axis=0)
        high = lax.reduce_precision(table, 8, 7)
        tables.append(jnp.stack([high.astype(jnp.bfloat16), (table - high).astype(jnp.bfloat16)]))
        ramps.append(jnp.stack(cols))
    return jnp.stack(tables), jnp.concatenate(ramps, axis=1)


def on_device(strain, bank, assignment, slides, bounds, antenna):
    tm = lax.axis_index("tm")
    det = lax.axis_index("det")
    grp = lax.axis_index("grp")
    packed = bank.reshape(8, 8, COLS)
    both = lax.all_gather(packed, "grp", axis=0, tiled=True)
    mine = lax.dynamic_slice_in_dim(assignment, grp * 8, 8)
    chosen = jnp.take(both, jnp.repeat(mine, 4), axis=0)
    tmpl = lax.all_to_all(chosen, "tm", split_axis=0, concat_axis=0, tiled=True)
    signal = lax.all_gather(strain.reshape(8, COLS), ("det", "tm"), axis=0, tiled=False)
    part = tm % 4
    mine = lax.dynamic_slice_in_dim(slides, det * 2, 2)
    net_tables, ramp = dynamic_tables(part, det, mine, antenna)
    rows = filter_rows(
        part, det, tmpl.reshape(256, COLS), signal.reshape(2, 256, COLS), bounds, net_tables, ramp,
        jnp.sum(antenna * antenna)[None],
    )
    sent = lax.all_to_all(jnp.swapaxes(rows, 0, 1), "tm", split_axis=0, concat_axis=0, tiled=True)
    sent = sent.reshape(8, 4, 3, COLS)
    return sent[None, :, :, 0], jnp.swapaxes(sent[:, :, 1:], 1, 2)


def solution(mesh):
    P = jax.sharding.PartitionSpec
    return jax.shard_map(
        on_device,
        mesh=mesh,
        in_specs=(P("det", None, "tm", None), P("grp", None, "tm", None), P(), P(), P(), P()),
        out_specs=(P("det", "grp", "tm", None), P("grp", "det", "tm", None)),
        check_vma=False,
    )
```

```python
import math

import jax
import jax.numpy as jnp
import numpy as np
from jax import lax
from jax.experimental import pallas as pl
from jax.experimental.pallas import tpu as pltpu

FOLD = 128
COLS = 4096
BINS = FOLD * COLS
BANDS = 8
CHUNK = 512
STEPS = COLS // CHUNK
LANES = 128
OUT_ROWS = 32


def rows_of(part):
    tau = np.arange(OUT_ROWS)
    return OUT_ROWS * part + tau


def halves(table):
    high = np.asarray(table, np.float32).astype(jnp.bfloat16)
    low = (np.asarray(table, np.float64) - high.astype(np.float64)).astype(np.float32)
    return high, low.astype(jnp.bfloat16)


def pack_columns(real, imag):
    m = real.shape[0]
    parts = np.stack([real.reshape(m, 32, 4), imag.reshape(m, 32, 4)], axis=2)
    return parts.reshape(m, 256)


def stacked_rows(cos, sin):
    top = pack_columns(cos, -sin)
    bottom = pack_columns(sin, cos)
    return np.concatenate([top, bottom], axis=0)


def constant_tables():
    b = np.arange(FOLD)
    even, odd, twiddle = [], [], []
    for part in range(4):
        e = rows_of(part)
        angle = 2 * np.pi * ((e[:, None] * b[None, :]) % FOLD) / FOLD
        cos, sin = np.cos(angle), np.sin(angle)
        for parity, group in ((0, even), (1, odd)):
            blocks = []
            for band in range(parity, BANDS, 2):
                inside = (b >= 16 * band - 8) & (b < 16 * band + 24)
                blocks.append(stacked_rows(cos * inside, sin * inside))
            group.append(np.concatenate(blocks, axis=0))
        a = np.arange(COLS)
        angle = 2 * np.pi * (e[:, None] * a[None, :]) / BINS
        twiddle.append(np.stack([np.cos(angle), np.sin(angle)]))
    even = halves(np.stack(even))
    odd = halves(np.stack(odd))
    bands = np.stack([even[0], even[1], odd[0], odd[1]], axis=1)
    twiddle = np.stack(twiddle).astype(np.float32)
    a1 = np.arange(LANES)
    q2 = np.arange(32)
    angle = 2 * np.pi * (a1[None, :] * q2[:, None]) / COLS
    inner = np.stack([np.cos(angle), np.sin(angle)]).astype(np.float32)
    angle = 2 * np.pi * ((a1[:, None] * a1[None, :]) % LANES) / LANES
    cos, sin = np.cos(angle), np.sin(angle)
    last = np.stack(halves(np.block([[cos, sin], [-sin, cos]])))
    place = np.zeros((512, 512), np.float32)
    u1, u2 = np.meshgrid(np.arange(128), np.arange(4), indexing="ij")
    place[(u2 * 128 + u1).ravel(), (u2 + 4 * u1).ravel()] = 1.0
    return bands, twiddle, inner, last, place.astype(jnp.bfloat16)


def split_two(x):
    high = x.astype(jnp.bfloat16)
    low = (x - high.astype(jnp.float32)).astype(jnp.bfloat16)
    return high, low


def mm(a, b):
    return jnp.dot(a, b, preferred_element_type=jnp.float32)


ROOT = math.sqrt(0.5)


def eight(x):
    def add(p, q):
        return (p[0] + q[0], p[1] + q[1])

    def sub(p, q):
        return (p[0] - q[0], p[1] - q[1])

    def turn(p):
        return (-p[1], p[0])

    def addi(p, q):
        return (p[0] - q[1], p[1] + q[0])

    def subi(p, q):
        return (p[0] + q[1], p[1] - q[0])

    def four(z):
        s02, d02 = add(z[0], z[2]), sub(z[0], z[2])
        s13, d13 = add(z[1], z[3]), sub(z[1], z[3])
        return [add(s02, s13), addi(d02, d13), sub(s02, s13), subi(d02, d13)]

    ev = four([x[0], x[2], x[4], x[6]])
    od = four([x[1], x[3], x[5], x[7]])
    o1 = ((od[1][0] - od[1][1]) * ROOT, (od[1][0] + od[1][1]) * ROOT)
    o3 = ((od[3][0] + od[3][1]) * ROOT, (od[3][1] - od[3][0]) * ROOT)
    return [
        add(ev[0], od[0]),
        add(ev[1], o1),
        addi(ev[2], od[2]),
        sub(ev[3], o3),
        sub(ev[0], od[0]),
        sub(ev[1], o1),
        subi(ev[2], od[2]),
        add(ev[3], o3),
    ]


def four_point(z):
    s0 = (z[0][0] + z[2][0], z[0][1] + z[2][1])
    d0 = (z[0][0] - z[2][0], z[0][1] - z[2][1])
    s1 = (z[1][0] + z[3][0], z[1][1] + z[3][1])
    d1 = (z[1][0] - z[3][0], z[1][1] - z[3][1])
    return [
        (s0[0] + s1[0], s0[1] + s1[1]),
        (d0[0] - d1[1], d0[1] + d1[0]),
        (s0[0] - s1[0], s0[1] - s1[1]),
        (d0[0] + d1[1], d0[1] - d1[0]),
    ]


def times(x, c, s):
    return (x[0] * c - x[1] * s, x[0] * s + x[1] * c)


def swap_halves(x):
    rows, width = x.shape
    return pltpu.roll(x.reshape(rows // 8, 8, width), 4, 1).reshape(rows, width)


def kernel(
    where_ref, bounds_ref, tmpl_ref, own_ref, oth_ref, bands_ref, twiddle_ref,
    inner_ref, last_ref, place_ref, slides_ref, antenna_ref, out_ref,
    net_ref, ramp_ref, series, net_oth, xe, xo, xn, power, zbuf, bbuf, vbuf,
):
    step = pl.program_id(0)
    start = step * CHUNK

    @pl.when(step == 0)
    def _():
        power[...] = jnp.zeros_like(power)
        part, det = where_ref[0], where_ref[1]
        column = (
            lax.broadcasted_iota(jnp.int32, (32, LANES), 0) * LANES
            + lax.broadcasted_iota(jnp.int32, (32, LANES), 1)
        )
        row = lax.broadcasted_iota(jnp.int32, (OUT_ROWS, 256), 0) + OUT_ROWS * part
        packed = lax.broadcasted_iota(jnp.int32, (OUT_ROWS, 256), 1)
        bin_row = (packed >> 3) * 4 + (packed & 3)
        quarter = ((packed >> 2) & 1) * (FOLD // 4)
        for side in range(2):
            which = det if side == 0 else 1 - det
            weight_re, weight_im = antenna_ref[which, 0], antenna_ref[which, 1]
            for slide in range(2):
                shift = which * slides_ref[2 * det + slide]
                angle = (((row + shift) * bin_row + quarter) & (FOLD - 1)).astype(jnp.float32) * (2.0 * math.pi / FOLD)
                for half, table in ((0, jnp.cos(angle)), (1, jnp.sin(angle))):
                    high, low = split_two(table)
                    at = slice(64 * slide + 32 * half, 64 * slide + 32 * half + 32)
                    net_ref[side, 0, at, :] = high
                    net_ref[side, 1, at, :] = low
                angle = ((column * shift) & (BINS - 1)).astype(jnp.float32) * (2.0 * math.pi / BINS)
                cos, sin = jnp.cos(angle), jnp.sin(angle)
                ramp_ref[slide, 2 * side] = weight_re * cos - weight_im * sin
                ramp_ref[slide, 2 * side + 1] = weight_re * sin + weight_im * cos

    sub = lax.broadcasted_iota(jnp.int32, (16, CHUNK), 0)
    lane = lax.broadcasted_iota(jnp.int32, (16, CHUNK), 1)
    top = (sub & 7) < 4
    place_in = ((sub >> 3) * 4 + (sub & 3)) * COLS + lane + start
    for group in range(16):
        rows = slice(16 * group, 16 * group + 16)
        wave = tmpl_ref[rows, :]
        rolled = swap_halves(wave)
        wave_re = jnp.where(top, wave, rolled)
        wave_im = jnp.where(top, rolled, -wave)
        own = own_ref[0, rows, :]
        own = own * wave_re + swap_halves(own) * wave_im
        oth = oth_ref[0, rows, :]
        oth = oth * wave_re + swap_halves(oth) * wave_im
        bound = (group - 1) // 2
        upper = (place_in + 8 * group * COLS) >= bounds_ref[bound + 1]
        even = upper if bound % 2 else jnp.logical_not(upper)
        squares = wave * wave
        low_sum = jnp.where(upper, 0.0, squares)
        fold = lambda v: sum(
            v[r : r + 8, c : c + LANES] for r in (0, 8) for c in range(0, CHUNK, LANES)
        )
        power[2 * group] += fold(low_sum)
        power[2 * group + 1] += fold(squares)
        high = own.astype(jnp.bfloat16).astype(jnp.float32)
        low = own - high
        xe[0, rows, :] = jnp.where(even, high, 0.0).astype(jnp.bfloat16)
        xe[1, rows, :] = jnp.where(even, low, 0.0).astype(jnp.bfloat16)
        xo[0, rows, :] = jnp.where(even, 0.0, high).astype(jnp.bfloat16)
        xo[1, rows, :] = jnp.where(even, 0.0, low).astype(jnp.bfloat16)
        high, low = split_two(oth)
        xn[0, rows, :] = high
        xn[1, rows, :] = low
    cols = pl.ds(pl.multiple_of(start, CHUNK), CHUNK)

    def three(high, low, x):
        return mm(high, x[0]) + mm(low, x[0]) + mm(high, x[1])

    series[0:256, cols] = three(bands_ref[0, 0], bands_ref[0, 1], xe)
    series[256:512, cols] = three(bands_ref[0, 2], bands_ref[0, 3], xo)
    series[512:640, cols] = three(net_ref[0, 0], net_ref[0, 1], xe) + three(net_ref[0, 0], net_ref[0, 1], xo)
    net_oth[:, cols] = three(net_ref[1, 0], net_ref[1, 1], xn)

    @pl.when(step == STEPS - 1)
    def _():
        total = jnp.zeros((1, 1), jnp.float32)
        powers = []
        for band in range(BANDS):
            acc = jnp.zeros((8, LANES), jnp.float32)
            for group in range(16):
                bound = (group - 1) // 2
                if bound == band:
                    acc += power[2 * group]
                if bound + 1 == band:
                    acc += power[2 * group + 1] - power[2 * group]
            value = jnp.sum(jnp.sum(acc, axis=0, keepdims=True), axis=1, keepdims=True)
            powers.append(value)
            total = total + value
        shares = [value / total for value in powers]
        inverse = [(1.0 / (2 * BANDS - 2)) / (total * share) for share in shares]
        response = sum(antenna_ref[d, c] * antenna_ref[d, c] for d in range(2) for c in range(2))
        net_scale = 1.0 / (total * response)

        def block(eb, carry):
            first = pl.multiple_of(eb * 8, 8)
            erows = pl.ds(first, 8)

            def load(item, a2):
                columns = slice(a2 * LANES, (a2 + 1) * LANES)
                if item < 8:
                    base = (item // 2) * 64 + (item % 2) * 256
                    re = series[pl.ds(base + first, 8), columns]
                    im = series[pl.ds(base + 32 + first, 8), columns]
                else:
                    slide = item - 8
                    base = 512 + 64 * slide
                    own = (series[pl.ds(base + first, 8), columns], series[pl.ds(base + 32 + first, 8), columns])
                    base = 64 * slide
                    oth = (net_oth[pl.ds(base + first, 8), columns], net_oth[pl.ds(base + 32 + first, 8), columns])
                    own = times(own, ramp_ref[slide, 0, a2 : a2 + 1, :], ramp_ref[slide, 1, a2 : a2 + 1, :])
                    oth = times(oth, ramp_ref[slide, 2, a2 : a2 + 1, :], ramp_ref[slide, 3, a2 : a2 + 1, :])
                    re, im = own[0] + oth[0], own[1] + oth[1]
                return times((re, im), twiddle_ref[0, 0, erows, columns], twiddle_ref[0, 1, erows, columns])

            for item in range(10):
                slot = item % 2
                halfway = []
                for r2 in range(4):
                    values = eight([load(item, 4 * s + r2) for s in range(8)])
                    turned = []
                    for v in range(8):
                        if r2 * v == 0:
                            turned.append(values[v])
                        else:
                            angle = 2 * math.pi * r2 * v / 32
                            turned.append(times(values[v], math.cos(angle), math.sin(angle)))
                    halfway.append(turned)
                for v in range(8):
                    done = four_point([halfway[r2][v] for r2 in range(4)])
                    for u2 in range(4):
                        q2 = v + 8 * u2
                        z = times(done[u2], inner_ref[0, q2 : q2 + 1, :], inner_ref[1, q2 : q2 + 1, :])
                        zbuf[slot, q2 * 8 : q2 * 8 + 8, 0:LANES] = z[0]
                        zbuf[slot, q2 * 8 : q2 * 8 + 8, LANES : 2 * LANES] = z[1]
                high, low = split_two(zbuf[slot])
                bbuf[item] = mm(high, last_ref[0]) + mm(low, last_ref[0]) + mm(high, last_ref[1])
            for q2 in range(32):
                rows = slice(q2 * 8, q2 * 8 + 8)
                v, u2 = q2 % 8, q2 // 8
                at = (slice(v * 8, v * 8 + 8), slice(u2 * LANES, (u2 + 1) * LANES))
                re = [bbuf[band, rows, 0:LANES] for band in range(BANDS)]
                im = [bbuf[band, rows, LANES : 2 * LANES] for band in range(BANDS)]
                whole_re, whole_im = sum(re), sum(im)
                chi = jnp.zeros((8, LANES), jnp.float32)
                for band in range(BANDS):
                    gap_re = re[band] - shares[band] * whole_re
                    gap_im = im[band] - shares[band] * whole_im
                    chi = chi + (gap_re * gap_re + gap_im * gap_im) * inverse[band]
                vbuf[0, at[0], at[1]] = chi
                for slide in range(2):
                    re = bbuf[8 + slide, rows, 0:LANES]
                    im = bbuf[8 + slide, rows, LANES : 2 * LANES]
                    vbuf[1 + slide, at[0], at[1]] = (re * re + im * im) * net_scale
            for kind in range(3):
                high, low = split_two(vbuf[kind])
                done = mm(high, place_ref[...]) + mm(low, place_ref[...])
                for v in range(8):
                    both = done[v * 8 : v * 8 + 8, :]
                    out_ref[kind, 2 * eb, :, v * 512 : (v + 1) * 512] = both[0:4]
                    out_ref[kind, 2 * eb + 1, :, v * 512 : (v + 1) * 512] = both[4:8]
            return carry

        lax.fori_loop(0, OUT_ROWS // 8, block, 0)


def filter_rows(part, det, tmpl, strain, bounds, slides, antenna):
    bands, twiddle, inner, last, place = constant_tables()
    where = jnp.stack([part, det]).astype(jnp.int32)
    edges = jnp.concatenate([jnp.zeros((1,), jnp.int32), bounds, jnp.full((1,), BINS, jnp.int32)])
    one = pl.Buffered(1)
    spec = pltpu.PrefetchScalarGridSpec(
        num_scalar_prefetch=2,
        grid=(STEPS,),
        in_specs=[
            pl.BlockSpec((256, CHUNK), lambda i, w, e: (0, i)),
            pl.BlockSpec((1, 256, CHUNK), lambda i, w, e: (w[1], 0, i)),
            pl.BlockSpec((1, 256, CHUNK), lambda i, w, e: (1 - w[1], 0, i)),
            pl.BlockSpec((1, 4, 256, 256), lambda i, w, e: (w[0], 0, 0, 0), pipeline_mode=one),
            pl.BlockSpec((1, 2, OUT_ROWS, COLS), lambda i, w, e: (w[0], 0, 0, 0), pipeline_mode=one),
            pl.BlockSpec((2, 32, LANES), lambda i, w, e: (0, 0, 0), pipeline_mode=one),
            pl.BlockSpec((2, 256, 256), lambda i, w, e: (0, 0, 0), pipeline_mode=one),
            pl.BlockSpec((512, 512), lambda i, w, e: (0, 0), pipeline_mode=one),
            pl.BlockSpec(memory_space=pltpu.SMEM),
            pl.BlockSpec(memory_space=pltpu.SMEM),
        ],
        out_specs=pl.BlockSpec((3, 8, 4, COLS), lambda i, w, e: (0, 0, 0, 0), pipeline_mode=one),
        scratch_shapes=[
            pltpu.VMEM((2, 2, 128, 256), jnp.bfloat16),
            pltpu.VMEM((2, 4, 32, LANES), jnp.float32),
            pltpu.VMEM((640, COLS), jnp.float32),
            pltpu.VMEM((128, COLS), jnp.float32),
            pltpu.VMEM((2, 256, CHUNK), jnp.bfloat16),
            pltpu.VMEM((2, 256, CHUNK), jnp.bfloat16),
            pltpu.VMEM((2, 256, CHUNK), jnp.bfloat16),
            pltpu.VMEM((32, 8, LANES), jnp.float32),
            pltpu.VMEM((2, 256, 256), jnp.float32),
            pltpu.VMEM((10, 256, 256), jnp.float32),
            pltpu.VMEM((3, 64, 512), jnp.float32),
        ],
    )
    return pl.pallas_call(
        kernel,
        grid_spec=spec,
        out_shape=jax.ShapeDtypeStruct((3, 8, 4, COLS), jnp.float32),
        compiler_params=pltpu.CompilerParams(vmem_limit_bytes=48 * 2**20),
        cost_estimate=pl.CostEstimate(flops=20 * 10**9, bytes_accessed=20 * 10**6, transcendentals=0),
    )(
        where, edges, tmpl, strain, strain, jnp.asarray(bands), jnp.asarray(twiddle),
        jnp.asarray(inner), jnp.asarray(last), jnp.asarray(place), slides, antenna,
    )

MESH = pl.DeviceIdType.MESH
HALF = COLS // 2
PORTIONS = ((0, 640), (640, 640), (1280, 768))
ORDERS = (("x", "y", "z"), ("y", "z", "x"), ("z", "x", "y"))


def gather_kernel(
    assign, bank, strain, tmpl, signal, everything, staged,
    local_sem, swap_send, swap_recv, wide_send, wide_recv, pass_send, pass_recv,
    far_send, far_recv, near_send, near_recv,
):
    det, grp, tm = lax.axis_index("det"), lax.axis_index("grp"), lax.axis_index("tm")
    here = {"y": tm // 8, "z": det * 2 + (tm // 4) % 2, "x": tm % 4}
    peer = {"grp": 1 - grp}
    half = pl.ds(pl.multiple_of(grp * HALF, HALF), HALF)
    other = pl.ds(pl.multiple_of((1 - grp) * HALF, HALF), HALF)

    def moved(axis, by):
        there = dict(here)
        there[axis] = (here[axis] + by + 4) % 4
        return there

    def tm_of(place):
        return place["y"] * 8 + (place["z"] % 2) * 4 + place["x"]

    def ident(place):
        return {"det": place["z"] // 2, "tm": tm_of(place)}

    def shifted(d):
        dy, dz, dx = d // 8, (d // 4) % 2, d % 4
        y, z, x = here["y"], here["z"] % 2, here["x"]
        to = ((y + dy) % 4) * 8 + ((z + dz) % 2) * 4 + (x + dx) % 4
        back = ((y - dy + 4) % 4) * 8 + ((z - dz + 2) % 2) * 4 + (x - dx + 4) % 4
        return to, back

    barrier = pltpu.get_barrier_semaphore()

    def greet(d, carry):
        pl.semaphore_signal(barrier, inc=1, device_id={"tm": shifted(d)[0]}, device_id_type=MESH)
        return carry

    lax.fori_loop(1, 32, greet, 0)
    for z in range(2):
        place = dict(here)
        place["z"] = (1 - det) * 2 + z
        pl.semaphore_signal(barrier, inc=1, device_id=ident(place), device_id_type=MESH)
    pl.semaphore_signal(barrier, inc=1, device_id=peer, device_id_type=MESH)
    pl.semaphore_wait(barrier, 34)

    def remote(src, dst, send, recv, device):
        return pltpu.make_async_remote_copy(
            src_ref=src, dst_ref=dst, send_sem=send, recv_sem=recv, device_id=device, device_id_type=MESH
        )

    swap = remote(bank.at[:, :, other], everything.at[pl.ds(grp * 8, 8)], swap_send, swap_recv, peer)
    swap.start()
    keep = pltpu.make_async_copy(bank.at[:, :, half], everything.at[pl.ds(grp * 8, 8)], local_sem.at[0])
    keep.start()
    own = pltpu.make_async_copy(
        strain, signal.at[det, here["y"], here["z"] % 2, here["x"]], local_sem.at[1]
    )
    own.start()

    def columns(portion, core):
        first, width = PORTIONS[portion]
        return pl.ds(pl.multiple_of(core * HALF + first, LANES), width)

    def region(portion, stage, place, core):
        done = ORDERS[portion][:stage]
        every = lambda axis, value, size: pl.ds(0, size) if axis in done else value
        return signal.at[
            every("z", place["z"] // 2, 2), every("y", place["y"], 4), every("z", place["z"] % 2, 2),
            every("x", place["x"], 4), :, columns(portion, core),
        ]

    def wide(portion, stage, d):
        axis = ORDERS[portion][stage]
        dst = region(portion, stage, here, grp)
        src = strain.at[:, columns(portion, grp)] if stage == 0 else dst
        at = (portion, stage, d - 1)
        return remote(src, dst, wide_send.at[at], wide_recv.at[at], ident(moved(axis, d)))

    def arrived(portion, stage, d):
        axis = ORDERS[portion][stage]
        at = (portion, stage, d - 1)
        got = region(portion, stage, moved(axis, -d), grp)
        remote(got, got, wide_send.at[at], wide_recv.at[at], peer).wait_recv()
        remote(got, got, pass_send.at[at], pass_recv.at[at], peer).start()

    for portion in range(3):
        for d in (1, 3, 2):
            wide(portion, 0, d).start()

    swap.wait_recv()
    keep.wait()
    for slot in range(16):
        staged[slot] = everything[assign[slot]]

    def far(d):
        to, back = shifted(d)
        return remote(
            staged.at[to % 16], tmpl.at[tm, :, half], far_send.at[d], far_recv.at[d], {"tm": to}
        ), back

    def send_far(d, carry):
        far(d)[0].start()
        return carry

    lax.fori_loop(1, 32, send_far, 0)
    mine = pltpu.make_async_copy(staged.at[tm % 16], tmpl.at[tm, :, half], local_sem.at[2])
    mine.start()
    remote(staged.at[tm % 16], tmpl.at[tm, :, half], near_send.at[0], near_recv.at[0], peer).start()

    own.wait()
    for stage in range(3):
        for portion in range(3):
            for d in (1, 3, 2):
                arrived(portion, stage, d)
            if stage < 2:
                for d in (1, 3, 2):
                    wide(portion, stage + 1, d).start()
        if stage == 1:

            def got_far(d, carry):
                copy, back = far(d)
                got = tmpl.at[back, :, half]
                remote(got, got, far_send.at[d], far_recv.at[d], peer).wait_recv()
                remote(got, got, near_send.at[d], near_recv.at[d], peer).start()
                return carry

            lax.fori_loop(1, 32, got_far, 0)

    mine.wait()
    swap.wait_send()
    for stage in range(3):
        for portion in range(3):
            for d in (1, 3, 2):
                wide(portion, stage, d).wait_send()
                at = (portion, stage, d - 1)
                place = moved(ORDERS[portion][stage], -d)
                got = region(portion, stage, place, grp)
                remote(got, got, pass_send.at[at], pass_recv.at[at], peer).wait_send()
                come = region(portion, stage, place, 1 - grp)
                remote(come, come, pass_send.at[at], pass_recv.at[at], peer).wait_recv()

    def rest(d, carry):
        copy, back = far(d)
        piece = tmpl.at[back, :, other]
        near = remote(piece, piece, near_send.at[d], near_recv.at[d], peer)
        near.wait_recv()
        near.wait_send()

        @pl.when(d > 0)
        def _():
            copy.wait_send()

        return carry

    lax.fori_loop(0, 32, rest, 0)


def gather(assignment, bank, strain):
    dma = pltpu.SemaphoreType.DMA
    return pl.pallas_call(
        gather_kernel,
        out_shape=(
            jax.ShapeDtypeStruct((32, 8, COLS), jnp.float32),
            jax.ShapeDtypeStruct((2, 4, 2, 4, 8, COLS), jnp.float32),
        ),
        in_specs=[
            pl.BlockSpec(memory_space=pltpu.SMEM),
            pl.BlockSpec(memory_space=pl.ANY),
            pl.BlockSpec(memory_space=pl.ANY),
        ],
        out_specs=[pl.BlockSpec(memory_space=pl.ANY), pl.BlockSpec(memory_space=pl.ANY)],
        scratch_shapes=[
            pltpu.VMEM((16, 8, HALF), jnp.float32),
            pltpu.VMEM((16, 8, HALF), jnp.float32),
            dma((3,)), dma, dma, dma((3, 3, 3)), dma((3, 3, 3)), dma((3, 3, 3)), dma((3, 3, 3)),
            dma((32,)), dma((32,)), dma((32,)), dma((32,)),
        ],
        compiler_params=pltpu.CompilerParams(collective_id=0, has_side_effects=True),
    )(assignment, bank, strain)


def scatter_kernel(rows, chi, net, send, recv):
    grp, tm = lax.axis_index("grp"), lax.axis_index("tm")
    slot = tm % 16
    to_grp = slot // 8
    at = slot % 8
    part = 2 * (tm // 16) + grp
    from_part = tm // 8
    from_grp = from_part % 2
    self_too = (tm // 8) % 2 == grp
    barrier = pltpu.get_barrier_semaphore()

    def target(i):
        return 8 * part + (tm + i) % 8

    def source(k):
        return 8 * grp + k + 16 * (from_part // 2)

    def greet(i, carry):
        for device, group in ((target(i), to_grp), (source(i), from_grp)):
            @pl.when(jnp.logical_not((device == tm) & (group == grp)))
            def _():
                pl.semaphore_signal(
                    barrier, inc=1, device_id={"grp": group, "tm": device}, device_id_type=MESH
                )
        return carry

    lax.fori_loop(0, 8, greet, 0)

    @pl.when(self_too)
    def _():
        pl.semaphore_wait(barrier, 14)

    @pl.when(jnp.logical_not(self_too))
    def _():
        pl.semaphore_wait(barrier, 16)

    def parts(i):
        piece = target(i) % 8
        return ((rows.at[0, piece], chi.at[at]), (rows.at[pl.ds(1, 2), piece], net.at[at]))

    def copy(i, kind):
        src, dst = parts(i)[kind]
        return pltpu.make_async_remote_copy(
            src_ref=src, dst_ref=dst, send_sem=send.at[kind, i], recv_sem=recv.at[kind, at],
            device_id={"grp": to_grp, "tm": target(i)}, device_id_type=MESH,
        )

    def start(i, carry):
        is_self = (target(i) == tm) & (to_grp == grp)
        for kind in range(2):
            @pl.when(is_self)
            def _():
                src, dst = parts(i)[kind]
                pltpu.make_async_copy(src, dst, recv.at[kind, at]).start()

            @pl.when(jnp.logical_not(is_self))
            def _():
                copy(i, kind).start()
        return carry

    lax.fori_loop(0, 8, start, 0)

    def finish(i, carry):
        is_self = (target(i) == tm) & (to_grp == grp)

        for kind, dst in ((0, chi), (1, net)):
            pltpu.make_async_copy(dst.at[i], dst.at[i], recv.at[kind, i]).wait()

            @pl.when(jnp.logical_not(is_self))
            def _():
                copy(i, kind).wait_send()
        return carry

    lax.fori_loop(0, 8, finish, 0)


def scatter(rows):
    dma = pltpu.SemaphoreType.DMA
    return pl.pallas_call(
        scatter_kernel,
        out_shape=(
            jax.ShapeDtypeStruct((8, 4, COLS), jnp.float32),
            jax.ShapeDtypeStruct((8, 2, 4, COLS), jnp.float32),
        ),
        in_specs=[pl.BlockSpec(memory_space=pl.ANY)],
        out_specs=[pl.BlockSpec(memory_space=pl.ANY), pl.BlockSpec(memory_space=pl.ANY)],
        scratch_shapes=[dma((2, 8)), dma((2, 8))],
        compiler_params=pltpu.CompilerParams(collective_id=1, has_side_effects=True),
    )(rows)


def on_device(strain, bank, assignment, slides, bounds, antenna):
    tm = lax.axis_index("tm")
    det = lax.axis_index("det")
    grp = lax.axis_index("grp")
    tmpl, signal = gather(assignment, bank.reshape(8, 8, COLS), strain.reshape(8, COLS))
    part = 2 * (tm // 16) + grp
    rows = filter_rows(part, det, tmpl.reshape(256, COLS), signal.reshape(2, 256, COLS), bounds, slides, antenna)
    chi, net = scatter(rows)
    return chi[None], net


def solution(mesh):
    P = jax.sharding.PartitionSpec
    return jax.shard_map(
        on_device,
        mesh=mesh,
        in_specs=(P("det", None, "tm", None), P("grp", None, "tm", None), P(), P(), P(), P()),
        out_specs=(P("det", "grp", "tm", None), P("grp", "det", "tm", None)),
        check_vma=False,
    )
```

```python
import math

import jax
import jax.numpy as jnp
import numpy as np
from jax import lax
from jax.experimental import pallas as pl
from jax.experimental.pallas import tpu as pltpu

FOLD = 128
COLS = 4096
BINS = FOLD * COLS
BANDS = 8
CHUNK = 512
STEPS = COLS // CHUNK
LANES = 128
OUT_ROWS = 32


def rows_of(part):
    tau = np.arange(OUT_ROWS)
    return 64 * (part % 2) + 32 * (tau // 16) + 16 * (part // 2) + tau % 16


def halves(table):
    high = np.asarray(table, np.float32).astype(jnp.bfloat16)
    low = (np.asarray(table, np.float64) - high.astype(np.float64)).astype(np.float32)
    return high, low.astype(jnp.bfloat16)


def pack_columns(real, imag):
    m = real.shape[0]
    parts = np.stack([real.reshape(m, 32, 4), imag.reshape(m, 32, 4)], axis=2)
    return parts.reshape(m, 256)


def stacked_rows(cos, sin):
    top = pack_columns(cos, -sin)
    bottom = pack_columns(sin, cos)
    return np.concatenate([top, bottom], axis=0)


def constant_tables():
    b = np.arange(FOLD)
    even, odd, twiddle = [], [], []
    for part in range(4):
        e = rows_of(part)
        angle = 2 * np.pi * ((e[:, None] * b[None, :]) % FOLD) / FOLD
        cos, sin = np.cos(angle), np.sin(angle)
        for parity, group in ((0, even), (1, odd)):
            blocks = []
            for band in range(parity, BANDS, 2):
                inside = (b >= 16 * band - 8) & (b < 16 * band + 24)
                blocks.append(stacked_rows(cos * inside, sin * inside))
            group.append(np.concatenate(blocks, axis=0))
        a = np.arange(COLS)
        angle = 2 * np.pi * (e[:, None] * a[None, :]) / BINS
        twiddle.append(np.stack([np.cos(angle), np.sin(angle)]))
    even = halves(np.stack(even))
    odd = halves(np.stack(odd))
    bands = np.stack([even[0], even[1], odd[0], odd[1]], axis=1)
    twiddle = np.stack(twiddle).astype(np.float32)
    a1 = np.arange(LANES)
    q2 = np.arange(32)
    angle = 2 * np.pi * (a1[None, :] * q2[:, None]) / COLS
    inner = np.stack([np.cos(angle), np.sin(angle)]).astype(np.float32)
    angle = 2 * np.pi * ((a1[:, None] * a1[None, :]) % LANES) / LANES
    cos, sin = np.cos(angle), np.sin(angle)
    last = np.stack(halves(np.block([[cos, sin], [-sin, cos]])))
    place = np.zeros((512, 512), np.float32)
    u1, u2 = np.meshgrid(np.arange(128), np.arange(4), indexing="ij")
    place[(u2 * 128 + u1).ravel(), (u2 + 4 * u1).ravel()] = 1.0
    return bands, twiddle, inner, last, place.astype(jnp.bfloat16)


def split_two(x):
    high = x.astype(jnp.bfloat16)
    low = (x - high.astype(jnp.float32)).astype(jnp.bfloat16)
    return high, low


def mm(a, b):
    return jnp.dot(a, b, preferred_element_type=jnp.float32)


ROOT = math.sqrt(0.5)


def eight(x):
    def add(p, q):
        return (p[0] + q[0], p[1] + q[1])

    def sub(p, q):
        return (p[0] - q[0], p[1] - q[1])

    def turn(p):
        return (-p[1], p[0])

    def addi(p, q):
        return (p[0] - q[1], p[1] + q[0])

    def subi(p, q):
        return (p[0] + q[1], p[1] - q[0])

    def four(z):
        s02, d02 = add(z[0], z[2]), sub(z[0], z[2])
        s13, d13 = add(z[1], z[3]), sub(z[1], z[3])
        return [add(s02, s13), addi(d02, d13), sub(s02, s13), subi(d02, d13)]

    ev = four([x[0], x[2], x[4], x[6]])
    od = four([x[1], x[3], x[5], x[7]])
    o1 = ((od[1][0] - od[1][1]) * ROOT, (od[1][0] + od[1][1]) * ROOT)
    o3 = ((od[3][0] + od[3][1]) * ROOT, (od[3][1] - od[3][0]) * ROOT)
    return [
        add(ev[0], od[0]),
        add(ev[1], o1),
        addi(ev[2], od[2]),
        sub(ev[3], o3),
        sub(ev[0], od[0]),
        sub(ev[1], o1),
        subi(ev[2], od[2]),
        add(ev[3], o3),
    ]


def four_point(z):
    s0 = (z[0][0] + z[2][0], z[0][1] + z[2][1])
    d0 = (z[0][0] - z[2][0], z[0][1] - z[2][1])
    s1 = (z[1][0] + z[3][0], z[1][1] + z[3][1])
    d1 = (z[1][0] - z[3][0], z[1][1] - z[3][1])
    return [
        (s0[0] + s1[0], s0[1] + s1[1]),
        (d0[0] - d1[1], d0[1] + d1[0]),
        (s0[0] - s1[0], s0[1] - s1[1]),
        (d0[0] + d1[1], d0[1] - d1[0]),
    ]


def times(x, c, s):
    return (x[0] * c - x[1] * s, x[0] * s + x[1] * c)


def swap_halves(x):
    rows, width = x.shape
    return pltpu.roll(x.reshape(rows // 8, 8, width), 4, 1).reshape(rows, width)


def kernel(
    where_ref, bounds_ref, tmpl_ref, own_ref, oth_ref, bands_hbm, twiddle_hbm,
    inner_hbm, last_hbm, place_hbm, slides_ref, antenna_ref, out_ref,
    bands_ref, twiddle_ref, inner_ref, last_ref, place_ref, table_sem,
    net_ref, ramp_ref, series, net_oth, xe, xo, xn, power, zbuf, bbuf, vbuf,
):
    step = pl.program_id(0)
    start = step * CHUNK

    tables = [
        pltpu.make_async_copy(src, dst, table_sem.at[i])
        for i, (src, dst) in enumerate((
            (bands_hbm.at[where_ref[0]], bands_ref.at[0]),
            (twiddle_hbm.at[where_ref[0]], twiddle_ref.at[0]),
            (inner_hbm, inner_ref),
            (last_hbm, last_ref),
            (place_hbm, place_ref),
        ))
    ]

    @pl.when(step == 0)
    def _():
        for copy in tables:
            copy.start()
        power[...] = jnp.zeros_like(power)
        part, det = where_ref[0], where_ref[1]
        column = (
            lax.broadcasted_iota(jnp.int32, (32, LANES), 0) * LANES
            + lax.broadcasted_iota(jnp.int32, (32, LANES), 1)
        )
        tau = lax.broadcasted_iota(jnp.int32, (OUT_ROWS, 256), 0)
        row = 64 * (part & 1) + 32 * (tau >> 4) + 16 * (part >> 1) + (tau & 15)
        packed = lax.broadcasted_iota(jnp.int32, (OUT_ROWS, 256), 1)
        bin_row = (packed >> 3) * 4 + (packed & 3)
        quarter = ((packed >> 2) & 1) * (FOLD // 4)
        for side in range(2):
            which = det if side == 0 else 1 - det
            weight_re, weight_im = antenna_ref[which, 0], antenna_ref[which, 1]
            for slide in range(2):
                shift = which * slides_ref[2 * det + slide]
                angle = (((row + shift) * bin_row + quarter) & (FOLD - 1)).astype(jnp.float32) * (2.0 * math.pi / FOLD)
                for half, table in ((0, jnp.cos(angle)), (1, jnp.sin(angle))):
                    high, low = split_two(table)
                    at = slice(64 * slide + 32 * half, 64 * slide + 32 * half + 32)
                    net_ref[side, 0, at, :] = high
                    net_ref[side, 1, at, :] = low
                angle = ((column * shift) & (BINS - 1)).astype(jnp.float32) * (2.0 * math.pi / BINS)
                cos, sin = jnp.cos(angle), jnp.sin(angle)
                ramp_ref[slide, 2 * side] = weight_re * cos - weight_im * sin
                ramp_ref[slide, 2 * side + 1] = weight_re * sin + weight_im * cos

    sub = lax.broadcasted_iota(jnp.int32, (16, CHUNK), 0)
    lane = lax.broadcasted_iota(jnp.int32, (16, CHUNK), 1)
    top = (sub & 7) < 4
    place_in = ((sub >> 3) * 4 + (sub & 3)) * COLS + lane + start
    for group in range(16):
        rows = slice(16 * group, 16 * group + 16)
        wave = tmpl_ref[rows, :]
        rolled = swap_halves(wave)
        wave_re = jnp.where(top, wave, rolled)
        wave_im = jnp.where(top, rolled, -wave)
        own = own_ref[0, rows, :]
        own = own * wave_re + swap_halves(own) * wave_im
        oth = oth_ref[0, rows, :]
        oth = oth * wave_re + swap_halves(oth) * wave_im
        bound = (group - 1) // 2
        upper = (place_in + 8 * group * COLS) >= bounds_ref[bound + 1]
        even = upper if bound % 2 else jnp.logical_not(upper)
        squares = wave * wave
        low_sum = jnp.where(upper, 0.0, squares)
        fold = lambda v: sum(
            v[r : r + 8, c : c + LANES] for r in (0, 8) for c in range(0, CHUNK, LANES)
        )
        power[2 * group] += fold(low_sum)
        power[2 * group + 1] += fold(squares)
        high = own.astype(jnp.bfloat16).astype(jnp.float32)
        low = own - high
        xe[0, rows, :] = jnp.where(even, high, 0.0).astype(jnp.bfloat16)
        xe[1, rows, :] = jnp.where(even, low, 0.0).astype(jnp.bfloat16)
        xo[0, rows, :] = jnp.where(even, 0.0, high).astype(jnp.bfloat16)
        xo[1, rows, :] = jnp.where(even, 0.0, low).astype(jnp.bfloat16)
        high, low = split_two(oth)
        xn[0, rows, :] = high
        xn[1, rows, :] = low
    cols = pl.ds(pl.multiple_of(start, CHUNK), CHUNK)

    @pl.when(step == 0)
    def _():
        for copy in tables:
            copy.wait()

    def three(high, low, x):
        return mm(high, x[0]) + mm(low, x[0]) + mm(high, x[1])

    series[0:256, cols] = three(bands_ref[0, 0], bands_ref[0, 1], xe)
    series[256:512, cols] = three(bands_ref[0, 2], bands_ref[0, 3], xo)
    series[512:640, cols] = three(net_ref[0, 0], net_ref[0, 1], xe) + three(net_ref[0, 0], net_ref[0, 1], xo)
    net_oth[:, cols] = three(net_ref[1, 0], net_ref[1, 1], xn)

    @pl.when(step == STEPS - 1)
    def _():
        total = jnp.zeros((1, 1), jnp.float32)
        powers = []
        for band in range(BANDS):
            acc = jnp.zeros((8, LANES), jnp.float32)
            for group in range(16):
                bound = (group - 1) // 2
                if bound == band:
                    acc += power[2 * group]
                if bound + 1 == band:
                    acc += power[2 * group + 1] - power[2 * group]
            value = jnp.sum(jnp.sum(acc, axis=0, keepdims=True), axis=1, keepdims=True)
            powers.append(value)
            total = total + value
        shares = [value / total for value in powers]
        inverse = [(1.0 / (2 * BANDS - 2)) / (total * share) for share in shares]
        response = sum(antenna_ref[d, c] * antenna_ref[d, c] for d in range(2) for c in range(2))
        net_scale = 1.0 / (total * response)

        def block(eb, carry):
            first = pl.multiple_of(eb * 8, 8)
            erows = pl.ds(first, 8)

            def load(item, a2):
                columns = slice(a2 * LANES, (a2 + 1) * LANES)
                if item < 8:
                    base = (item // 2) * 64 + (item % 2) * 256
                    re = series[pl.ds(base + first, 8), columns]
                    im = series[pl.ds(base + 32 + first, 8), columns]
                else:
                    slide = item - 8
                    base = 512 + 64 * slide
                    own = (series[pl.ds(base + first, 8), columns], series[pl.ds(base + 32 + first, 8), columns])
                    base = 64 * slide
                    oth = (net_oth[pl.ds(base + first, 8), columns], net_oth[pl.ds(base + 32 + first, 8), columns])
                    own = times(own, ramp_ref[slide, 0, a2 : a2 + 1, :], ramp_ref[slide, 1, a2 : a2 + 1, :])
                    oth = times(oth, ramp_ref[slide, 2, a2 : a2 + 1, :], ramp_ref[slide, 3, a2 : a2 + 1, :])
                    re, im = own[0] + oth[0], own[1] + oth[1]
                return times((re, im), twiddle_ref[0, 0, erows, columns], twiddle_ref[0, 1, erows, columns])

            for item in range(10):
                slot = item % 2
                halfway = []
                for r2 in range(4):
                    values = eight([load(item, 4 * s + r2) for s in range(8)])
                    turned = []
                    for v in range(8):
                        if r2 * v == 0:
                            turned.append(values[v])
                        else:
                            angle = 2 * math.pi * r2 * v / 32
                            turned.append(times(values[v], math.cos(angle), math.sin(angle)))
                    halfway.append(turned)
                for v in range(8):
                    done = four_point([halfway[r2][v] for r2 in range(4)])
                    for u2 in range(4):
                        q2 = v + 8 * u2
                        z = times(done[u2], inner_ref[0, q2 : q2 + 1, :], inner_ref[1, q2 : q2 + 1, :])
                        zbuf[slot, q2 * 8 : q2 * 8 + 8, 0:LANES] = z[0]
                        zbuf[slot, q2 * 8 : q2 * 8 + 8, LANES : 2 * LANES] = z[1]
                high, low = split_two(zbuf[slot])
                bbuf[item] = mm(high, last_ref[0]) + mm(low, last_ref[0]) + mm(high, last_ref[1])
            for q2 in range(32):
                rows = slice(q2 * 8, q2 * 8 + 8)
                v, u2 = q2 % 8, q2 // 8
                at = (slice(v * 8, v * 8 + 8), slice(u2 * LANES, (u2 + 1) * LANES))
                re = [bbuf[band, rows, 0:LANES] for band in range(BANDS)]
                im = [bbuf[band, rows, LANES : 2 * LANES] for band in range(BANDS)]
                whole_re, whole_im = sum(re), sum(im)
                chi = jnp.zeros((8, LANES), jnp.float32)
                for band in range(BANDS):
                    gap_re = re[band] - shares[band] * whole_re
                    gap_im = im[band] - shares[band] * whole_im
                    chi = chi + (gap_re * gap_re + gap_im * gap_im) * inverse[band]
                vbuf[0, at[0], at[1]] = chi
                for slide in range(2):
                    re = bbuf[8 + slide, rows, 0:LANES]
                    im = bbuf[8 + slide, rows, LANES : 2 * LANES]
                    vbuf[1 + slide, at[0], at[1]] = (re * re + im * im) * net_scale
            for kind in range(3):
                high, low = split_two(vbuf[kind])
                done = mm(high, place_ref[...]) + mm(low, place_ref[...])
                for v in range(8):
                    both = done[v * 8 : v * 8 + 8, :]
                    out_ref[kind, 2 * eb, :, v * 512 : (v + 1) * 512] = both[0:4]
                    out_ref[kind, 2 * eb + 1, :, v * 512 : (v + 1) * 512] = both[4:8]
            return carry

        lax.fori_loop(0, OUT_ROWS // 8, block, 0)


def filter_rows(part, det, tmpl, strain, bounds, slides, antenna):
    bands, twiddle, inner, last, place = constant_tables()
    where = jnp.stack([part, det]).astype(jnp.int32)
    edges = jnp.concatenate([jnp.zeros((1,), jnp.int32), bounds, jnp.full((1,), BINS, jnp.int32)])
    one = pl.Buffered(1)
    spec = pltpu.PrefetchScalarGridSpec(
        num_scalar_prefetch=2,
        grid=(STEPS,),
        in_specs=[
            pl.BlockSpec((256, CHUNK), lambda i, w, e: (0, i)),
            pl.BlockSpec((1, 256, CHUNK), lambda i, w, e: (w[1], 0, i)),
            pl.BlockSpec((1, 256, CHUNK), lambda i, w, e: (1 - w[1], 0, i)),
            *[pl.BlockSpec(memory_space=pltpu.HBM)] * 5,
            pl.BlockSpec(memory_space=pltpu.SMEM),
            pl.BlockSpec(memory_space=pltpu.SMEM),
        ],
        out_specs=pl.BlockSpec((3, 8, 4, COLS), lambda i, w, e: (0, 0, 0, 0), pipeline_mode=one),
        scratch_shapes=[
            pltpu.VMEM((1, 4, 256, 256), jnp.bfloat16),
            pltpu.VMEM((1, 2, OUT_ROWS, COLS), jnp.float32),
            pltpu.VMEM((2, 32, LANES), jnp.float32),
            pltpu.VMEM((2, 256, 256), jnp.bfloat16),
            pltpu.VMEM((512, 512), jnp.bfloat16),
            pltpu.SemaphoreType.DMA((5,)),
            pltpu.VMEM((2, 2, 128, 256), jnp.bfloat16),
            pltpu.VMEM((2, 4, 32, LANES), jnp.float32),
            pltpu.VMEM((640, COLS), jnp.float32),
            pltpu.VMEM((128, COLS), jnp.float32),
            pltpu.VMEM((2, 256, CHUNK), jnp.bfloat16),
            pltpu.VMEM((2, 256, CHUNK), jnp.bfloat16),
            pltpu.VMEM((2, 256, CHUNK), jnp.bfloat16),
            pltpu.VMEM((32, 8, LANES), jnp.float32),
            pltpu.VMEM((2, 256, 256), jnp.float32),
            pltpu.VMEM((10, 256, 256), jnp.float32),
            pltpu.VMEM((3, 64, 512), jnp.float32),
        ],
    )
    return pl.pallas_call(
        kernel,
        grid_spec=spec,
        out_shape=jax.ShapeDtypeStruct((3, 8, 4, COLS), jnp.float32),
        compiler_params=pltpu.CompilerParams(vmem_limit_bytes=48 * 2**20),
        cost_estimate=pl.CostEstimate(flops=20 * 10**9, bytes_accessed=20 * 10**6, transcendentals=0),
    )(
        where, edges, tmpl, strain, strain, jnp.asarray(bands), jnp.asarray(twiddle),
        jnp.asarray(inner), jnp.asarray(last), jnp.asarray(place), slides, antenna,
    )

MESH = pl.DeviceIdType.MESH
HALF = COLS // 2
PORTIONS = ((0, 640), (640, 640), (1280, 768))
ORDERS = (("x", "y", "z"), ("y", "z", "x"), ("z", "x", "y"))


def gather_kernel(
    assign, bank, strain, tmpl, signal, everything, staged, loaded, packed,
    local_sem, swap_send, swap_recv, wide_send, wide_recv, pass_send, pass_recv,
    far_send, far_recv, deep_send, deep_recv, near_send, near_recv,
):
    det, grp, tm = lax.axis_index("det"), lax.axis_index("grp"), lax.axis_index("tm")
    low_z = (tm // 4) % 2
    here = {"y": tm // 8, "z": det * 2 + low_z, "x": tm % 4}
    peer = {"grp": 1 - grp}
    half = pl.ds(pl.multiple_of(grp * HALF, HALF), HALF)
    other = pl.ds(pl.multiple_of((1 - grp) * HALF, HALF), HALF)

    def moved(axis, by):
        there = dict(here)
        there[axis] = (here[axis] + by + 4) % 4
        return there

    def ident(place):
        return {"det": place["z"] // 2, "tm": place["y"] * 8 + (place["z"] % 2) * 4 + place["x"]}

    def shifted(d, sign=1):
        there = dict(here)
        there["y"] = (here["y"] + sign * (d // 4) + 4) % 4
        there["x"] = (here["x"] + sign * (d % 4) + 4) % 4
        return there

    keep = pltpu.make_async_copy(bank.at[:, :, :, half], everything.at[pl.ds(grp * 8, 8)], local_sem.at[0])
    keep.start()
    own = pltpu.make_async_copy(strain, loaded, local_sem.at[1])
    own.start()

    barrier = pltpu.get_barrier_semaphore()

    def greet(d, carry):
        pl.semaphore_signal(barrier, inc=1, device_id=ident(shifted(d)), device_id_type=MESH)
        return carry

    lax.fori_loop(1, 16, greet, 0)
    for d in (1, 2, 3):
        pl.semaphore_signal(barrier, inc=1, device_id=ident(moved("z", d)), device_id_type=MESH)
    pl.semaphore_signal(barrier, inc=1, device_id=peer, device_id_type=MESH)
    pl.semaphore_wait(barrier, 19)

    def remote(src, dst, send, recv, device):
        return pltpu.make_async_remote_copy(
            src_ref=src, dst_ref=dst, send_sem=send, recv_sem=recv, device_id=device, device_id_type=MESH
        )

    swap = remote(bank.at[:, :, :, other], everything.at[pl.ds(grp * 8, 8)], swap_send, swap_recv, peer)
    swap.start()

    def columns(portion, core):
        first, width = PORTIONS[portion]
        return pl.ds(pl.multiple_of(core * HALF + first, LANES), width)

    def region(portion, stage, place, core, part=None):
        done = ORDERS[portion][:stage]
        cut = "x" if ORDERS[portion][2] == "y" else "y"

        def every(axis, value, size):
            if axis not in done:
                return value
            if part is not None and axis == cut:
                return pl.ds(2 * part, 2)
            return pl.ds(0, size)

        return signal.at[
            every("z", place["z"] // 2, 2), every("y", place["y"], 4), every("z", place["z"] % 2, 2),
            every("x", place["x"], 4), :, columns(portion, core),
        ]

    def wide(portion, stage, d):
        dst = region(portion, stage, here, grp)
        src = packed.at[:, columns(portion, grp)] if stage == 0 else dst
        at = (portion, stage, d - 1)
        return remote(src, dst, wide_send.at[at], wide_recv.at[at], ident(moved(ORDERS[portion][stage], d)))

    def relay(portion, part):
        axis = ORDERS[portion][2]
        got = region(portion, 2, moved(axis, -1 if part == 0 else 1), grp, part)
        at = (portion, 2 + part, 1)
        return remote(got, got, wide_send.at[at], wide_recv.at[at], ident(moved(axis, 1 if part == 0 else -1)))

    def incoming(portion, stage, d, core):
        axis = ORDERS[portion][min(stage, 2)]
        if stage < 2 or d != 2:
            part = None
        else:
            part = stage - 2
        return region(portion, min(stage, 2), moved(axis, -d), core, part), (portion, stage, d - 1)

    def arrived(portion, stage, d):
        got, at = incoming(portion, stage, d, grp)
        remote(got, got, wide_send.at[at], wide_recv.at[at], peer).wait_recv()
        remote(got, got, pass_send.at[at], pass_recv.at[at], peer).start()

    own.wait()
    packed[0:4, :] = loaded[0, 0]
    packed[4:8, :] = loaded[0, 1]
    for portion in range(3):
        for d in (1, 3, 2):
            wide(portion, 0, d).start()
    mine = pltpu.make_async_copy(packed, signal.at[det, here["y"], low_z, here["x"]], local_sem.at[1])
    mine.start()

    swap.wait_recv()
    keep.wait()
    for slot in range(16):
        wave = everything[assign[slot]]
        staged[slot, 0:4, :] = wave[0]
        staged[slot, 4:8, :] = wave[1]

    def far(d):
        to = shifted(d)
        return remote(
            staged.at[to["y"] * 4 + to["x"]], tmpl.at[here["y"], low_z, here["x"], :, half],
            far_send.at[d], far_recv.at[d], ident(to),
        )

    def piece(place, plane, columns):
        return tmpl.at[place["y"], plane, place["x"], :, columns]

    def deep(place):
        got = piece(place, low_z, half)
        at = place["y"] * 4 + place["x"]
        to = moved("z", jnp.where(place["y"] < 2, 1, 3))
        return remote(got, got, deep_send.at[at], deep_recv.at[at], ident(to))

    def near(place, plane, columns):
        got = piece(place, plane, columns)
        at = (plane, place["y"] * 4 + place["x"])
        return remote(got, got, near_send.at[at], near_recv.at[at], peer)

    def send_far(d, carry):
        far(d).start()
        return carry

    lax.fori_loop(1, 16, send_far, 0)
    slot_here = here["y"] * 4 + here["x"]
    kept = pltpu.make_async_copy(staged.at[slot_here], piece(here, low_z, half), local_sem.at[2])
    kept.start()

    mine.wait()
    for portion in range(3):
        for d in (1, 3, 2):
            arrived(portion, 0, d)
        for d in (1, 3, 2):
            wide(portion, 1, d).start()
    kept.wait()
    deep(here).start()
    near(here, low_z, half).start()

    def got_far(d, carry):
        place = shifted(d, -1)
        got = piece(place, low_z, half)
        remote(got, got, far_send.at[d], far_recv.at[d], peer).wait_recv()
        deep(place).start()
        near(place, low_z, half).start()
        return carry

    lax.fori_loop(1, 16, got_far, 0)
    for portion in range(3):
        for d in (1, 3, 2):
            arrived(portion, 1, d)
        for d in (1, 3):
            wide(portion, 2, d).start()

    def place_at(p):
        return {"y": p // 4, "x": p % 4}

    def got_deep(p, carry):
        got = piece(place_at(p), 1 - low_z, half)
        remote(got, got, deep_send.at[p], deep_recv.at[p], peer).wait_recv()
        near(place_at(p), 1 - low_z, half).start()
        return carry

    lax.fori_loop(0, 16, got_deep, 0)
    for portion in range(3):
        for d, part in ((1, 0), (3, 1)):
            arrived(portion, 2, d)
            relay(portion, part).start()
    for portion in range(3):
        for part in range(2):
            arrived(portion, 2 + part, 2)

    swap.wait_send()

    def rest(p, carry):
        deep(place_at(p)).wait_send()
        for plane in range(2):
            near(place_at(p), plane, half).wait_send()
            near(place_at(p), plane, other).wait_recv()

        @pl.when(p > 0)
        def _():
            far(p).wait_send()

        return carry

    lax.fori_loop(0, 16, rest, 0)
    for portion in range(3):
        for stage, d in ((0, 1), (0, 2), (0, 3), (1, 1), (1, 2), (1, 3), (2, 1), (2, 3), (2, 2), (3, 2)):
            if stage < 2 or d != 2:
                wide(portion, stage, d).wait_send()
            else:
                relay(portion, stage - 2).wait_send()
            got, at = incoming(portion, stage, d, grp)
            remote(got, got, pass_send.at[at], pass_recv.at[at], peer).wait_send()
            come, at = incoming(portion, stage, d, 1 - grp)
            remote(come, come, pass_send.at[at], pass_recv.at[at], peer).wait_recv()


def gather(assignment, bank, strain):
    dma = pltpu.SemaphoreType.DMA
    return pl.pallas_call(
        gather_kernel,
        out_shape=(
            jax.ShapeDtypeStruct((4, 2, 4, 8, COLS), jnp.float32),
            jax.ShapeDtypeStruct((2, 4, 2, 4, 8, COLS), jnp.float32),
        ),
        in_specs=[
            pl.BlockSpec(memory_space=pltpu.SMEM),
            pl.BlockSpec(memory_space=pltpu.HBM),
            pl.BlockSpec(memory_space=pltpu.HBM),
        ],
        out_specs=[pl.BlockSpec(memory_space=pltpu.HBM), pl.BlockSpec(memory_space=pltpu.HBM)],
        scratch_shapes=[
            pltpu.VMEM((16, 2, 4, HALF), jnp.float32),
            pltpu.VMEM((16, 8, HALF), jnp.float32),
            pltpu.VMEM((1, 2, 4, COLS), jnp.float32),
            pltpu.VMEM((8, COLS), jnp.float32),
            dma((3,)), dma, dma, dma((3, 4, 3)), dma((3, 4, 3)), dma((3, 4, 3)), dma((3, 4, 3)),
            dma((16,)), dma((16,)), dma((16,)), dma((16,)), dma((2, 16)), dma((2, 16)),
        ],
        compiler_params=pltpu.CompilerParams(collective_id=0, has_side_effects=True, vmem_limit_bytes=32 * 2**20),
    )(assignment, bank, strain)


def scatter_kernel(rows, chi, net, send, recv):
    grp, tm = lax.axis_index("grp"), lax.axis_index("tm")
    y, low_z, x = tm // 8, (tm // 4) % 2, tm % 4
    to_grp = y // 2
    at = 4 * (y % 2) + x
    self_too = y // 2 == grp
    barrier = pltpu.get_barrier_semaphore()

    def row_group(i):
        return (at + i) % 8

    def target(i):
        return (2 * grp + i // 4) * 8 + low_z * 4 + i % 4

    def greet(i, carry):
        @pl.when(jnp.logical_not((target(i) == tm) & self_too))
        def _():
            pl.semaphore_signal(
                barrier, inc=1, device_id={"grp": to_grp, "tm": target(i)}, device_id_type=MESH
            )

        return carry

    lax.fori_loop(0, 8, greet, 0)

    @pl.when(self_too)
    def _():
        pl.semaphore_wait(barrier, 7)

    @pl.when(jnp.logical_not(self_too))
    def _():
        pl.semaphore_wait(barrier, 8)

    def parts(i):
        return ((rows.at[0, i], chi.at[at]), (rows.at[pl.ds(1, 2), i], net.at[at]))

    def copy(i, kind):
        src, dst = parts(i)[kind]
        return pltpu.make_async_remote_copy(
            src_ref=src, dst_ref=dst, send_sem=send.at[kind, i], recv_sem=recv.at[kind, at],
            device_id={"grp": to_grp, "tm": target(i)}, device_id_type=MESH,
        )

    def start(step, carry):
        i = row_group(step)
        is_self = (target(i) == tm) & self_too
        for kind in range(2):
            @pl.when(is_self)
            def _():
                src, dst = parts(i)[kind]
                pltpu.make_async_copy(src, dst, recv.at[kind, at]).start()

            @pl.when(jnp.logical_not(is_self))
            def _():
                copy(i, kind).start()
        return carry

    lax.fori_loop(0, 8, start, 0)

    def finish(i, carry):
        is_self = (target(i) == tm) & self_too

        for kind, dst in ((0, chi), (1, net)):
            pltpu.make_async_copy(dst.at[i], dst.at[i], recv.at[kind, i]).wait()

            @pl.when(jnp.logical_not(is_self))
            def _():
                copy(i, kind).wait_send()
        return carry

    lax.fori_loop(0, 8, finish, 0)


def scatter(rows):
    dma = pltpu.SemaphoreType.DMA
    return pl.pallas_call(
        scatter_kernel,
        out_shape=(
            jax.ShapeDtypeStruct((8, 4, COLS), jnp.float32),
            jax.ShapeDtypeStruct((8, 2, 4, COLS), jnp.float32),
        ),
        in_specs=[pl.BlockSpec(memory_space=pltpu.HBM)],
        out_specs=[pl.BlockSpec(memory_space=pltpu.HBM), pl.BlockSpec(memory_space=pltpu.HBM)],
        scratch_shapes=[dma((2, 8)), dma((2, 8))],
        compiler_params=pltpu.CompilerParams(collective_id=1, has_side_effects=True),
    )(rows)


def finish_kernel(chi, net, chi_out, net_out, sem):
    copies = []
    for k in range(8):
        copies.append(pltpu.make_async_copy(chi.at[k], chi_out.at[k], sem.at[0, k]))
        copies.append(pltpu.make_async_copy(net.at[k], net_out.at[k], sem.at[1, k]))
    for copy in copies:
        copy.start()
    for copy in copies:
        copy.wait()


def finish(chi, net):
    spec = pl.BlockSpec(memory_space=pltpu.HBM)
    return pl.pallas_call(
        finish_kernel,
        out_shape=(
            jax.ShapeDtypeStruct(chi.shape, jnp.float32), jax.ShapeDtypeStruct(net.shape, jnp.float32)
        ),
        in_specs=[spec, spec],
        out_specs=[spec, spec],
        scratch_shapes=[pltpu.SemaphoreType.DMA((2, 8))],
    )(chi, net)


def on_device(strain, bank, assignment, slides, bounds, antenna):
    tm = lax.axis_index("tm")
    det = lax.axis_index("det")
    grp = lax.axis_index("grp")
    tmpl, signal = gather(assignment, bank, strain)
    part = 2 * ((tm >> 2) & 1) + grp
    rows = filter_rows(part, det, tmpl.reshape(256, COLS), signal.reshape(2, 256, COLS), bounds, slides, antenna)
    chi, net = finish(*scatter(rows))
    return chi[None], net


def solution(mesh):
    P = jax.sharding.PartitionSpec
    return jax.shard_map(
        on_device,
        mesh=mesh,
        in_specs=(P("det", None, "tm", None), P("grp", None, "tm", None), P(), P(), P(), P()),
        out_specs=(P("det", "grp", "tm", None), P("grp", "det", "tm", None)),
        check_vma=False,
    )
```

```python
import functools
import math

import jax
import jax.numpy as jnp
import numpy as np
from jax import lax
from jax.experimental import pallas as pl
from jax.experimental.pallas import tpu as pltpu

FOLD = 128
COLS = 4096
BINS = FOLD * COLS
BANDS = 8
CHUNK = 512
STEPS = COLS // CHUNK
LANES = 128
OUT_ROWS = 32


def rows_of(part):
    tau = np.arange(OUT_ROWS)
    return 64 * (part % 2) + 32 * (tau // 16) + 16 * (part // 2) + tau % 16


def halves(table):
    high = np.asarray(table, np.float32).astype(jnp.bfloat16)
    low = (np.asarray(table, np.float64) - high.astype(np.float64)).astype(np.float32)
    return high, low.astype(jnp.bfloat16)


def pack_columns(real, imag):
    m = real.shape[0]
    parts = np.stack([real.reshape(m, 32, 4), imag.reshape(m, 32, 4)], axis=2)
    return parts.reshape(m, 256)


def stacked_rows(cos, sin):
    top = pack_columns(cos, -sin)
    bottom = pack_columns(sin, cos)
    return np.concatenate([top, bottom], axis=0)


def constant_tables():
    b = np.arange(FOLD)
    even, odd, twiddle = [], [], []
    for part in range(4):
        e = rows_of(part)
        angle = 2 * np.pi * ((e[:, None] * b[None, :]) % FOLD) / FOLD
        cos, sin = np.cos(angle), np.sin(angle)
        for parity, group in ((0, even), (1, odd)):
            blocks = []
            for band in range(parity, BANDS, 2):
                inside = (b >= 16 * band - 8) & (b < 16 * band + 24)
                blocks.append(stacked_rows(cos * inside, sin * inside))
            group.append(np.concatenate(blocks, axis=0))
        a = np.arange(COLS)
        angle = 2 * np.pi * (e[:, None] * a[None, :]) / BINS
        twiddle.append(np.stack([np.cos(angle), np.sin(angle)]))
    even = halves(np.stack(even))
    odd = halves(np.stack(odd))
    bands = np.stack([even[0], even[1], odd[0], odd[1]], axis=1)
    twiddle = np.stack(twiddle).astype(np.float32).reshape(4, 2, 4, 8, 32, LANES).swapaxes(3, 4).copy()
    a1 = np.arange(LANES)
    q2 = np.arange(32)
    v, r2 = np.meshgrid(np.arange(8), np.arange(4), indexing="ij")
    angle = (2 * np.pi * v * r2 / 32)[..., None, None] * np.ones((8, LANES))
    turn = np.stack([np.cos(angle), np.sin(angle)]).astype(np.float32)
    angle = 2 * np.pi * (a1[None, :] * q2[:, None]) / COLS
    inner = np.stack([np.cos(angle), np.sin(angle)]).astype(np.float32)
    angle = 2 * np.pi * ((a1[:, None] * a1[None, :]) % LANES) / LANES
    cos, sin = np.cos(angle), np.sin(angle)
    last = np.stack(halves(np.block([[cos, sin], [-sin, cos]])))
    place = np.zeros((512, 512), np.float32)
    u1, u2 = np.meshgrid(np.arange(128), np.arange(4), indexing="ij")
    place[(u2 * 128 + u1).ravel(), (u2 + 4 * u1).ravel()] = 1.0
    return bands, twiddle, turn, inner, last, place.astype(jnp.bfloat16)


def split_two(x):
    high = x.astype(jnp.bfloat16)
    low = (x - high.astype(jnp.float32)).astype(jnp.bfloat16)
    return high, low


def mm(a, b):
    return jnp.dot(a, b, preferred_element_type=jnp.float32)


ROOT = math.sqrt(0.5)


def eight(x):
    def add(p, q):
        return (p[0] + q[0], p[1] + q[1])

    def sub(p, q):
        return (p[0] - q[0], p[1] - q[1])

    def turn(p):
        return (-p[1], p[0])

    def addi(p, q):
        return (p[0] - q[1], p[1] + q[0])

    def subi(p, q):
        return (p[0] + q[1], p[1] - q[0])

    def four(z):
        s02, d02 = add(z[0], z[2]), sub(z[0], z[2])
        s13, d13 = add(z[1], z[3]), sub(z[1], z[3])
        return [add(s02, s13), addi(d02, d13), sub(s02, s13), subi(d02, d13)]

    ev = four([x[0], x[2], x[4], x[6]])
    od = four([x[1], x[3], x[5], x[7]])
    o1 = ((od[1][0] - od[1][1]) * ROOT, (od[1][0] + od[1][1]) * ROOT)
    o3 = ((od[3][0] + od[3][1]) * ROOT, (od[3][1] - od[3][0]) * ROOT)
    return [
        add(ev[0], od[0]),
        add(ev[1], o1),
        addi(ev[2], od[2]),
        sub(ev[3], o3),
        sub(ev[0], od[0]),
        sub(ev[1], o1),
        subi(ev[2], od[2]),
        add(ev[3], o3),
    ]


def four_point(z):
    s0 = (z[0][0] + z[2][0], z[0][1] + z[2][1])
    d0 = (z[0][0] - z[2][0], z[0][1] - z[2][1])
    s1 = (z[1][0] + z[3][0], z[1][1] + z[3][1])
    d1 = (z[1][0] - z[3][0], z[1][1] - z[3][1])
    return [
        (s0[0] + s1[0], s0[1] + s1[1]),
        (d0[0] - d1[1], d0[1] + d1[0]),
        (s0[0] - s1[0], s0[1] - s1[1]),
        (d0[0] + d1[1], d0[1] - d1[0]),
    ]


def times(x, c, s):
    return (x[0] * c - x[1] * s, x[0] * s + x[1] * c)


def prepare(part, det, slides, antenna, net, ramp):
    column = (
        lax.broadcasted_iota(jnp.int32, (32, LANES), 0) * LANES
        + lax.broadcasted_iota(jnp.int32, (32, LANES), 1)
    )
    tau = lax.broadcasted_iota(jnp.int32, (OUT_ROWS, 256), 0)
    row = 64 * (part & 1) + 32 * (tau >> 4) + 16 * (part >> 1) + (tau & 15)
    packed = lax.broadcasted_iota(jnp.int32, (OUT_ROWS, 256), 1)
    bin_row = (packed >> 3) * 4 + (packed & 3)
    quarter = ((packed >> 2) & 1) * (FOLD // 4)
    for side in range(2):
        which = det if side == 0 else 1 - det
        first = which == 0
        weight_re = jnp.where(first, antenna[0, 0], antenna[1, 0])
        weight_im = jnp.where(first, antenna[0, 1], antenna[1, 1])
        for slide in range(2):
            shift = which * jnp.where(det == 0, slides[slide], slides[2 + slide])
            angle = (((row + shift) * bin_row + quarter) & (FOLD - 1)).astype(jnp.float32) * (2.0 * math.pi / FOLD)
            for half, table in ((0, jnp.cos(angle)), (1, jnp.sin(angle))):
                high, low = split_two(table)
                at = slice(64 * slide + 32 * half, 64 * slide + 32 * half + 32)
                net[side, 0, at, :] = high
                net[side, 1, at, :] = low
            angle = ((column * shift) & (BINS - 1)).astype(jnp.float32) * (2.0 * math.pi / BINS)
            cos, sin = jnp.cos(angle), jnp.sin(angle)
            ramp[slide, 2 * side] = weight_re * cos - weight_im * sin
            ramp[slide, 2 * side + 1] = weight_re * sin + weight_im * cos


def first_stage(chunk, det, bounds, tmpl, signal, bands, net, series, xe, xo, xn, power):
    start = pl.multiple_of(chunk * CHUNK, CHUNK)
    cols = pl.ds(start, CHUNK)
    src = lax.broadcasted_iota(jnp.int32, (2, 8, CHUNK), 0)
    sub = lax.broadcasted_iota(jnp.int32, (2, 8, CHUNK), 1)
    lane = lax.broadcasted_iota(jnp.int32, (2, 8, CHUNK), 2)
    top = sub < 4
    place_in = (src * 4 + (sub & 3)) * COLS + lane + start

    def group(i, carry):
        y, low_z, x = i // 4, (i // 2) % 2, pl.ds(2 * (i % 2), 2)
        rows = pl.ds(pl.multiple_of(16 * i, 16), 16)
        wave = tmpl[y, low_z, x, :, cols]
        rolled = pltpu.roll(wave, 4, 1)
        wave_re = jnp.where(top, wave, rolled)
        wave_im = jnp.where(top, rolled, -wave)
        own = signal[det, y, low_z, x, :, cols]
        own = own * wave_re + pltpu.roll(own, 4, 1) * wave_im
        oth = signal[1 - det, y, low_z, x, :, cols]
        oth = oth * wave_re + pltpu.roll(oth, 4, 1) * wave_im
        slot = (i + 1) // 2
        edge = jnp.where(slot == 0, 0, jnp.where(slot == BANDS, BINS, bounds[jnp.clip(slot - 1, 0, BANDS - 2)]))
        upper = (place_in + 8 * i * COLS) >= edge
        even = upper == (slot % 2 == 0)
        squares = wave * wave
        low_sum = jnp.where(upper, 0.0, squares)

        def fold(v):
            v = v[0] + v[1]
            return v[:, 0:128] + v[:, 128:256] + v[:, 256:384] + v[:, 384:512]

        power[i, 0] += fold(low_sum)
        power[i, 1] += fold(squares)
        high = own.astype(jnp.bfloat16).astype(jnp.float32)
        low = own - high

        def keep(value):
            return value.reshape(16, CHUNK).astype(jnp.bfloat16)

        xe[0, rows, :] = keep(jnp.where(even, high, 0.0))
        xe[1, rows, :] = keep(jnp.where(even, low, 0.0))
        xo[0, rows, :] = keep(jnp.where(even, 0.0, high))
        xo[1, rows, :] = keep(jnp.where(even, 0.0, low))
        high, low = split_two(oth.reshape(16, CHUNK))
        xn[0, rows, :] = high
        xn[1, rows, :] = low
        return carry

    lax.fori_loop(0, 16, group, 0)

    def three(high, low, x):
        return mm(high, x[0]) + mm(low, x[0]) + mm(high, x[1])

    def put(first, value):
        rows = value.shape[0] // 8
        for tile in range(CHUNK // LANES):
            piece = value[:, tile * LANES : (tile + 1) * LANES].reshape(rows, 8, LANES)
            series[pl.ds(first, rows), chunk * (CHUNK // LANES) + tile] = piece

    put(0, three(bands[0], bands[1], xe))
    put(32, three(bands[2], bands[3], xo))
    put(64, three(net[0, 0], net[0, 1], xe) + three(net[0, 0], net[0, 1], xo))
    put(80, three(net[1, 0], net[1, 1], xn))


def power_shares(power):
    powers = []
    for band in range(BANDS):
        acc = jnp.zeros((8, LANES), jnp.float32)
        for i in range(16):
            bound = (i - 1) // 2
            if bound == band:
                acc += power[i, 0]
            if bound + 1 == band:
                acc += power[i, 1] - power[i, 0]
        powers.append(jnp.sum(jnp.sum(acc, axis=0, keepdims=True), axis=1, keepdims=True))
    total = sum(powers)
    return total, [value / total for value in powers]


def second_stage(eb, total, shares, response, series, twiddle, turn, inner, last, place, ramp, zbuf, bbuf, vbuf, rows):
    inverse = [(1.0 / (2 * BANDS - 2)) / (total * share) for share in shares]
    net_scale = 1.0 / (total * response)
    cos, sin = twiddle[0, eb], twiddle[1, eb]
    inner_re, inner_im = inner[0][:, None, :], inner[1][:, None, :]

    def transform(item, z):
        z = times(z, cos, sin)
        re, im = z[0].reshape(8, 4, 8, LANES), z[1].reshape(8, 4, 8, LANES)
        values = eight([(re[s], im[s]) for s in range(8)])
        values = [values[0]] + [times(values[v], turn[0, v], turn[1, v]) for v in range(1, 8)]
        re = jnp.stack([value[0] for value in values])
        im = jnp.stack([value[1] for value in values])
        done = four_point([(re[:, r2], im[:, r2]) for r2 in range(4)])
        re = jnp.concatenate([value[0] for value in done], axis=0)
        im = jnp.concatenate([value[1] for value in done], axis=0)
        z = times((re, im), inner_re, inner_im)
        slot = item % 2
        zbuf[slot, :, 0:LANES] = z[0].reshape(256, LANES)
        zbuf[slot, :, LANES : 2 * LANES] = z[1].reshape(256, LANES)
        high, low = split_two(zbuf[slot])
        bbuf[item] = mm(high, last[0]) + mm(low, last[0]) + mm(high, last[1])

    for item in range(BANDS):
        base = (item // 2) * 8 + (item % 2) * 32 + eb
        transform(item, (series[base], series[base + 4]))
    for slide in range(2):
        own = (series[64 + 8 * slide + eb], series[64 + 8 * slide + 4 + eb])
        oth = (series[80 + 8 * slide + eb], series[80 + 8 * slide + 4 + eb])
        line = [ramp[slide, k][:, None, :] for k in range(4)]
        own, oth = times(own, line[0], line[1]), times(oth, line[2], line[3])
        transform(BANDS + slide, (own[0] + oth[0], own[1] + oth[1]))

    for u2 in range(4):
        part = slice(64 * u2, 64 * u2 + 64)
        re = [bbuf[band, part, 0:LANES] for band in range(BANDS)]
        im = [bbuf[band, part, LANES : 2 * LANES] for band in range(BANDS)]
        whole_re, whole_im = sum(re), sum(im)
        chi = None
        for band in range(BANDS):
            gap_re = re[band] - shares[band] * whole_re
            gap_im = im[band] - shares[band] * whole_im
            term = (gap_re * gap_re + gap_im * gap_im) * inverse[band]
            chi = term if chi is None else chi + term
        columns = slice(u2 * LANES, (u2 + 1) * LANES)
        vbuf[0:64, columns] = chi
        for slide in range(2):
            re = bbuf[BANDS + slide, part, 0:LANES]
            im = bbuf[BANDS + slide, part, LANES : 2 * LANES]
            vbuf[64 + 64 * slide : 128 + 64 * slide, columns] = (re * re + im * im) * net_scale
    high, low = split_two(vbuf[...])
    done = mm(high, place[...]) + mm(low, place[...])
    for kind in range(3):
        for v in range(8):
            both = done[kind * 64 + v * 8 : kind * 64 + v * 8 + 8, :]
            rows[kind, 2 * eb, :, v * 512 : (v + 1) * 512] = both[0:4]
            rows[kind, 2 * eb + 1, :, v * 512 : (v + 1) * 512] = both[4:8]


def compute_scratch():
    return [
        pltpu.VMEM((2, 2, 128, 256), jnp.bfloat16),
        pltpu.VMEM((2, 4, 32, LANES), jnp.float32),
        pltpu.VMEM((96, 32, 8, LANES), jnp.float32),
        pltpu.VMEM((2, 256, CHUNK), jnp.bfloat16),
        pltpu.VMEM((2, 256, CHUNK), jnp.bfloat16),
        pltpu.VMEM((2, 256, CHUNK), jnp.bfloat16),
        pltpu.VMEM((16, 2, 8, LANES), jnp.float32),
        pltpu.VMEM((2, 256, 256), jnp.float32),
        pltpu.VMEM((10, 256, 256), jnp.float32),
        pltpu.VMEM((192, 512), jnp.float32),
        pltpu.VMEM((4, 256, 256), jnp.bfloat16),
        pltpu.VMEM((2, 4, 32, 8, LANES), jnp.float32),
        pltpu.VMEM((2, 8, 4, 8, LANES), jnp.float32),
        pltpu.VMEM((2, 32, LANES), jnp.float32),
        pltpu.VMEM((2, 256, 256), jnp.bfloat16),
        pltpu.VMEM((512, 512), jnp.bfloat16),
    ]


MESH = pl.DeviceIdType.MESH
HALF = COLS // 2
PORTIONS = ((0, 640), (640, 640), (1280, 768))
ORDERS = (("x", "y", "z"), ("y", "z", "x"), ("z", "x", "y"))


def kernel(
    assign, bounds, slides, antenna, bank, strain, bands_hbm, twiddle_hbm, turn_hbm, inner_hbm, last_hbm, place_hbm,
    chi, net_out, tmpl, signal, everything, staged, loaded, packed, rows,
    local_sem, swap_send, swap_recv, wide_send, wide_recv, pass_send, pass_recv,
    far_send, far_recv, deep_send, deep_recv, near_send, near_recv, out_send, out_recv, table_sem,
    net, ramp, series, xe, xo, xn, power, zbuf, bbuf, vbuf, bands, twiddle, turn, inner, last, place,
):
    det, grp, tm = lax.axis_index("det"), lax.axis_index("grp"), lax.axis_index("tm")
    low_z = (tm // 4) % 2
    here = {"y": tm // 8, "z": det * 2 + low_z, "x": tm % 4}
    peer = {"grp": 1 - grp}
    half = pl.ds(pl.multiple_of(grp * HALF, HALF), HALF)
    other = pl.ds(pl.multiple_of((1 - grp) * HALF, HALF), HALF)

    def moved(axis, by):
        there = dict(here)
        there[axis] = (here[axis] + by + 4) % 4
        return there

    def ident(place):
        return {"det": place["z"] // 2, "tm": place["y"] * 8 + (place["z"] % 2) * 4 + place["x"]}

    def shifted(d, sign=1):
        there = dict(here)
        there["y"] = (here["y"] + sign * (d // 4) + 4) % 4
        there["x"] = (here["x"] + sign * (d % 4) + 4) % 4
        return there

    keep = pltpu.make_async_copy(bank.at[:, :, :, half], everything.at[pl.ds(grp * 8, 8)], local_sem.at[0])
    keep.start()
    own = pltpu.make_async_copy(strain, loaded, local_sem.at[1])
    own.start()

    part = 2 * low_z + grp
    tables = [
        pltpu.make_async_copy(src, dst, table_sem.at[i])
        for i, (src, dst) in enumerate((
            (bands_hbm.at[part], bands), (twiddle_hbm.at[part], twiddle), (turn_hbm, turn),
            (inner_hbm, inner), (last_hbm, last), (place_hbm, place),
        ))
    ]
    for copy in tables:
        copy.start()

    to_grp = here["y"] // 2
    same_core = to_grp == grp
    slot_at = 4 * (here["y"] % 2) + here["x"]

    def target(i):
        return (2 * grp + i // 4) * 8 + low_z * 4 + i % 4

    barrier = pltpu.get_barrier_semaphore()

    def greet(d, carry):
        pl.semaphore_signal(barrier, inc=1, device_id=ident(shifted(d)), device_id_type=MESH)
        return carry

    lax.fori_loop(1, 16, greet, 0)
    for d in (1, 2, 3):
        pl.semaphore_signal(barrier, inc=1, device_id=ident(moved("z", d)), device_id_type=MESH)
    pl.semaphore_signal(barrier, inc=1, device_id=peer, device_id_type=MESH)

    @pl.when(same_core)
    def _():
        pl.semaphore_wait(barrier, 19)

    @pl.when(jnp.logical_not(same_core))
    def _():
        def greet_other(i, carry):
            pl.semaphore_signal(
                barrier, inc=1, device_id={"grp": 1 - grp, "tm": target(i)}, device_id_type=MESH
            )
            return carry

        lax.fori_loop(0, 8, greet_other, 0)
        pl.semaphore_wait(barrier, 27)

    def remote(src, dst, send, recv, device):
        return pltpu.make_async_remote_copy(
            src_ref=src, dst_ref=dst, send_sem=send, recv_sem=recv, device_id=device, device_id_type=MESH
        )

    swap = remote(bank.at[:, :, :, other], everything.at[pl.ds(grp * 8, 8)], swap_send, swap_recv, peer)
    swap.start()

    def columns(portion, core):
        first, width = PORTIONS[portion]
        return pl.ds(pl.multiple_of(core * HALF + first, LANES), width)

    def region(portion, stage, place, core, part=None):
        done = ORDERS[portion][:stage]
        cut = "x" if ORDERS[portion][2] == "y" else "y"

        def every(axis, value, size):
            if axis not in done:
                return value
            if part is not None and axis == cut:
                return pl.ds(2 * part, 2)
            return pl.ds(0, size)

        return signal.at[
            every("z", place["z"] // 2, 2), every("y", place["y"], 4), every("z", place["z"] % 2, 2),
            every("x", place["x"], 4), :, columns(portion, core),
        ]

    def wide(portion, stage, d):
        dst = region(portion, stage, here, grp)
        src = packed.at[:, columns(portion, grp)] if stage == 0 else dst
        at = (portion, stage, d - 1)
        return remote(src, dst, wide_send.at[at], wide_recv.at[at], ident(moved(ORDERS[portion][stage], d)))

    def relay(portion, part):
        axis = ORDERS[portion][2]
        got = region(portion, 2, moved(axis, -1 if part == 0 else 1), grp, part)
        at = (portion, 2 + part, 1)
        return remote(got, got, wide_send.at[at], wide_recv.at[at], ident(moved(axis, 1 if part == 0 else -1)))

    def incoming(portion, stage, d, core):
        axis = ORDERS[portion][min(stage, 2)]
        if stage < 2 or d != 2:
            part = None
        else:
            part = stage - 2
        return region(portion, min(stage, 2), moved(axis, -d), core, part), (portion, stage, d - 1)

    def arrived(portion, stage, d):
        got, at = incoming(portion, stage, d, grp)
        remote(got, got, wide_send.at[at], wide_recv.at[at], peer).wait_recv()
        remote(got, got, pass_send.at[at], pass_recv.at[at], peer).start()

    own.wait()
    packed[0:4, :] = loaded[0, 0]
    packed[4:8, :] = loaded[0, 1]
    for portion in range(3):
        for d in (1, 3, 2):
            wide(portion, 0, d).start()
    mine = pltpu.make_async_copy(packed, signal.at[det, here["y"], low_z, here["x"]], local_sem.at[1])
    mine.start()

    swap.wait_recv()
    keep.wait()
    for slot in range(16):
        wave = everything[assign[slot]]
        staged[slot, 0:4, :] = wave[0]
        staged[slot, 4:8, :] = wave[1]

    def far(d):
        to = shifted(d)
        return remote(
            staged.at[to["y"] * 4 + to["x"]], tmpl.at[here["y"], low_z, here["x"], :, half],
            far_send.at[d], far_recv.at[d], ident(to),
        )

    def piece(place, plane, columns):
        return tmpl.at[place["y"], plane, place["x"], :, columns]

    def deep(place):
        got = piece(place, low_z, half)
        at = place["y"] * 4 + place["x"]
        to = moved("z", jnp.where(place["y"] < 2, 1, 3))
        return remote(got, got, deep_send.at[at], deep_recv.at[at], ident(to))

    def near(place, plane, columns):
        got = piece(place, plane, columns)
        at = (plane, place["y"] * 4 + place["x"])
        return remote(got, got, near_send.at[at], near_recv.at[at], peer)

    def send_far(d, carry):
        far(d).start()
        return carry

    lax.fori_loop(1, 16, send_far, 0)
    slot_here = here["y"] * 4 + here["x"]
    kept = pltpu.make_async_copy(staged.at[slot_here], piece(here, low_z, half), local_sem.at[2])
    kept.start()

    prepare(part, det, slides, antenna, net, ramp)
    power[...] = jnp.zeros_like(power)
    mine.wait()
    for portion in range(3):
        for d in (1, 3, 2):
            arrived(portion, 0, d)
        for d in (1, 3, 2):
            wide(portion, 1, d).start()
    kept.wait()
    deep(here).start()
    near(here, low_z, half).start()

    def got_far(d, carry):
        place = shifted(d, -1)
        got = piece(place, low_z, half)
        remote(got, got, far_send.at[d], far_recv.at[d], peer).wait_recv()
        deep(place).start()
        near(place, low_z, half).start()
        return carry

    lax.fori_loop(1, 16, got_far, 0)
    for portion in range(3):
        for d in (1, 3, 2):
            arrived(portion, 1, d)
        for d in (1, 3):
            wide(portion, 2, d).start()

    def place_at(p):
        return {"y": p // 4, "x": p % 4}

    def got_deep(p, carry):
        got = piece(place_at(p), 1 - low_z, half)
        remote(got, got, deep_send.at[p], deep_recv.at[p], peer).wait_recv()
        near(place_at(p), 1 - low_z, half).start()
        return carry

    lax.fori_loop(0, 16, got_deep, 0)
    for portion in range(3):
        for d, part in ((1, 0), (3, 1)):
            arrived(portion, 2, d)
            relay(portion, part).start()
    for portion in range(3):
        for part in range(2):
            arrived(portion, 2 + part, 2)

    def arrivals(p, carry):
        for plane in range(2):
            near(place_at(p), plane, other).wait_recv()
        return carry

    lax.fori_loop(0, 16, arrivals, 0)
    events = ((0, 1), (0, 2), (0, 3), (1, 1), (1, 2), (1, 3), (2, 1), (2, 3), (2, 2), (3, 2))
    for portion in range(3):
        for stage, d in events:
            come, at = incoming(portion, stage, d, 1 - grp)
            remote(come, come, pass_send.at[at], pass_recv.at[at], peer).wait_recv()
    for copy in tables:
        copy.wait()

    def chunk(i, carry):
        first_stage(i, det, bounds, tmpl, signal, bands, net, series, xe, xo, xn, power)
        return carry

    lax.fori_loop(0, STEPS, chunk, 0)
    total, shares = power_shares(power)
    response = sum(antenna[d, c] * antenna[d, c] for d in range(2) for c in range(2))

    def parts(i):
        return ((rows.at[0, i], chi.at[slot_at]), (rows.at[pl.ds(1, 2), i], net_out.at[slot_at]))

    def give(i, kind):
        src, dst = parts(i)[kind]
        return pltpu.make_async_remote_copy(
            src_ref=src, dst_ref=dst, send_sem=out_send.at[kind, i], recv_sem=out_recv.at[kind, slot_at],
            device_id={"grp": to_grp, "tm": target(i)}, device_id_type=MESH,
        )

    def block(eb, carry):
        second_stage(
            eb, total, shares, response, series, twiddle, turn, inner, last, place, ramp, zbuf, bbuf, vbuf, rows
        )
        for k in range(2):
            i = 2 * eb + k
            is_self = (target(i) == tm) & same_core
            for kind in range(2):
                @pl.when(is_self)
                def _():
                    src, dst = parts(i)[kind]
                    pltpu.make_async_copy(src, dst, out_recv.at[kind, slot_at]).start()

                @pl.when(jnp.logical_not(is_self))
                def _():
                    give(i, kind).start()
        return carry

    lax.fori_loop(0, 4, block, 0)

    swap.wait_send()

    def rest(p, carry):
        deep(place_at(p)).wait_send()
        for plane in range(2):
            near(place_at(p), plane, half).wait_send()

        @pl.when(p > 0)
        def _():
            far(p).wait_send()

        return carry

    lax.fori_loop(0, 16, rest, 0)
    for portion in range(3):
        for stage, d in events:
            if stage < 2 or d != 2:
                wide(portion, stage, d).wait_send()
            else:
                relay(portion, stage - 2).wait_send()
            got, at = incoming(portion, stage, d, grp)
            remote(got, got, pass_send.at[at], pass_recv.at[at], peer).wait_send()

    def finish(i, carry):
        is_self = (target(i) == tm) & same_core
        for kind, dst in ((0, chi), (1, net_out)):
            pltpu.make_async_copy(dst.at[i], dst.at[i], out_recv.at[kind, i]).wait()

            @pl.when(jnp.logical_not(is_self))
            def _():
                give(i, kind).wait_send()
        return carry

    lax.fori_loop(0, 8, finish, 0)


def on_device(strain, bank, assignment, slides, bounds, antenna):
    dma = pltpu.SemaphoreType.DMA
    smem, hbm = pl.BlockSpec(memory_space=pltpu.SMEM), pl.BlockSpec(memory_space=pltpu.HBM)
    chi, net = pl.pallas_call(
        kernel,
        out_shape=(
            jax.ShapeDtypeStruct((8, 4, COLS), jnp.float32),
            jax.ShapeDtypeStruct((8, 2, 4, COLS), jnp.float32),
        ),
        in_specs=[smem] * 4 + [hbm] * 8,
        out_specs=[hbm, hbm],
        scratch_shapes=[
            pltpu.VMEM((4, 2, 4, 8, COLS), jnp.float32),
            pltpu.VMEM((2, 4, 2, 4, 8, COLS), jnp.float32),
            pltpu.VMEM((16, 2, 4, HALF), jnp.float32),
            pltpu.VMEM((16, 8, HALF), jnp.float32),
            pltpu.VMEM((1, 2, 4, COLS), jnp.float32),
            pltpu.VMEM((8, COLS), jnp.float32),
            pltpu.VMEM((3, 8, 4, COLS), jnp.float32),
            dma((3,)), dma, dma, dma((3, 4, 3)), dma((3, 4, 3)), dma((3, 4, 3)), dma((3, 4, 3)),
            dma((16,)), dma((16,)), dma((16,)), dma((16,)), dma((2, 16)), dma((2, 16)), dma((2, 8)), dma((2, 8)),
            dma((6,)),
        ] + compute_scratch(),
        compiler_params=pltpu.CompilerParams(collective_id=0, has_side_effects=True, vmem_limit_bytes=60 * 2**20),
        cost_estimate=pl.CostEstimate(flops=20 * 10**9, bytes_accessed=20 * 10**6, transcendentals=0),
    )(assignment, bounds, slides, antenna, bank, strain, *[jnp.asarray(table) for table in constant_tables()])
    return chi[None], net


def solution(mesh):
    P = jax.sharding.PartitionSpec
    return jax.shard_map(
        on_device,
        mesh=mesh,
        in_specs=(P("det", None, "tm", None), P("grp", None, "tm", None), P(), P(), P(), P()),
        out_specs=(P("det", "grp", "tm", None), P("grp", "det", "tm", None)),
        check_vma=False,
    )
```

```python
import functools
import math

import jax
import jax.numpy as jnp
import numpy as np
from jax import lax
from jax.experimental import pallas as pl
from jax.experimental.pallas import tpu as pltpu

FOLD = 128
COLS = 4096
BINS = FOLD * COLS
BANDS = 8
CHUNK = 512
STEPS = COLS // CHUNK
LANES = 128
OUT_ROWS = 32


def rows_of(part):
    tau = np.arange(OUT_ROWS)
    return 64 * (part % 2) + 32 * (tau // 16) + 16 * (part // 2) + tau % 16


def halves(table):
    high = np.asarray(table, np.float32).astype(jnp.bfloat16)
    low = (np.asarray(table, np.float64) - high.astype(np.float64)).astype(np.float32)
    return high, low.astype(jnp.bfloat16)


def pack_columns(real, imag):
    m = real.shape[0]
    parts = np.stack([real.reshape(m, 32, 4), imag.reshape(m, 32, 4)], axis=2)
    return parts.reshape(m, 256)


def stacked_rows(cos, sin):
    top = pack_columns(cos, -sin)
    bottom = pack_columns(sin, cos)
    return np.concatenate([top, bottom], axis=0)


def constant_tables():
    b = np.arange(FOLD)
    even, odd, twiddle = [], [], []
    for part in range(4):
        e = rows_of(part)
        angle = 2 * np.pi * ((e[:, None] * b[None, :]) % FOLD) / FOLD
        cos, sin = np.cos(angle), np.sin(angle)
        for parity, group in ((0, even), (1, odd)):
            blocks = []
            for band in range(parity, BANDS, 2):
                inside = (b >= 16 * band - 8) & (b < 16 * band + 24)
                blocks.append(stacked_rows(cos * inside, sin * inside))
            group.append(np.concatenate(blocks, axis=0))
        a = np.arange(COLS)
        angle = 2 * np.pi * (e[:, None] * a[None, :]) / BINS
        twiddle.append(np.stack([np.cos(angle), np.sin(angle)]))
    even = halves(np.stack(even))
    odd = halves(np.stack(odd))
    bands = np.stack([even[0], even[1], odd[0], odd[1]], axis=1)
    twiddle = np.stack(twiddle).astype(np.float32).reshape(4, 2, 4, 8, 32, LANES).swapaxes(3, 4).copy()
    a1 = np.arange(LANES)
    q2 = np.arange(32)
    v, r2 = np.meshgrid(np.arange(8), np.arange(4), indexing="ij")
    angle = (2 * np.pi * v * r2 / 32)[..., None, None] * np.ones((8, LANES))
    turn = np.stack([np.cos(angle), np.sin(angle)]).astype(np.float32)
    angle = 2 * np.pi * (a1[None, :] * q2[:, None]) / COLS
    inner = np.stack([np.cos(angle), np.sin(angle)]).astype(np.float32)
    angle = 2 * np.pi * ((a1[:, None] * a1[None, :]) % LANES) / LANES
    cos, sin = np.cos(angle), np.sin(angle)
    last = np.stack(halves(np.block([[cos, sin], [-sin, cos]])))
    place = np.zeros((512, 512), np.float32)
    u1, u2 = np.meshgrid(np.arange(128), np.arange(4), indexing="ij")
    place[(u2 * 128 + u1).ravel(), (u2 + 4 * u1).ravel()] = 1.0
    return bands, twiddle, turn, inner, last, place.astype(jnp.bfloat16)


def split_two(x):
    high = x.astype(jnp.bfloat16)
    low = (x - high.astype(jnp.float32)).astype(jnp.bfloat16)
    return high, low


def mm(a, b):
    return jnp.dot(a, b, preferred_element_type=jnp.float32)


ROOT = math.sqrt(0.5)


def eight(x):
    def add(p, q):
        return (p[0] + q[0], p[1] + q[1])

    def sub(p, q):
        return (p[0] - q[0], p[1] - q[1])

    def turn(p):
        return (-p[1], p[0])

    def addi(p, q):
        return (p[0] - q[1], p[1] + q[0])

    def subi(p, q):
        return (p[0] + q[1], p[1] - q[0])

    def four(z):
        s02, d02 = add(z[0], z[2]), sub(z[0], z[2])
        s13, d13 = add(z[1], z[3]), sub(z[1], z[3])
        return [add(s02, s13), addi(d02, d13), sub(s02, s13), subi(d02, d13)]

    ev = four([x[0], x[2], x[4], x[6]])
    od = four([x[1], x[3], x[5], x[7]])
    o1 = ((od[1][0] - od[1][1]) * ROOT, (od[1][0] + od[1][1]) * ROOT)
    o3 = ((od[3][0] + od[3][1]) * ROOT, (od[3][1] - od[3][0]) * ROOT)
    return [
        add(ev[0], od[0]),
        add(ev[1], o1),
        addi(ev[2], od[2]),
        sub(ev[3], o3),
        sub(ev[0], od[0]),
        sub(ev[1], o1),
        subi(ev[2], od[2]),
        add(ev[3], o3),
    ]


def four_point(z):
    s0 = (z[0][0] + z[2][0], z[0][1] + z[2][1])
    d0 = (z[0][0] - z[2][0], z[0][1] - z[2][1])
    s1 = (z[1][0] + z[3][0], z[1][1] + z[3][1])
    d1 = (z[1][0] - z[3][0], z[1][1] - z[3][1])
    return [
        (s0[0] + s1[0], s0[1] + s1[1]),
        (d0[0] - d1[1], d0[1] + d1[0]),
        (s0[0] - s1[0], s0[1] - s1[1]),
        (d0[0] + d1[1], d0[1] - d1[0]),
    ]


def times(x, c, s):
    return (x[0] * c - x[1] * s, x[0] * s + x[1] * c)


def prepare(part, det, slides, antenna, net, ramp):
    column = (
        lax.broadcasted_iota(jnp.int32, (32, LANES), 0) * LANES
        + lax.broadcasted_iota(jnp.int32, (32, LANES), 1)
    )
    tau = lax.broadcasted_iota(jnp.int32, (OUT_ROWS, 256), 0)
    row = 64 * (part & 1) + 32 * (tau >> 4) + 16 * (part >> 1) + (tau & 15)
    packed = lax.broadcasted_iota(jnp.int32, (OUT_ROWS, 256), 1)
    bin_row = (packed >> 3) * 4 + (packed & 3)
    quarter = ((packed >> 2) & 1) * (FOLD // 4)
    for side in range(2):
        which = det if side == 0 else 1 - det
        first = which == 0
        weight_re = jnp.where(first, antenna[0, 0], antenna[1, 0])
        weight_im = jnp.where(first, antenna[0, 1], antenna[1, 1])
        for slide in range(2):
            shift = which * jnp.where(det == 0, slides[slide], slides[2 + slide])
            angle = (((row + shift) * bin_row + quarter) & (FOLD - 1)).astype(jnp.float32) * (2.0 * math.pi / FOLD)
            for half, table in ((0, jnp.cos(angle)), (1, jnp.sin(angle))):
                high, low = split_two(table)
                at = slice(64 * slide + 32 * half, 64 * slide + 32 * half + 32)
                net[side, 0, at, :] = high
                net[side, 1, at, :] = low
            angle = ((column * shift) & (BINS - 1)).astype(jnp.float32) * (2.0 * math.pi / BINS)
            cos, sin = jnp.cos(angle), jnp.sin(angle)
            ramp[slide, 2 * side] = weight_re * cos - weight_im * sin
            ramp[slide, 2 * side + 1] = weight_re * sin + weight_im * cos


def column_block(step):
    return 2 * (step // 4) + step % 2 + 4 * ((step // 2) % 2)


def products(step, det, bounds, tmpl, signal, held, power):
    start = pl.multiple_of(column_block(step) * CHUNK, CHUNK)
    cols = pl.ds(start, CHUNK)
    src = lax.broadcasted_iota(jnp.int32, (2, 8, CHUNK), 0)
    sub = lax.broadcasted_iota(jnp.int32, (2, 8, CHUNK), 1)
    lane = lax.broadcasted_iota(jnp.int32, (2, 8, CHUNK), 2)
    top = sub < 4
    place_in = (src * 4 + (sub & 3)) * COLS + lane + start

    def fold(v):
        v = v[0] + v[1]
        return v[:, 0:128] + v[:, 128:256] + v[:, 256:384] + v[:, 384:512]

    def keep(value):
        return value.reshape(16, CHUNK).astype(jnp.bfloat16)

    for i in range(16):
        y, low_z, x = i // 4, (i // 2) % 2, slice(2 * (i % 2), 2 * (i % 2) + 2)
        rows = slice(16 * i, 16 * i + 16)
        wave = tmpl[y, low_z, x, :, cols]
        rolled = pltpu.roll(wave, 4, 1)
        wave_re = jnp.where(top, wave, rolled)
        wave_im = jnp.where(top, rolled, -wave)
        own = signal[det, y, low_z, x, :, cols]
        own = own * wave_re + pltpu.roll(own, 4, 1) * wave_im
        oth = signal[1 - det, y, low_z, x, :, cols]
        oth = oth * wave_re + pltpu.roll(oth, 4, 1) * wave_im
        bound = (i - 1) // 2
        squares = wave * wave
        high = own.astype(jnp.bfloat16).astype(jnp.float32)
        low = own - high
        if 0 <= bound < BANDS - 1:
            upper = place_in >= bounds[bound] - 8 * i * COLS
            power[i, 0] += fold(jnp.where(upper, 0.0, squares))
            cut = lambda value: jnp.where(upper, 0.0, value)
            high_low, low_low = cut(high), cut(low)
            lower = (keep(high_low), keep(low_low))
            higher = (keep(high - high_low), keep(low - low_low))
            even, odd = (higher, lower) if bound % 2 else (lower, higher)
        else:
            zero = jnp.zeros((16, CHUNK), jnp.bfloat16)
            even, odd = (keep(high), keep(low)), (zero, zero)
            if bound == BANDS - 1:
                even, odd = odd, even
                power[i, 0] += fold(squares)
        power[i, 1] += fold(squares)
        held[0, rows, :], held[1, rows, :] = even
        held[2, rows, :], held[3, rows, :] = odd
        held[4, rows, :], held[5, rows, :] = split_two(oth.reshape(16, CHUNK))


def first_stage(step, held, bands, net, series):
    tiles = CHUNK // LANES
    block = column_block(step) * tiles

    def three(high, low, k):
        return mm(high, held[k]) + mm(low, held[k]) + mm(high, held[k + 1])

    def put(first, value):
        rows = value.shape[0] // 8
        for tile in range(tiles):
            piece = value[:, tile * LANES : (tile + 1) * LANES].reshape(rows, 8, LANES)
            series[pl.ds(first, rows), block + tile] = piece

    put(0, three(bands[0], bands[1], 0))
    put(32, three(bands[2], bands[3], 2))
    put(64, three(net[0, 0], net[0, 1], 0) + three(net[0, 0], net[0, 1], 2))
    put(80, three(net[1, 0], net[1, 1], 4))


def power_shares(power):
    powers = []
    for band in range(BANDS):
        acc = jnp.zeros((8, LANES), jnp.float32)
        for i in range(16):
            bound = (i - 1) // 2
            if bound == band:
                acc += power[i, 0]
            if bound + 1 == band:
                acc += power[i, 1] - power[i, 0]
        powers.append(jnp.sum(jnp.sum(acc, axis=0, keepdims=True), axis=1, keepdims=True))
    total = sum(powers)
    return total, [value / total for value in powers]


def second_stage(eb, total, shares, response, series, twiddle, turn, inner, last, place, ramp, zbuf, bbuf, vbuf, rows):
    inverse = [(1.0 / (2 * BANDS - 2)) / (total * share) for share in shares]
    net_scale = 1.0 / (total * response)
    cos, sin = twiddle[0, eb], twiddle[1, eb]
    inner_re, inner_im = inner[0][:, None, :], inner[1][:, None, :]

    def transform(item, z):
        z = times(z, cos, sin)
        re, im = z[0].reshape(8, 4, 8, LANES), z[1].reshape(8, 4, 8, LANES)
        values = eight([(re[s], im[s]) for s in range(8)])
        values = [values[0]] + [times(values[v], turn[0, v], turn[1, v]) for v in range(1, 8)]
        re = jnp.stack([value[0] for value in values])
        im = jnp.stack([value[1] for value in values])
        done = four_point([(re[:, r2], im[:, r2]) for r2 in range(4)])
        re = jnp.concatenate([value[0] for value in done], axis=0)
        im = jnp.concatenate([value[1] for value in done], axis=0)
        z = times((re, im), inner_re, inner_im)
        slot = item % 2
        zbuf[slot, :, 0:LANES] = z[0].reshape(256, LANES)
        zbuf[slot, :, LANES : 2 * LANES] = z[1].reshape(256, LANES)
        high, low = split_two(zbuf[slot])
        bbuf[item] = mm(high, last[0]) + mm(low, last[0]) + mm(high, last[1])

    for item in range(BANDS):
        base = (item // 2) * 8 + (item % 2) * 32 + eb
        transform(item, (series[base], series[base + 4]))
    for slide in range(2):
        own = (series[64 + 8 * slide + eb], series[64 + 8 * slide + 4 + eb])
        oth = (series[80 + 8 * slide + eb], series[80 + 8 * slide + 4 + eb])
        line = [ramp[slide, k][:, None, :] for k in range(4)]
        own, oth = times(own, line[0], line[1]), times(oth, line[2], line[3])
        transform(BANDS + slide, (own[0] + oth[0], own[1] + oth[1]))

    for u2 in range(4):
        part = slice(64 * u2, 64 * u2 + 64)
        re = [bbuf[band, part, 0:LANES] for band in range(BANDS)]
        im = [bbuf[band, part, LANES : 2 * LANES] for band in range(BANDS)]
        whole_re, whole_im = sum(re), sum(im)
        chi = None
        for band in range(BANDS):
            gap_re = re[band] - shares[band] * whole_re
            gap_im = im[band] - shares[band] * whole_im
            term = (gap_re * gap_re + gap_im * gap_im) * inverse[band]
            chi = term if chi is None else chi + term
        columns = slice(u2 * LANES, (u2 + 1) * LANES)
        vbuf[0:64, columns] = chi
        for slide in range(2):
            re = bbuf[BANDS + slide, part, 0:LANES]
            im = bbuf[BANDS + slide, part, LANES : 2 * LANES]
            vbuf[64 + 64 * slide : 128 + 64 * slide, columns] = (re * re + im * im) * net_scale
    high, low = split_two(vbuf[...])
    done = mm(high, place[...]) + mm(low, place[...])
    for kind in range(3):
        for v in range(8):
            both = done[kind * 64 + v * 8 : kind * 64 + v * 8 + 8, :]
            rows[kind, 2 * eb, :, v * 512 : (v + 1) * 512] = both[0:4]
            rows[kind, 2 * eb + 1, :, v * 512 : (v + 1) * 512] = both[4:8]


def compute_scratch():
    return [
        pltpu.VMEM((2, 2, 128, 256), jnp.bfloat16),
        pltpu.VMEM((2, 4, 32, LANES), jnp.float32),
        pltpu.VMEM((96, 32, 8, LANES), jnp.float32),
        pltpu.VMEM((6, 256, CHUNK), jnp.bfloat16),
        pltpu.VMEM((6, 256, CHUNK), jnp.bfloat16),
        pltpu.VMEM((16, 2, 8, LANES), jnp.float32),
        pltpu.VMEM((2, 256, 256), jnp.float32),
        pltpu.VMEM((10, 256, 256), jnp.float32),
        pltpu.VMEM((192, 512), jnp.float32),
        pltpu.VMEM((4, 256, 256), jnp.bfloat16),
        pltpu.VMEM((2, 4, 32, 8, LANES), jnp.float32),
        pltpu.VMEM((2, 8, 4, 8, LANES), jnp.float32),
        pltpu.VMEM((2, 32, LANES), jnp.float32),
        pltpu.VMEM((2, 256, 256), jnp.bfloat16),
        pltpu.VMEM((512, 512), jnp.bfloat16),
    ]


MESH = pl.DeviceIdType.MESH
HALF = COLS // 2
PORTIONS = ((0, 384), (384, 384), (768, 256), (1024, 384), (1408, 256), (1664, 384))
ORDERS = (("x", "y", "z"), ("y", "z", "x"), ("z", "x", "y")) * 2
EARLY, LATE = (0, 1, 2), (3, 4, 5)
FAR = (1, 4, 3, 12, 5, 15, 7, 13, 2, 8, 6, 9, 11, 14, 10)


def kernel(
    assign, bounds, slides, antenna, bank, strain, bands_hbm, twiddle_hbm, turn_hbm, inner_hbm, last_hbm, place_hbm,
    chi, net_out, tmpl, signal, everything, staged, loaded, packed, rows,
    local_sem, swap_send, swap_recv, wide_send, wide_recv, pass_send, pass_recv,
    far_send, far_recv, deep_send, deep_recv, near_send, near_recv, out_send, out_recv, table_sem,
    net, ramp, series, held_a, held_b, power, zbuf, bbuf, vbuf, bands, twiddle, turn, inner, last, place,
):
    det, grp, tm = lax.axis_index("det"), lax.axis_index("grp"), lax.axis_index("tm")
    low_z = (tm // 4) % 2
    here = {"y": tm // 8, "z": det * 2 + low_z, "x": tm % 4}
    peer = {"grp": 1 - grp}
    half = pl.ds(pl.multiple_of(grp * HALF, HALF), HALF)
    other = pl.ds(pl.multiple_of((1 - grp) * HALF, HALF), HALF)

    def moved(axis, by):
        there = dict(here)
        there[axis] = (here[axis] + by + 4) % 4
        return there

    def ident(place):
        return {"det": place["z"] // 2, "tm": place["y"] * 8 + (place["z"] % 2) * 4 + place["x"]}

    def shifted(d, sign=1):
        there = dict(here)
        there["y"] = (here["y"] + sign * (d // 4) + 4) % 4
        there["x"] = (here["x"] + sign * (d % 4) + 4) % 4
        return there

    keep = pltpu.make_async_copy(bank.at[:, :, :, half], everything.at[pl.ds(grp * 8, 8)], local_sem.at[0])
    keep.start()
    own = pltpu.make_async_copy(strain, loaded, local_sem.at[1])
    own.start()

    part = 2 * low_z + grp
    tables = [
        pltpu.make_async_copy(src, dst, table_sem.at[i])
        for i, (src, dst) in enumerate((
            (bands_hbm.at[part], bands), (twiddle_hbm.at[part], twiddle), (turn_hbm, turn),
            (inner_hbm, inner), (last_hbm, last), (place_hbm, place),
        ))
    ]
    for copy in tables:
        copy.start()

    to_grp = here["y"] // 2
    same_core = to_grp == grp
    slot_at = 4 * (here["y"] % 2) + here["x"]

    def target(i):
        return (2 * grp + i // 4) * 8 + low_z * 4 + i % 4

    barrier = pltpu.get_barrier_semaphore()

    def greet(d, carry):
        pl.semaphore_signal(barrier, inc=1, device_id=ident(shifted(d)), device_id_type=MESH)
        return carry

    lax.fori_loop(1, 16, greet, 0)
    for d in (1, 2, 3):
        pl.semaphore_signal(barrier, inc=1, device_id=ident(moved("z", d)), device_id_type=MESH)
    pl.semaphore_signal(barrier, inc=1, device_id=peer, device_id_type=MESH)

    pl.semaphore_wait(barrier, 19)

    def remote(src, dst, send, recv, device):
        return pltpu.make_async_remote_copy(
            src_ref=src, dst_ref=dst, send_sem=send, recv_sem=recv, device_id=device, device_id_type=MESH
        )

    swap = remote(bank.at[:, :, :, other], everything.at[pl.ds(grp * 8, 8)], swap_send, swap_recv, peer)
    swap.start()

    def columns(portion, core):
        first, width = PORTIONS[portion]
        return pl.ds(pl.multiple_of(core * HALF + first, LANES), width)

    def region(portion, stage, place, core, part=None):
        done = ORDERS[portion][:stage]
        cut = "x" if ORDERS[portion][2] == "y" else "y"

        def every(axis, value, size):
            if axis not in done:
                return value
            if part is not None and axis == cut:
                return pl.ds(2 * part, 2)
            return pl.ds(0, size)

        return signal.at[
            every("z", place["z"] // 2, 2), every("y", place["y"], 4), every("z", place["z"] % 2, 2),
            every("x", place["x"], 4), :, columns(portion, core),
        ]

    def wide(portion, stage, d):
        dst = region(portion, stage, here, grp)
        src = packed.at[:, columns(portion, grp)] if stage == 0 else dst
        at = (portion, stage, d - 1)
        return remote(src, dst, wide_send.at[at], wide_recv.at[at], ident(moved(ORDERS[portion][stage], d)))

    def relay(portion, part):
        axis = ORDERS[portion][2]
        got = region(portion, 2, moved(axis, -1 if part == 0 else 1), grp, part)
        at = (portion, 2 + part, 1)
        return remote(got, got, wide_send.at[at], wide_recv.at[at], ident(moved(axis, 1 if part == 0 else -1)))

    def incoming(portion, stage, d, core):
        axis = ORDERS[portion][min(stage, 2)]
        if stage < 2 or d != 2:
            part = None
        else:
            part = stage - 2
        return region(portion, min(stage, 2), moved(axis, -d), core, part), (portion, stage, d - 1)

    def arrived(portion, stage, d):
        got, at = incoming(portion, stage, d, grp)
        remote(got, got, wide_send.at[at], wide_recv.at[at], peer).wait_recv()
        remote(got, got, pass_send.at[at], pass_recv.at[at], peer).start()

    def pass_on(portions):
        for portion in portions:
            for d, part in ((1, 0), (3, 1)):
                arrived(portion, 2, d)
                relay(portion, part).start()

    def pass_last(portions):
        for portion in portions:
            for part in range(2):
                arrived(portion, 2 + part, 2)

    def pass_first(portions):
        for portion in portions:
            for d in (1, 3, 2):
                arrived(portion, 0, d)
            for d in (1, 3, 2):
                wide(portion, 1, d).start()

    def pass_second(portions):
        for portion in portions:
            for d in (1, 3, 2):
                arrived(portion, 1, d)
            for d in (1, 3):
                wide(portion, 2, d).start()

    own.wait()
    packed[0:4, :] = loaded[0, 0]
    packed[4:8, :] = loaded[0, 1]
    for portion in EARLY + LATE:
        for d in (1, 3, 2):
            wide(portion, 0, d).start()
    mine = pltpu.make_async_copy(packed, signal.at[det, here["y"], low_z, here["x"]], local_sem.at[1])
    mine.start()

    swap.wait_recv()
    keep.wait()
    for slot in range(16):
        wave = everything[assign[slot]]
        staged[slot, 0:4, :] = wave[0]
        staged[slot, 4:8, :] = wave[1]

    def far(d):
        to = shifted(d)
        return remote(
            staged.at[to["y"] * 4 + to["x"]], tmpl.at[here["y"], low_z, here["x"], :, half],
            far_send.at[d], far_recv.at[d], ident(to),
        )

    def piece(place, plane, columns):
        return tmpl.at[place["y"], plane, place["x"], :, columns]

    def deep(place):
        got = piece(place, low_z, half)
        at = place["y"] * 4 + place["x"]
        to = moved("z", 1 + 2 * (place["x"] % 2))
        return remote(got, got, deep_send.at[at], deep_recv.at[at], ident(to))

    def near(place, plane, columns):
        got = piece(place, plane, columns)
        at = (plane, place["y"] * 4 + place["x"])
        return remote(got, got, near_send.at[at], near_recv.at[at], peer)

    mine.wait()
    pass_first(EARLY)
    for d in FAR:
        far(d).start()
    slot_here = here["y"] * 4 + here["x"]
    kept = pltpu.make_async_copy(staged.at[slot_here], piece(here, low_z, half), local_sem.at[2])
    kept.start()

    prepare(part, det, slides, antenna, net, ramp)
    power[...] = jnp.zeros_like(power)
    kept.wait()
    deep(here).start()
    near(here, low_z, half).start()

    def place_at(p):
        return {"y": p // 4, "x": p % 4}

    def got_far(order):
        for d in order:
            place = shifted(d, -1)
            got = piece(place, low_z, half)
            remote(got, got, far_send.at[d], far_recv.at[d], peer).wait_recv()
            deep(place).start()
            near(place, low_z, half).start()

    def got_deep(order):
        for d in order:
            place = shifted(d, -1)
            got = piece(place, 1 - low_z, half)
            at = place["y"] * 4 + place["x"]
            remote(got, got, deep_send.at[at], deep_recv.at[at], peer).wait_recv()
            near(place, 1 - low_z, half).start()

    pass_first(LATE)
    got_far(FAR[:4])
    pass_second(EARLY)
    got_far(FAR[4:8])
    pass_second(LATE)
    got_far(FAR[8:12])
    got_deep((0,) + FAR[:4])
    got_far(FAR[12:])
    pass_on(EARLY)
    got_deep(FAR[4:12])
    pass_on(LATE)
    got_deep(FAR[12:])
    pass_last(EARLY)

    events = ((0, 1), (0, 2), (0, 3), (1, 1), (1, 2), (1, 3), (2, 1), (2, 3), (2, 2), (3, 2))

    def complete(portions):
        for portion in portions:
            for stage, d in events:
                come, at = incoming(portion, stage, d, 1 - grp)
                remote(come, come, pass_send.at[at], pass_recv.at[at], peer).wait_recv()


    def arrivals(p, carry):
        for plane in range(2):
            near(place_at(p), plane, other).wait_recv()
        return carry

    lax.fori_loop(0, 16, arrivals, 0)
    complete(EARLY)
    for copy in tables:
        copy.wait()

    def build(step, held):
        products(step, det, bounds, tmpl, signal, held, power)

    def pair(p, carry):
        first_stage(2 * p, held_a, bands, net, series)
        build(2 * p + 1, held_b)

        @pl.when(p == 1)
        def _():
            pass_last(LATE)
            complete(LATE)

        first_stage(2 * p + 1, held_b, bands, net, series)
        build(2 * p + 2, held_a)

        return carry

    build(0, held_a)
    lax.fori_loop(0, 3, pair, 0)
    first_stage(6, held_a, bands, net, series)
    build(7, held_b)
    first_stage(7, held_b, bands, net, series)
    total, shares = power_shares(power)
    response = sum(antenna[d, c] * antenna[d, c] for d in range(2) for c in range(2))

    def parts(i):
        return ((rows.at[0, i], chi.at[slot_at]), (rows.at[pl.ds(1, 2), i], net_out.at[slot_at]))

    def give(i, kind):
        src, dst = parts(i)[kind]
        return pltpu.make_async_remote_copy(
            src_ref=src, dst_ref=dst, send_sem=out_send.at[kind, i], recv_sem=out_recv.at[kind, slot_at],
            device_id={"grp": to_grp, "tm": target(i)}, device_id_type=MESH,
        )

    def block(step, carry):
        eb = (2 * (here["y"] % 2) + here["x"] // 2) ^ (3 - step)
        second_stage(
            eb, total, shares, response, series, twiddle, turn, inner, last, place, ramp, zbuf, bbuf, vbuf, rows
        )
        for k in range(2):
            i = 2 * eb + k
            is_self = (target(i) == tm) & same_core
            for kind in range(2):
                @pl.when(is_self)
                def _():
                    src, dst = parts(i)[kind]
                    pltpu.make_async_copy(src, dst, out_recv.at[kind, slot_at]).start()

                @pl.when(jnp.logical_not(is_self))
                def _():
                    give(i, kind).start()
        return carry

    lax.fori_loop(0, 4, block, 0)

    swap.wait_send()

    def rest(p, carry):
        deep(place_at(p)).wait_send()
        for plane in range(2):
            near(place_at(p), plane, half).wait_send()

        @pl.when(p > 0)
        def _():
            far(p).wait_send()

        return carry

    lax.fori_loop(0, 16, rest, 0)
    for portion in EARLY + LATE:
        for stage, d in events:
            if stage < 2 or d != 2:
                wide(portion, stage, d).wait_send()
            else:
                relay(portion, stage - 2).wait_send()
            got, at = incoming(portion, stage, d, grp)
            remote(got, got, pass_send.at[at], pass_recv.at[at], peer).wait_send()

    def finish(i, carry):
        is_self = (target(i) == tm) & same_core
        for kind, dst in ((0, chi), (1, net_out)):
            pltpu.make_async_copy(dst.at[i], dst.at[i], out_recv.at[kind, i]).wait()

            @pl.when(jnp.logical_not(is_self))
            def _():
                give(i, kind).wait_send()
        return carry

    lax.fori_loop(0, 8, finish, 0)


def settle_kernel(chi, net, chi_out, net_out):
    chi_out[...] = chi[...]
    net_out[...] = net[...]


def settle(chi, net):
    one = pl.BlockSpec((4, 4, COLS), lambda i: (i, 0, 0))
    two = pl.BlockSpec((4, 2, 4, COLS), lambda i: (i, 0, 0, 0))
    chi, net = pl.pallas_call(
        settle_kernel,
        grid=(2,),
        out_shape=(jax.ShapeDtypeStruct(chi.shape, chi.dtype), jax.ShapeDtypeStruct(net.shape, net.dtype)),
        in_specs=[one, two],
        out_specs=[one, two],
        compiler_params=pltpu.CompilerParams(vmem_limit_bytes=60 * 2**20),
        cost_estimate=pl.CostEstimate(flops=0, bytes_accessed=3 * 2**20, transcendentals=0),
    )(chi, net)
    return chi[None], net


def on_device(strain, bank, assignment, slides, bounds, antenna):
    dma = pltpu.SemaphoreType.DMA
    smem, hbm = pl.BlockSpec(memory_space=pltpu.SMEM), pl.BlockSpec(memory_space=pltpu.HBM)
    chi, net = pl.pallas_call(
        kernel,
        out_shape=(
            jax.ShapeDtypeStruct((8, 4, COLS), jnp.float32),
            jax.ShapeDtypeStruct((8, 2, 4, COLS), jnp.float32),
        ),
        in_specs=[smem] * 4 + [hbm] * 8,
        out_specs=[hbm, hbm],
        scratch_shapes=[
            pltpu.VMEM((4, 2, 4, 8, COLS), jnp.float32),
            pltpu.VMEM((2, 4, 2, 4, 8, COLS), jnp.float32),
            pltpu.VMEM((16, 2, 4, HALF), jnp.float32),
            pltpu.VMEM((16, 8, HALF), jnp.float32),
            pltpu.VMEM((1, 2, 4, COLS), jnp.float32),
            pltpu.VMEM((8, COLS), jnp.float32),
            pltpu.VMEM((3, 8, 4, COLS), jnp.float32),
            dma((3,)), dma, dma, dma((6, 4, 3)), dma((6, 4, 3)), dma((6, 4, 3)), dma((6, 4, 3)),
            dma((16,)), dma((16,)), dma((16,)), dma((16,)), dma((2, 16)), dma((2, 16)), dma((2, 8)), dma((2, 8)),
            dma((6,)),
        ] + compute_scratch(),
        compiler_params=pltpu.CompilerParams(collective_id=0, has_side_effects=True, vmem_limit_bytes=60 * 2**20),
        cost_estimate=pl.CostEstimate(flops=20 * 10**9, bytes_accessed=20 * 10**6, transcendentals=0),
    )(assignment, bounds, slides, antenna, bank, strain, *[jnp.asarray(table) for table in constant_tables()])
    return settle(chi, net)


def solution(mesh):
    P = jax.sharding.PartitionSpec
    return jax.shard_map(
        on_device,
        mesh=mesh,
        in_specs=(P("det", None, "tm", None), P("grp", None, "tm", None), P(), P(), P(), P()),
        out_specs=(P("det", "grp", "tm", None), P("grp", "det", "tm", None)),
        check_vma=False,
    )
```

```python
import functools
import math

import jax
import jax.numpy as jnp
import numpy as np
from jax import lax
from jax.experimental import pallas as pl
from jax.experimental.pallas import tpu as pltpu

FOLD = 128
COLS = 4096
BINS = FOLD * COLS
BANDS = 8
CHUNK = 512
STEPS = COLS // CHUNK
LANES = 128
OUT_ROWS = 32


def rows_of(part):
    tau = np.arange(OUT_ROWS)
    return 64 * (part % 2) + 32 * (tau // 16) + 16 * (part // 2) + tau % 16


def halves(table):
    high = np.asarray(table, np.float32).astype(jnp.bfloat16)
    low = (np.asarray(table, np.float64) - high.astype(np.float64)).astype(np.float32)
    return high, low.astype(jnp.bfloat16)


def pack_columns(real, imag):
    m = real.shape[0]
    parts = np.stack([real.reshape(m, 32, 4), imag.reshape(m, 32, 4)], axis=2)
    return parts.reshape(m, 256)


def stacked_rows(cos, sin):
    top = pack_columns(cos, -sin)
    bottom = pack_columns(sin, cos)
    return np.concatenate([top, bottom], axis=0)


def constant_tables():
    b = np.arange(FOLD)
    even, odd, twiddle = [], [], []
    for part in range(4):
        e = rows_of(part)
        angle = 2 * np.pi * ((e[:, None] * b[None, :]) % FOLD) / FOLD
        cos, sin = np.cos(angle), np.sin(angle)
        for parity, group in ((0, even), (1, odd)):
            blocks = []
            for band in range(parity, BANDS, 2):
                inside = (b >= 16 * band - 8) & (b < 16 * band + 24)
                blocks.append(stacked_rows(cos * inside, sin * inside))
            group.append(np.concatenate(blocks, axis=0))
        a = np.arange(COLS)
        angle = 2 * np.pi * (e[:, None] * a[None, :]) / BINS
        twiddle.append(np.stack([np.cos(angle), np.sin(angle)]))
    even = halves(np.stack(even))
    odd = halves(np.stack(odd))
    bands = np.stack([np.stack([even[1], even[0]], axis=1), np.stack([odd[1], odd[0]], axis=1)], axis=1)
    twiddle = np.stack(twiddle).astype(np.float32).reshape(4, 2, 4, 8, 32, LANES).swapaxes(3, 4).copy()
    a1 = np.arange(LANES)
    q2 = np.arange(32)
    v, r2 = np.meshgrid(np.arange(8), np.arange(4), indexing="ij")
    angle = (2 * np.pi * v * r2 / 32)[..., None, None] * np.ones((8, LANES))
    turn = np.stack([np.cos(angle), np.sin(angle)]).astype(np.float32)
    angle = 2 * np.pi * (a1[None, :] * q2[:, None]) / COLS
    inner = np.stack([np.cos(angle), np.sin(angle)]).astype(np.float32)
    angle = 2 * np.pi * ((a1[:, None] * a1[None, :]) % LANES) / LANES
    cos, sin = np.cos(angle), np.sin(angle)
    last = np.stack(halves(np.block([[cos, sin], [-sin, cos]])))
    place = np.zeros((512, 512), np.float32)
    u1, u2 = np.meshgrid(np.arange(128), np.arange(4), indexing="ij")
    place[(u2 * 128 + u1).ravel(), (u2 + 4 * u1).ravel()] = 1.0
    return bands, twiddle, turn, inner, last, place.astype(jnp.bfloat16)


def split_two(x):
    high = x.astype(jnp.bfloat16)
    low = (x - high.astype(jnp.float32)).astype(jnp.bfloat16)
    return high, low


def mm(a, b):
    return jnp.dot(a, b, preferred_element_type=jnp.float32)


ROOT = math.sqrt(0.5)


def eight(x):
    def add(p, q):
        return (p[0] + q[0], p[1] + q[1])

    def sub(p, q):
        return (p[0] - q[0], p[1] - q[1])

    def turn(p):
        return (-p[1], p[0])

    def addi(p, q):
        return (p[0] - q[1], p[1] + q[0])

    def subi(p, q):
        return (p[0] + q[1], p[1] - q[0])

    def four(z):
        s02, d02 = add(z[0], z[2]), sub(z[0], z[2])
        s13, d13 = add(z[1], z[3]), sub(z[1], z[3])
        return [add(s02, s13), addi(d02, d13), sub(s02, s13), subi(d02, d13)]

    ev = four([x[0], x[2], x[4], x[6]])
    od = four([x[1], x[3], x[5], x[7]])
    o1 = ((od[1][0] - od[1][1]) * ROOT, (od[1][0] + od[1][1]) * ROOT)
    o3 = ((od[3][0] + od[3][1]) * ROOT, (od[3][1] - od[3][0]) * ROOT)
    return [
        add(ev[0], od[0]),
        add(ev[1], o1),
        addi(ev[2], od[2]),
        sub(ev[3], o3),
        sub(ev[0], od[0]),
        sub(ev[1], o1),
        subi(ev[2], od[2]),
        add(ev[3], o3),
    ]


def four_point(z):
    s0 = (z[0][0] + z[2][0], z[0][1] + z[2][1])
    d0 = (z[0][0] - z[2][0], z[0][1] - z[2][1])
    s1 = (z[1][0] + z[3][0], z[1][1] + z[3][1])
    d1 = (z[1][0] - z[3][0], z[1][1] - z[3][1])
    return [
        (s0[0] + s1[0], s0[1] + s1[1]),
        (d0[0] - d1[1], d0[1] + d1[0]),
        (s0[0] - s1[0], s0[1] - s1[1]),
        (d0[0] + d1[1], d0[1] - d1[0]),
    ]


def times(x, c, s):
    return (x[0] * c - x[1] * s, x[0] * s + x[1] * c)


def prepare(part, det, slides, antenna, bands, net, ramp):
    column = (
        lax.broadcasted_iota(jnp.int32, (32, LANES), 0) * LANES
        + lax.broadcasted_iota(jnp.int32, (32, LANES), 1)
    )
    tau = lax.broadcasted_iota(jnp.int32, (OUT_ROWS, 256), 0)
    row = 64 * (part & 1) + 32 * (tau >> 4) + 16 * (part >> 1) + (tau & 15)
    packed = lax.broadcasted_iota(jnp.int32, (OUT_ROWS, 256), 1)
    bin_row = (packed >> 3) * 4 + (packed & 3)
    quarter = ((packed >> 2) & 1) * (FOLD // 4)
    for side in range(2):
        which = det if side == 0 else 1 - det
        first = which == 0
        weight_re = jnp.where(first, antenna[0, 0], antenna[1, 0])
        weight_im = jnp.where(first, antenna[0, 1], antenna[1, 1])
        for slide in range(2):
            shift = which * jnp.where(det == 0, slides[slide], slides[2 + slide])
            angle = (((row + shift) * bin_row + quarter) & (FOLD - 1)).astype(jnp.float32) * (2.0 * math.pi / FOLD)
            for half, table in ((0, jnp.cos(angle)), (1, jnp.sin(angle))):
                high, low = split_two(table)
                at = 64 * slide + 32 * half
                if side == 0:
                    for parity in range(2):
                        bands[parity, 256 + at : 288 + at, :] = low
                        bands[parity, 640 + at : 672 + at, :] = high
                else:
                    net[at : at + 32, :] = low
                    net[128 + at : 160 + at, :] = high
            angle = ((column * shift) & (BINS - 1)).astype(jnp.float32) * (2.0 * math.pi / BINS)
            cos, sin = jnp.cos(angle), jnp.sin(angle)
            ramp[slide, 2 * side] = weight_re * cos - weight_im * sin
            ramp[slide, 2 * side + 1] = weight_re * sin + weight_im * cos


def column_block(step):
    return jnp.where(step < 6, step % 3 + 4 * (step // 3), 4 * step - 21)


def products(step, det, bounds, tmpl, signal, held, power):
    start = pl.multiple_of(column_block(step) * CHUNK, CHUNK)
    cols = pl.ds(start, CHUNK)
    src = lax.broadcasted_iota(jnp.int32, (2, 8, CHUNK), 0)
    sub = lax.broadcasted_iota(jnp.int32, (2, 8, CHUNK), 1)
    lane = lax.broadcasted_iota(jnp.int32, (2, 8, CHUNK), 2)
    top = sub < 4
    place_in = (src * 4 + (sub & 3)) * COLS + lane + start

    def fold(v):
        v = v[0] + v[1]
        return v[:, 0:128] + v[:, 128:256] + v[:, 256:384] + v[:, 384:512]

    def keep(value):
        return value.reshape(16, CHUNK).astype(jnp.bfloat16)

    for i in range(16):
        y, low_z, x = i // 4, (i // 2) % 2, slice(2 * (i % 2), 2 * (i % 2) + 2)
        rows = slice(16 * i, 16 * i + 16)
        wave = tmpl[y, low_z, x, :, cols]
        rolled = pltpu.roll(wave, 4, 1)
        wave_re = jnp.where(top, wave, rolled)
        wave_im = jnp.where(top, rolled, -wave)
        own = signal[det, y, low_z, x, :, cols]
        own = own * wave_re + pltpu.roll(own, 4, 1) * wave_im
        oth = signal[1 - det, y, low_z, x, :, cols]
        oth = oth * wave_re + pltpu.roll(oth, 4, 1) * wave_im
        bound = (i - 1) // 2
        squares = wave * wave
        high = own.astype(jnp.bfloat16).astype(jnp.float32)
        low = own - high
        if 0 <= bound < BANDS - 1:
            upper = place_in >= bounds[bound] - 8 * i * COLS
            power[i, 0] += fold(jnp.where(upper, 0.0, squares))
            cut = lambda value: jnp.where(upper, 0.0, value)
            high_low, low_low = cut(high), cut(low)
            lower = (keep(high_low), keep(low_low))
            higher = (keep(high - high_low), keep(low - low_low))
            even, odd = (higher, lower) if bound % 2 else (lower, higher)
        else:
            zero = jnp.zeros((16, CHUNK), jnp.bfloat16)
            even, odd = (keep(high), keep(low)), (zero, zero)
            if bound == BANDS - 1:
                even, odd = odd, even
                power[i, 0] += fold(squares)
        power[i, 1] += fold(squares)
        held[0, rows, :], held[1, rows, :] = even
        held[2, rows, :], held[3, rows, :] = odd
        held[4, rows, :], held[5, rows, :] = split_two(oth.reshape(16, CHUNK))


def first_stage(step, held, bands, net, series):
    tiles = CHUNK // LANES
    block = column_block(step) * tiles

    def put(first, value):
        rows = value.shape[0] // 8
        for tile in range(tiles):
            piece = value[:, tile * LANES : (tile + 1) * LANES].reshape(rows, 8, LANES)
            series[pl.ds(first, rows), block + tile] = piece

    net_sum = None
    for parity in range(2):
        both = mm(bands[parity], held[2 * parity])
        fine = mm(bands[parity, 384:768, :], held[2 * parity + 1])
        value = both[0:384] + both[384:768] + fine
        put(32 * parity, value[0:256])
        net_sum = value[256:384] if net_sum is None else net_sum + value[256:384]
    put(64, net_sum)
    both = mm(net[...], held[4])
    fine = mm(net[128:256, :], held[5])
    put(80, both[0:128] + both[128:256] + fine)


def power_shares(power):
    powers = []
    for band in range(BANDS):
        acc = jnp.zeros((8, LANES), jnp.float32)
        for i in range(16):
            bound = (i - 1) // 2
            if bound == band:
                acc += power[i, 0]
            if bound + 1 == band:
                acc += power[i, 1] - power[i, 0]
        powers.append(jnp.sum(jnp.sum(acc, axis=0, keepdims=True), axis=1, keepdims=True))
    total = sum(powers)
    return total, [value / total for value in powers]


def second_stage(eb, total, shares, response, series, twiddle, turn, inner, last, place, ramp, zbuf, bbuf, vbuf, rows):
    inverse = [(1.0 / (2 * BANDS - 2)) / (total * share) for share in shares]
    net_scale = 1.0 / (total * response)
    cos, sin = twiddle[0, eb], twiddle[1, eb]
    inner_re, inner_im = inner[0][:, None, :], inner[1][:, None, :]

    def transform(item, z):
        z = times(z, cos, sin)
        re, im = z[0].reshape(8, 4, 8, LANES), z[1].reshape(8, 4, 8, LANES)
        values = eight([(re[s], im[s]) for s in range(8)])
        values = [values[0]] + [times(values[v], turn[0, v], turn[1, v]) for v in range(1, 8)]
        re = jnp.stack([value[0] for value in values])
        im = jnp.stack([value[1] for value in values])
        done = four_point([(re[:, r2], im[:, r2]) for r2 in range(4)])
        re = jnp.concatenate([value[0] for value in done], axis=0)
        im = jnp.concatenate([value[1] for value in done], axis=0)
        z = times((re, im), inner_re, inner_im)
        slot = item % 2
        zbuf[slot, :, 0:LANES] = z[0].reshape(256, LANES)
        zbuf[slot, :, LANES : 2 * LANES] = z[1].reshape(256, LANES)
        high, low = split_two(zbuf[slot])
        bbuf[item] = mm(high, last[0]) + mm(low, last[0]) + mm(high, last[1])

    for item in range(BANDS):
        base = (item // 2) * 8 + (item % 2) * 32 + eb
        transform(item, (series[base], series[base + 4]))
    for slide in range(2):
        own = (series[64 + 8 * slide + eb], series[64 + 8 * slide + 4 + eb])
        oth = (series[80 + 8 * slide + eb], series[80 + 8 * slide + 4 + eb])
        line = [ramp[slide, k][:, None, :] for k in range(4)]
        own, oth = times(own, line[0], line[1]), times(oth, line[2], line[3])
        transform(BANDS + slide, (own[0] + oth[0], own[1] + oth[1]))

    for u2 in range(4):
        part = slice(64 * u2, 64 * u2 + 64)
        re = [bbuf[band, part, 0:LANES] for band in range(BANDS)]
        im = [bbuf[band, part, LANES : 2 * LANES] for band in range(BANDS)]
        whole_re, whole_im = sum(re), sum(im)
        chi = None
        for band in range(BANDS):
            gap_re = re[band] - shares[band] * whole_re
            gap_im = im[band] - shares[band] * whole_im
            term = (gap_re * gap_re + gap_im * gap_im) * inverse[band]
            chi = term if chi is None else chi + term
        columns = slice(u2 * LANES, (u2 + 1) * LANES)
        vbuf[0:64, columns] = chi
        for slide in range(2):
            re = bbuf[BANDS + slide, part, 0:LANES]
            im = bbuf[BANDS + slide, part, LANES : 2 * LANES]
            vbuf[64 + 64 * slide : 128 + 64 * slide, columns] = (re * re + im * im) * net_scale
    high, low = split_two(vbuf[...])
    done = mm(high, place[...]) + mm(low, place[...])
    for kind in range(3):
        for v in range(8):
            both = done[kind * 64 + v * 8 : kind * 64 + v * 8 + 8, :]
            rows[kind, 2 * eb, :, v * 512 : (v + 1) * 512] = both[0:4]
            rows[kind, 2 * eb + 1, :, v * 512 : (v + 1) * 512] = both[4:8]


def compute_scratch():
    return [
        pltpu.VMEM((256, 256), jnp.bfloat16),
        pltpu.VMEM((2, 4, 32, LANES), jnp.float32),
        pltpu.VMEM((96, 32, 8, LANES), jnp.float32),
        pltpu.VMEM((6, 256, CHUNK), jnp.bfloat16),
        pltpu.VMEM((6, 256, CHUNK), jnp.bfloat16),
        pltpu.VMEM((16, 2, 8, LANES), jnp.float32),
        pltpu.VMEM((2, 256, 256), jnp.float32),
        pltpu.VMEM((10, 256, 256), jnp.float32),
        pltpu.VMEM((192, 512), jnp.float32),
        pltpu.VMEM((2, 768, 256), jnp.bfloat16),
        pltpu.VMEM((2, 4, 32, 8, LANES), jnp.float32),
        pltpu.VMEM((2, 8, 4, 8, LANES), jnp.float32),
        pltpu.VMEM((2, 32, LANES), jnp.float32),
        pltpu.VMEM((2, 256, 256), jnp.bfloat16),
        pltpu.VMEM((512, 512), jnp.bfloat16),
    ]


MESH = pl.DeviceIdType.MESH
HALF = COLS // 2
PORTIONS = ((0, 512), (512, 512), (1024, 512), (1536, 128), (1664, 128), (1792, 256))
ORDERS = (("x", "y", "z"), ("y", "z", "x"), ("z", "x", "y")) * 2
EARLY, LATE = (0, 1, 2), (3, 4, 5)
FAR = (1, 4, 3, 12, 5, 15, 7, 13, 2, 8, 6, 9, 11, 14, 10)


def kernel(
    assign, bounds, slides, antenna, bank, strain, bands_hbm, twiddle_hbm, turn_hbm, inner_hbm, last_hbm, place_hbm,
    chi, net_out, tmpl, signal, everything, staged, loaded, packed, rows,
    local_sem, swap_send, swap_recv, wide_send, wide_recv, pass_send, pass_recv,
    far_send, far_recv, deep_send, deep_recv, near_send, near_recv, out_send, out_recv, table_sem,
    net, ramp, series, held_a, held_b, power, zbuf, bbuf, vbuf, bands, twiddle, turn, inner, last, weave,
):
    det, grp, tm = lax.axis_index("det"), lax.axis_index("grp"), lax.axis_index("tm")
    low_z = lax.rem(lax.div(tm, 4), 2)
    here = {"y": lax.div(tm, 8), "z": det * 2 + low_z, "x": lax.rem(tm, 4)}
    onward = {axis: [value] + [lax.rem(value + k, 4) for k in (1, 2, 3)] for axis, value in here.items()}
    split_z = [(det, low_z)] + [(lax.div(z, 2), lax.rem(z, 2)) for z in onward["z"][1:]]
    peer = {"grp": 1 - grp}
    half = pl.ds(pl.multiple_of(grp * HALF, HALF), HALF)
    other = pl.ds(pl.multiple_of((1 - grp) * HALF, HALF), HALF)

    AXES = ("y", "z", "x")

    def moved(axis, by):
        return tuple(by % 4 if name == axis else 0 for name in AXES)

    def shifted(d, sign=1):
        return ((sign * (d // 4)) % 4, 0, (sign * (d % 4)) % 4)

    def at_y(place):
        return onward["y"][place[0]]

    def at_x(place):
        return onward["x"][place[2]]

    tm_at = {}

    def ident(place):
        if place not in tm_at:
            tm_at[place] = at_y(place) * 8 + split_z[place[1]][1] * 4 + at_x(place)
        return {"det": split_z[place[1]][0], "tm": tm_at[place]}

    slots = {}

    def number(place):
        if place not in slots:
            slots[place] = at_y(place) * 4 + at_x(place)
        return slots[place]

    HERE = (0, 0, 0)
    PLANE = [shifted(d) for d in range(16)]
    for place in PLANE + [moved("z", d) for d in (1, 2, 3)]:
        ident(place)
        number(place)

    keep = pltpu.make_async_copy(bank.at[:, :, :, half], everything.at[pl.ds(grp * 8, 8)], local_sem.at[0])
    keep.start()
    own = pltpu.make_async_copy(strain, loaded, local_sem.at[1])
    own.start()

    part = 2 * low_z + grp
    tables = [
        pltpu.make_async_copy(src, dst, table_sem.at[i])
        for i, (src, dst) in enumerate((
            (bands_hbm.at[part, 0, 0], bands.at[0, pl.ds(0, 256)]), (bands_hbm.at[part, 0, 1], bands.at[0, pl.ds(384, 256)]),
            (bands_hbm.at[part, 1, 0], bands.at[1, pl.ds(0, 256)]), (bands_hbm.at[part, 1, 1], bands.at[1, pl.ds(384, 256)]),
            (twiddle_hbm.at[part], twiddle), (turn_hbm, turn),
            (inner_hbm, inner), (last_hbm, last), (place_hbm, weave),
        ))
    ]
    for copy in tables:
        copy.start()

    to_grp = lax.div(here["y"], 2)
    same_core = to_grp == grp
    slot_at = 4 * lax.rem(here["y"], 2) + here["x"]

    def target(i):
        return (2 * grp + i // 4) * 8 + low_z * 4 + i % 4

    barrier = pltpu.get_barrier_semaphore()

    for place in PLANE[1:]:
        pl.semaphore_signal(barrier, inc=1, device_id=ident(place), device_id_type=MESH)
    for d in (1, 2, 3):
        pl.semaphore_signal(barrier, inc=1, device_id=ident(moved("z", d)), device_id_type=MESH)
    pl.semaphore_signal(barrier, inc=1, device_id=peer, device_id_type=MESH)

    pl.semaphore_wait(barrier, 19)

    def remote(src, dst, send, recv, device):
        return pltpu.make_async_remote_copy(
            src_ref=src, dst_ref=dst, send_sem=send, recv_sem=recv, device_id=device, device_id_type=MESH
        )

    swap = remote(bank.at[:, :, :, other], everything.at[pl.ds(grp * 8, 8)], swap_send, swap_recv, peer)
    swap.start()

    def columns(portion, core):
        first, width = PORTIONS[portion]
        return pl.ds(pl.multiple_of(core * HALF + first, LANES), width)

    def region(portion, stage, place, core, part=None):
        done = ORDERS[portion][:stage]
        cut = "x" if ORDERS[portion][2] == "y" else "y"

        def every(axis, value, size):
            if axis not in done:
                return value
            if part is not None and axis == cut:
                return pl.ds(2 * part, 2)
            return pl.ds(0, size)

        return signal.at[
            every("z", split_z[place[1]][0], 2), every("y", at_y(place), 4), every("z", split_z[place[1]][1], 2),
            every("x", at_x(place), 4), :, columns(portion, core),
        ]

    def wide(portion, stage, d):
        dst = region(portion, stage, HERE, grp)
        src = packed.at[:, columns(portion, grp)] if stage == 0 else dst
        at = (portion, stage, d - 1)
        return remote(src, dst, wide_send.at[at], wide_recv.at[at], ident(moved(ORDERS[portion][stage], d)))

    def relay(portion, part):
        axis = ORDERS[portion][2]
        got = region(portion, 2, moved(axis, -1 if part == 0 else 1), grp, part)
        at = (portion, 2 + part, 1)
        return remote(got, got, wide_send.at[at], wide_recv.at[at], ident(moved(axis, 1 if part == 0 else -1)))

    def incoming(portion, stage, d, core):
        axis = ORDERS[portion][min(stage, 2)]
        if stage < 2 or d != 2:
            part = None
        else:
            part = stage - 2
        return region(portion, min(stage, 2), moved(axis, -d), core, part), (portion, stage, d - 1)

    def arrived(portion, stage, d):
        got, at = incoming(portion, stage, d, grp)
        remote(got, got, wide_send.at[at], wide_recv.at[at], peer).wait_recv()
        remote(got, got, pass_send.at[at], pass_recv.at[at], peer).start()

    def pass_on(portions):
        for portion in portions:
            for d, part in ((1, 0), (3, 1)):
                arrived(portion, 2, d)
                relay(portion, part).start()

    def pass_last(portions):
        for portion in portions:
            for part in range(2):
                arrived(portion, 2 + part, 2)

    def pass_first(portions):
        for portion in portions:
            for d in (1, 3, 2):
                arrived(portion, 0, d)
            for d in (1, 3, 2):
                wide(portion, 1, d).start()

    def pass_second(portions):
        for portion in portions:
            for d in (1, 3, 2):
                arrived(portion, 1, d)
            for d in (1, 3):
                wide(portion, 2, d).start()

    own.wait()
    packed[0:4, :] = loaded[0, 0]
    packed[4:8, :] = loaded[0, 1]
    for portion in EARLY + LATE:
        for d in (1, 3, 2):
            wide(portion, 0, d).start()
    mine = pltpu.make_async_copy(packed, signal.at[det, here["y"], low_z, here["x"]], local_sem.at[1])
    mine.start()

    swap.wait_recv()
    keep.wait()
    for slot in range(16):
        wave = everything[assign[slot]]
        staged[slot, 0:4, :] = wave[0]
        staged[slot, 4:8, :] = wave[1]

    def far(d):
        to = shifted(d)
        return remote(
            staged.at[number(to)], tmpl.at[here["y"], low_z, here["x"], :, half],
            far_send.at[d], far_recv.at[d], ident(to),
        )

    def piece(place, plane, columns):
        return tmpl.at[at_y(place), plane, at_x(place), :, columns]

    def deep(place):
        got = piece(place, low_z, half)
        to = moved("z", 1 + 2 * (place[2] % 2))
        at = DEEP(place)
        return remote(got, got, deep_send.at[at], deep_recv.at[at], ident(to))

    def DEEP(place):
        return place[0] * 4 + place[2]

    def near(place, plane, columns):
        got = piece(place, low_z if plane == 0 else 1 - low_z, columns)
        at = (plane, DEEP(place))
        return remote(got, got, near_send.at[at], near_recv.at[at], peer)

    mine.wait()
    pass_first(EARLY)
    for d in FAR:
        far(d).start()
    kept = pltpu.make_async_copy(staged.at[number(HERE)], piece(HERE, low_z, half), local_sem.at[2])
    kept.start()
    prepare(part, det, slides, antenna, bands, net, ramp)
    power[...] = jnp.zeros_like(power)
    kept.wait()
    deep(HERE).start()
    near(HERE, 0, half).start()

    def got_far(order):
        for d in order:
            place = shifted(d, -1)
            got = piece(place, low_z, half)
            remote(got, got, far_send.at[d], far_recv.at[d], peer).wait_recv()
            deep(place).start()
            near(place, 0, half).start()

    def got_deep(order):
        for d in order:
            place = shifted(d, -1)
            got = piece(place, 1 - low_z, half)
            at = DEEP(place)
            remote(got, got, deep_send.at[at], deep_recv.at[at], peer).wait_recv()
            near(place, 1, half).start()

    pass_second(EARLY)
    pass_first(LATE)
    got_far(FAR)
    got_deep((0,) + FAR[:8])
    pass_on(EARLY)
    pass_second(LATE)
    got_deep(FAR[8:])
    pass_last(EARLY)

    events = ((0, 1), (0, 2), (0, 3), (1, 1), (1, 2), (1, 3), (2, 1), (2, 3), (2, 2), (3, 2))

    def complete(portions):
        for portion in portions:
            for stage, d in events:
                come, at = incoming(portion, stage, d, 1 - grp)
                remote(come, come, pass_send.at[at], pass_recv.at[at], peer).wait_recv()


    for place in PLANE:
        for plane in range(2):
            near(place, plane, other).wait_recv()
    complete(EARLY)
    for copy in tables:
        copy.wait()

    def build(step, held):
        products(step, det, bounds, tmpl, signal, held, power)

    def pair(p, carry):
        first_stage(2 * p, held_a, bands, net, series)
        build(2 * p + 1, held_b)

        @pl.when(p == 2)
        def _():
            pass_last(LATE)
            complete(LATE)

        first_stage(2 * p + 1, held_b, bands, net, series)
        build(2 * p + 2, held_a)
        return carry

    build(0, held_a)
    pass_on(LATE)
    lax.fori_loop(0, 3, pair, 0)
    first_stage(6, held_a, bands, net, series)
    build(7, held_b)
    first_stage(7, held_b, bands, net, series)
    total, shares = power_shares(power)
    response = sum(antenna[d, c] * antenna[d, c] for d in range(2) for c in range(2))

    def parts(i):
        return ((rows.at[0, i], chi.at[slot_at]), (rows.at[pl.ds(1, 2), i], net_out.at[slot_at]))

    def give(i, kind):
        src, dst = parts(i)[kind]
        return pltpu.make_async_remote_copy(
            src_ref=src, dst_ref=dst, send_sem=out_send.at[kind, i], recv_sem=out_recv.at[kind, slot_at],
            device_id={"grp": to_grp, "tm": target(i)}, device_id_type=MESH,
        )

    def block(step, carry):
        eb = (2 * lax.rem(here["y"], 2) + lax.div(here["x"], 2)) ^ (3 - step)
        second_stage(
            eb, total, shares, response, series, twiddle, turn, inner, last, weave, ramp, zbuf, bbuf, vbuf, rows
        )
        for k in range(2):
            i = 2 * eb + k
            is_self = (target(i) == tm) & same_core
            for kind in range(2):
                @pl.when(is_self)
                def _():
                    src, dst = parts(i)[kind]
                    pltpu.make_async_copy(src, dst, out_recv.at[kind, slot_at]).start()

                @pl.when(jnp.logical_not(is_self))
                def _():
                    give(i, kind).start()
        return carry

    lax.fori_loop(0, 4, block, 0)

    swap.wait_send()

    for d, place in enumerate(PLANE):
        deep(place).wait_send()
        for plane in range(2):
            near(place, plane, half).wait_send()
        if d > 0:
            far(d).wait_send()
    for portion in EARLY + LATE:
        for stage, d in events:
            if stage < 2 or d != 2:
                wide(portion, stage, d).wait_send()
            else:
                relay(portion, stage - 2).wait_send()
            got, at = incoming(portion, stage, d, grp)
            remote(got, got, pass_send.at[at], pass_recv.at[at], peer).wait_send()

    def finish(i, carry):
        is_self = (target(i) == tm) & same_core
        for kind, dst in ((0, chi), (1, net_out)):
            pltpu.make_async_copy(dst.at[i], dst.at[i], out_recv.at[kind, i]).wait()

            @pl.when(jnp.logical_not(is_self))
            def _():
                give(i, kind).wait_send()
        return carry

    lax.fori_loop(0, 8, finish, 0)


def settle_kernel(chi, net, chi_out, net_out):
    chi_out[...] = chi[...]
    net_out[...] = net[...]


def settle(chi, net):
    one = pl.BlockSpec((4, 4, COLS), lambda i: (i, 0, 0))
    two = pl.BlockSpec((4, 2, 4, COLS), lambda i: (i, 0, 0, 0))
    chi, net = pl.pallas_call(
        settle_kernel,
        grid=(2,),
        out_shape=(jax.ShapeDtypeStruct(chi.shape, chi.dtype), jax.ShapeDtypeStruct(net.shape, net.dtype)),
        in_specs=[one, two],
        out_specs=[one, two],
        compiler_params=pltpu.CompilerParams(vmem_limit_bytes=60 * 2**20),
        cost_estimate=pl.CostEstimate(flops=0, bytes_accessed=3 * 2**20, transcendentals=0),
    )(chi, net)
    return chi[None], net


def on_device(strain, bank, assignment, slides, bounds, antenna):
    dma = pltpu.SemaphoreType.DMA
    smem, hbm = pl.BlockSpec(memory_space=pltpu.SMEM), pl.BlockSpec(memory_space=pltpu.HBM)
    chi, net = pl.pallas_call(
        kernel,
        out_shape=(
            jax.ShapeDtypeStruct((8, 4, COLS), jnp.float32),
            jax.ShapeDtypeStruct((8, 2, 4, COLS), jnp.float32),
        ),
        in_specs=[smem] * 4 + [hbm] * 8,
        out_specs=[hbm, hbm],
        scratch_shapes=[
            pltpu.VMEM((4, 2, 4, 8, COLS), jnp.float32),
            pltpu.VMEM((2, 4, 2, 4, 8, COLS), jnp.float32),
            pltpu.VMEM((16, 2, 4, HALF), jnp.float32),
            pltpu.VMEM((16, 8, HALF), jnp.float32),
            pltpu.VMEM((1, 2, 4, COLS), jnp.float32),
            pltpu.VMEM((8, COLS), jnp.float32),
            pltpu.VMEM((3, 8, 4, COLS), jnp.float32),
            dma((3,)), dma, dma, dma((6, 4, 3)), dma((6, 4, 3)), dma((6, 4, 3)), dma((6, 4, 3)),
            dma((16,)), dma((16,)), dma((16,)), dma((16,)), dma((2, 16)), dma((2, 16)), dma((2, 8)), dma((2, 8)),
            dma((9,)),
        ] + compute_scratch(),
        compiler_params=pltpu.CompilerParams(collective_id=0, has_side_effects=True, vmem_limit_bytes=60 * 2**20),
        cost_estimate=pl.CostEstimate(flops=20 * 10**9, bytes_accessed=20 * 10**6, transcendentals=0),
    )(assignment, bounds, slides, antenna, bank, strain, *[jnp.asarray(table) for table in constant_tables()])
    return settle(chi, net)


def solution(mesh):
    P = jax.sharding.PartitionSpec
    return jax.shard_map(
        on_device,
        mesh=mesh,
        in_specs=(P("det", None, "tm", None), P("grp", None, "tm", None), P(), P(), P(), P()),
        out_specs=(P("det", "grp", "tm", None), P("grp", "det", "tm", None)),
        check_vma=False,
    )
```

```python
import functools
import math

import jax
import jax.numpy as jnp
import numpy as np
from jax import lax
from jax.experimental import pallas as pl
from jax.experimental.pallas import tpu as pltpu

FOLD = 128
COLS = 4096
BINS = FOLD * COLS
BANDS = 8
CHUNK = 512
STEPS = COLS // CHUNK
LANES = 128
OUT_ROWS = 32


def rows_of(part):
    tau = np.arange(OUT_ROWS)
    return 64 * (part % 2) + 32 * (tau // 16) + 16 * (part // 2) + tau % 16


def halves(table):
    high = np.asarray(table, np.float32).astype(jnp.bfloat16)
    low = (np.asarray(table, np.float64) - high.astype(np.float64)).astype(np.float32)
    return high, low.astype(jnp.bfloat16)


def pack_columns(real, imag):
    m = real.shape[0]
    parts = np.stack([real.reshape(m, 32, 4), imag.reshape(m, 32, 4)], axis=2)
    return parts.reshape(m, 256)


def stacked_rows(cos, sin):
    top = pack_columns(cos, -sin)
    bottom = pack_columns(sin, cos)
    return np.concatenate([top, bottom], axis=0)


def constant_tables():
    b = np.arange(FOLD)
    even, odd, twiddle = [], [], []
    for part in range(4):
        e = rows_of(part)
        angle = 2 * np.pi * ((e[:, None] * b[None, :]) % FOLD) / FOLD
        cos, sin = np.cos(angle), np.sin(angle)
        for parity, group in ((0, even), (1, odd)):
            blocks = []
            for band in range(parity, BANDS, 2):
                inside = (b >= 16 * band - 8) & (b < 16 * band + 24)
                blocks.append(stacked_rows(cos * inside, sin * inside))
            group.append(np.concatenate(blocks, axis=0))
        a = np.arange(COLS)
        angle = 2 * np.pi * (e[:, None] * a[None, :]) / BINS
        twiddle.append(np.stack([np.cos(angle), np.sin(angle)]))
    even = halves(np.stack(even))
    odd = halves(np.stack(odd))
    bands = np.stack([np.stack([even[1], even[0]], axis=1), np.stack([odd[1], odd[0]], axis=1)], axis=1)
    twiddle = np.stack(twiddle).astype(np.float32).reshape(4, 2, 4, 8, 32, LANES).swapaxes(3, 4).copy()
    a1 = np.arange(LANES)
    q2 = np.arange(32)
    v, r2 = np.meshgrid(np.arange(8), np.arange(4), indexing="ij")
    angle = (2 * np.pi * v * r2 / 32)[..., None, None] * np.ones((8, LANES))
    turn = np.stack([np.cos(angle), np.sin(angle)]).astype(np.float32)
    angle = 2 * np.pi * (a1[None, :] * q2[:, None]) / COLS
    inner = np.stack([np.cos(angle), np.sin(angle)]).astype(np.float32)
    angle = 2 * np.pi * ((a1[:, None] * a1[None, :]) % LANES) / LANES
    cos, sin = np.cos(angle), np.sin(angle)
    last = np.stack(halves(np.block([[cos, sin], [-sin, cos]])))
    place = np.zeros((512, 512), np.float32)
    u1, u2 = np.meshgrid(np.arange(128), np.arange(4), indexing="ij")
    place[(u2 * 128 + u1).ravel(), (u2 + 4 * u1).ravel()] = 1.0
    return bands, twiddle, turn, inner, last, place.astype(jnp.bfloat16)


def split_two(x):
    high = x.astype(jnp.bfloat16)
    low = (x - high.astype(jnp.float32)).astype(jnp.bfloat16)
    return high, low


def mm(a, b):
    return jnp.dot(a, b, preferred_element_type=jnp.float32)


ROOT = math.sqrt(0.5)


def eight(x):
    def add(p, q):
        return (p[0] + q[0], p[1] + q[1])

    def sub(p, q):
        return (p[0] - q[0], p[1] - q[1])

    def turn(p):
        return (-p[1], p[0])

    def addi(p, q):
        return (p[0] - q[1], p[1] + q[0])

    def subi(p, q):
        return (p[0] + q[1], p[1] - q[0])

    def four(z):
        s02, d02 = add(z[0], z[2]), sub(z[0], z[2])
        s13, d13 = add(z[1], z[3]), sub(z[1], z[3])
        return [add(s02, s13), addi(d02, d13), sub(s02, s13), subi(d02, d13)]

    ev = four([x[0], x[2], x[4], x[6]])
    od = four([x[1], x[3], x[5], x[7]])
    o1 = ((od[1][0] - od[1][1]) * ROOT, (od[1][0] + od[1][1]) * ROOT)
    o3 = ((od[3][0] + od[3][1]) * ROOT, (od[3][1] - od[3][0]) * ROOT)
    return [
        add(ev[0], od[0]),
        add(ev[1], o1),
        addi(ev[2], od[2]),
        sub(ev[3], o3),
        sub(ev[0], od[0]),
        sub(ev[1], o1),
        subi(ev[2], od[2]),
        add(ev[3], o3),
    ]


def four_point(z):
    s0 = (z[0][0] + z[2][0], z[0][1] + z[2][1])
    d0 = (z[0][0] - z[2][0], z[0][1] - z[2][1])
    s1 = (z[1][0] + z[3][0], z[1][1] + z[3][1])
    d1 = (z[1][0] - z[3][0], z[1][1] - z[3][1])
    return [
        (s0[0] + s1[0], s0[1] + s1[1]),
        (d0[0] - d1[1], d0[1] + d1[0]),
        (s0[0] - s1[0], s0[1] - s1[1]),
        (d0[0] + d1[1], d0[1] - d1[0]),
    ]


def times(x, c, s):
    return (x[0] * c - x[1] * s, x[0] * s + x[1] * c)


def prepare(part, det, slides, antenna, bands, net, ramp):
    column = (
        lax.broadcasted_iota(jnp.int32, (32, LANES), 0) * LANES
        + lax.broadcasted_iota(jnp.int32, (32, LANES), 1)
    )
    tau = lax.broadcasted_iota(jnp.int32, (OUT_ROWS, 256), 0)
    row = 64 * (part & 1) + 32 * (tau >> 4) + 16 * (part >> 1) + (tau & 15)
    packed = lax.broadcasted_iota(jnp.int32, (OUT_ROWS, 256), 1)
    bin_row = (packed >> 3) * 4 + (packed & 3)
    quarter = ((packed >> 2) & 1) * (FOLD // 4)
    for side in range(2):
        which = det if side == 0 else 1 - det
        first = which == 0
        weight_re = jnp.where(first, antenna[0, 0], antenna[1, 0])
        weight_im = jnp.where(first, antenna[0, 1], antenna[1, 1])
        for slide in range(2):
            shift = which * jnp.where(det == 0, slides[slide], slides[2 + slide])
            angle = (((row + shift) * bin_row + quarter) & (FOLD - 1)).astype(jnp.float32) * (2.0 * math.pi / FOLD)
            for half, table in ((0, jnp.cos(angle)), (1, jnp.sin(angle))):
                high, low = split_two(table)
                at = 64 * slide + 32 * half
                if side == 0:
                    for parity in range(2):
                        bands[parity, 256 + at : 288 + at, :] = low
                        bands[parity, 640 + at : 672 + at, :] = high
                else:
                    net[at : at + 32, :] = low
                    net[128 + at : 160 + at, :] = high
            angle = ((column * shift) & (BINS - 1)).astype(jnp.float32) * (2.0 * math.pi / BINS)
            cos, sin = jnp.cos(angle), jnp.sin(angle)
            ramp[slide, 2 * side] = weight_re * cos - weight_im * sin
            ramp[slide, 2 * side + 1] = weight_re * sin + weight_im * cos


def column_block(step):
    return jnp.where(step < 6, step % 3 + 4 * (step // 3), 4 * step - 21)


def products(step, det, bounds, tmpl, signal, held, power):
    start = pl.multiple_of(column_block(step) * CHUNK, CHUNK)
    cols = pl.ds(start, CHUNK)
    src = lax.broadcasted_iota(jnp.int32, (2, 8, CHUNK), 0)
    sub = lax.broadcasted_iota(jnp.int32, (2, 8, CHUNK), 1)
    lane = lax.broadcasted_iota(jnp.int32, (2, 8, CHUNK), 2)
    top = sub < 4
    place_in = (src * 4 + (sub & 3)) * COLS + lane + start

    def fold(v):
        v = v[0] + v[1]
        return v[:, 0:128] + v[:, 128:256] + v[:, 256:384] + v[:, 384:512]

    def keep(value):
        return value.reshape(16, CHUNK).astype(jnp.bfloat16)

    for i in range(16):
        y, low_z, x = i // 4, (i // 2) % 2, slice(2 * (i % 2), 2 * (i % 2) + 2)
        rows = slice(16 * i, 16 * i + 16)
        wave = tmpl[y, low_z, x, :, cols]
        rolled = pltpu.roll(wave, 4, 1)
        wave_re = jnp.where(top, wave, rolled)
        wave_im = jnp.where(top, rolled, -wave)
        own = signal[det, y, low_z, x, :, cols]
        own = own * wave_re + pltpu.roll(own, 4, 1) * wave_im
        oth = signal[1 - det, y, low_z, x, :, cols]
        oth = oth * wave_re + pltpu.roll(oth, 4, 1) * wave_im
        bound = (i - 1) // 2
        squares = wave * wave
        high = own.astype(jnp.bfloat16).astype(jnp.float32)
        low = own - high
        if 0 <= bound < BANDS - 1:
            upper = place_in >= bounds[bound] - 8 * i * COLS
            power[i, 0] += fold(jnp.where(upper, 0.0, squares))
            cut = lambda value: jnp.where(upper, 0.0, value)
            high_low, low_low = cut(high), cut(low)
            lower = (keep(high_low), keep(low_low))
            higher = (keep(high - high_low), keep(low - low_low))
            even, odd = (higher, lower) if bound % 2 else (lower, higher)
        else:
            zero = jnp.zeros((16, CHUNK), jnp.bfloat16)
            even, odd = (keep(high), keep(low)), (zero, zero)
            if bound == BANDS - 1:
                even, odd = odd, even
                power[i, 0] += fold(squares)
        power[i, 1] += fold(squares)
        held[0, rows, :], held[1, rows, :] = even
        held[2, rows, :], held[3, rows, :] = odd
        held[4, rows, :], held[5, rows, :] = split_two(oth.reshape(16, CHUNK))


def first_stage(step, held, bands, net, series):
    tiles = CHUNK // LANES
    block = column_block(step) * tiles

    def put(first, value):
        rows = value.shape[0] // 8
        for tile in range(tiles):
            piece = value[:, tile * LANES : (tile + 1) * LANES].reshape(rows, 8, LANES)
            series[pl.ds(first, rows), block + tile] = piece

    net_sum = None
    for parity in range(2):
        both = mm(bands[parity], held[2 * parity])
        fine = mm(bands[parity, 384:768, :], held[2 * parity + 1])
        value = both[0:384] + both[384:768] + fine
        put(32 * parity, value[0:256])
        net_sum = value[256:384] if net_sum is None else net_sum + value[256:384]
    put(64, net_sum)
    both = mm(net[...], held[4])
    fine = mm(net[128:256, :], held[5])
    put(80, both[0:128] + both[128:256] + fine)


def power_shares(power):
    powers = []
    for band in range(BANDS):
        acc = jnp.zeros((8, LANES), jnp.float32)
        for i in range(16):
            bound = (i - 1) // 2
            if bound == band:
                acc += power[i, 0]
            if bound + 1 == band:
                acc += power[i, 1] - power[i, 0]
        powers.append(jnp.sum(jnp.sum(acc, axis=0, keepdims=True), axis=1, keepdims=True))
    total = sum(powers)
    return total, [value / total for value in powers]


def second_stage(eb, total, shares, response, series, twiddle, turn, inner, last, place, ramp, zbuf, bbuf, vbuf, rows, first):
    inverse = [(1.0 / (2 * BANDS - 2)) / (total * share) for share in shares]
    net_scale = 1.0 / (total * response)
    cos, sin = twiddle[0, eb], twiddle[1, eb]
    inner_re, inner_im = inner[0][:, None, :], inner[1][:, None, :]

    def settle_rows(kinds):
        high, low = split_two(vbuf[64 * kinds[0] : 64 * kinds[-1] + 64, :])
        done = mm(high, place[...]) + mm(low, place[...])
        for at, kind in enumerate(kinds):
            for v in range(8):
                both = done[at * 64 + v * 8 : at * 64 + v * 8 + 8, :]
                rows[kind, 2 * eb, :, v * 512 : (v + 1) * 512] = both[0:4]
                rows[kind, 2 * eb + 1, :, v * 512 : (v + 1) * 512] = both[4:8]

    def transform(item, z):
        z = times(z, cos, sin)
        re, im = z[0].reshape(8, 4, 8, LANES), z[1].reshape(8, 4, 8, LANES)
        values = eight([(re[s], im[s]) for s in range(8)])
        turned = [(values[0][0][1:], values[0][1][1:])]
        turned += [times((values[v][0][1:], values[v][1][1:]), turn[0, v, 1:], turn[1, v, 1:]) for v in range(1, 8)]
        first = tuple(jnp.stack([value[c][0] for value in values]) for c in range(2))
        re = jnp.stack([value[0] for value in turned])
        im = jnp.stack([value[1] for value in turned])
        done = four_point([first] + [(re[:, r2], im[:, r2]) for r2 in range(3)])
        re = jnp.concatenate([value[0] for value in done], axis=0)
        im = jnp.concatenate([value[1] for value in done], axis=0)
        z = times((re, im), inner_re, inner_im)
        slot = item % 2
        zbuf[slot, :, 0:LANES] = z[0].reshape(256, LANES)
        zbuf[slot, :, LANES : 2 * LANES] = z[1].reshape(256, LANES)
        high, low = split_two(zbuf[slot])
        bbuf[item] = mm(high, last[0]) + mm(low, last[0]) + mm(high, last[1])

    for item in range(BANDS):
        base = (item // 2) * 8 + (item % 2) * 32 + eb
        transform(item, (series[base], series[base + 4]))
    for u2 in range(4):
        part = slice(64 * u2, 64 * u2 + 64)
        re = [bbuf[band, part, 0:LANES] for band in range(BANDS)]
        im = [bbuf[band, part, LANES : 2 * LANES] for band in range(BANDS)]
        whole_re, whole_im = sum(re), sum(im)
        chi = None
        for band in range(BANDS):
            gap_re = re[band] - shares[band] * whole_re
            gap_im = im[band] - shares[band] * whole_im
            term = (gap_re * gap_re + gap_im * gap_im) * inverse[band]
            chi = term if chi is None else chi + term
        columns = slice(u2 * LANES, (u2 + 1) * LANES)
        vbuf[0:64, columns] = chi
    settle_rows(range(1))
    first()
    for slide in range(2):
        own = (series[64 + 8 * slide + eb], series[64 + 8 * slide + 4 + eb])
        oth = (series[80 + 8 * slide + eb], series[80 + 8 * slide + 4 + eb])
        line = [ramp[slide, k][:, None, :] for k in range(4)]
        own, oth = times(own, line[0], line[1]), times(oth, line[2], line[3])
        transform(BANDS + slide, (own[0] + oth[0], own[1] + oth[1]))

    for u2 in range(4):
        part = slice(64 * u2, 64 * u2 + 64)
        columns = slice(u2 * LANES, (u2 + 1) * LANES)
        for slide in range(2):
            re = bbuf[BANDS + slide, part, 0:LANES]
            im = bbuf[BANDS + slide, part, LANES : 2 * LANES]
            vbuf[64 + 64 * slide : 128 + 64 * slide, columns] = (re * re + im * im) * net_scale
    settle_rows(range(1, 3))


def compute_scratch():
    return [
        pltpu.VMEM((256, 256), jnp.bfloat16),
        pltpu.VMEM((2, 4, 32, LANES), jnp.float32),
        pltpu.VMEM((96, 32, 8, LANES), jnp.float32),
        pltpu.VMEM((6, 256, CHUNK), jnp.bfloat16),
        pltpu.VMEM((6, 256, CHUNK), jnp.bfloat16),
        pltpu.VMEM((16, 2, 8, LANES), jnp.float32),
        pltpu.VMEM((2, 256, 256), jnp.float32),
        pltpu.VMEM((10, 256, 256), jnp.float32),
        pltpu.VMEM((192, 512), jnp.float32),
        pltpu.VMEM((2, 768, 256), jnp.bfloat16),
        pltpu.VMEM((2, 4, 32, 8, LANES), jnp.float32),
        pltpu.VMEM((2, 8, 4, 8, LANES), jnp.float32),
        pltpu.VMEM((2, 32, LANES), jnp.float32),
        pltpu.VMEM((2, 256, 256), jnp.bfloat16),
        pltpu.VMEM((512, 512), jnp.bfloat16),
    ]


MESH = pl.DeviceIdType.MESH
HALF = COLS // 2
PORTIONS = ((0, 512), (512, 512), (1024, 512), (1536, 128), (1664, 128), (1792, 256))
ORDERS = (("x", "y", "z"), ("y", "z", "x"), ("z", "x", "y")) * 2
EARLY, LATE = (0, 1, 2), (3, 4, 5)
FAR = (1, 4, 3, 12, 2, 8, 5, 15, 7, 13, 6, 9, 11, 14, 10)


def kernel(
    assign, bounds, slides, antenna, bank, strain, bands_hbm, twiddle_hbm, turn_hbm, inner_hbm, last_hbm, place_hbm,
    chi, net_out, tmpl, signal, everything, staged, loaded, packed, rows,
    local_sem, swap_send, swap_recv, wide_send, wide_recv, pass_send, pass_recv,
    far_send, far_recv, deep_send, deep_recv, near_send, near_recv, out_send, out_recv, table_sem,
    net, ramp, series, held_a, held_b, power, zbuf, bbuf, vbuf, bands, twiddle, turn, inner, last, weave,
):
    det, grp, tm = lax.axis_index("det"), lax.axis_index("grp"), lax.axis_index("tm")
    low_z = lax.rem(lax.div(tm, 4), 2)
    here = {"y": lax.div(tm, 8), "z": det * 2 + low_z, "x": lax.rem(tm, 4)}
    onward = {axis: [value] + [lax.rem(value + k, 4) for k in (1, 2, 3)] for axis, value in here.items()}
    split_z = [(det, low_z)] + [(lax.div(z, 2), lax.rem(z, 2)) for z in onward["z"][1:]]
    peer = {"grp": 1 - grp}
    half = pl.ds(pl.multiple_of(grp * HALF, HALF), HALF)
    other = pl.ds(pl.multiple_of((1 - grp) * HALF, HALF), HALF)

    AXES = ("y", "z", "x")

    def moved(axis, by):
        return tuple(by % 4 if name == axis else 0 for name in AXES)

    def shifted(d, sign=1):
        return ((sign * (d // 4)) % 4, 0, (sign * (d % 4)) % 4)

    def at_y(place):
        return onward["y"][place[0]]

    def at_x(place):
        return onward["x"][place[2]]

    tm_at = {}

    def ident(place):
        if place not in tm_at:
            tm_at[place] = at_y(place) * 8 + split_z[place[1]][1] * 4 + at_x(place)
        return {"det": split_z[place[1]][0], "tm": tm_at[place]}

    slots = {}

    def number(place):
        if place not in slots:
            slots[place] = at_y(place) * 4 + at_x(place)
        return slots[place]

    HERE = (0, 0, 0)
    PLANE = [shifted(d) for d in range(16)]
    for place in PLANE + [moved("z", d) for d in (1, 2, 3)]:
        ident(place)
        number(place)

    keep = pltpu.make_async_copy(bank.at[:, :, :, half], everything.at[pl.ds(grp * 8, 8)], local_sem.at[0])
    keep.start()
    own = pltpu.make_async_copy(strain, loaded, local_sem.at[1])
    own.start()

    part = 2 * low_z + grp
    tables = [
        pltpu.make_async_copy(src, dst, table_sem.at[i])
        for i, (src, dst) in enumerate((
            (bands_hbm.at[part, 0, 0], bands.at[0, pl.ds(0, 256)]), (bands_hbm.at[part, 0, 1], bands.at[0, pl.ds(384, 256)]),
            (bands_hbm.at[part, 1, 0], bands.at[1, pl.ds(0, 256)]), (bands_hbm.at[part, 1, 1], bands.at[1, pl.ds(384, 256)]),
            (twiddle_hbm.at[part], twiddle), (turn_hbm, turn),
            (inner_hbm, inner), (last_hbm, last), (place_hbm, weave),
        ))
    ]
    for copy in tables:
        copy.start()

    to_grp = lax.div(here["y"], 2)
    same_core = to_grp == grp
    slot_at = 4 * lax.rem(here["y"], 2) + here["x"]

    def target(i):
        return (2 * grp + i // 4) * 8 + low_z * 4 + i % 4

    barrier = pltpu.get_barrier_semaphore()

    for place in PLANE[1:]:
        pl.semaphore_signal(barrier, inc=1, device_id=ident(place), device_id_type=MESH)
    for d in (1, 2, 3):
        pl.semaphore_signal(barrier, inc=1, device_id=ident(moved("z", d)), device_id_type=MESH)
    pl.semaphore_signal(barrier, inc=1, device_id=peer, device_id_type=MESH)

    pl.semaphore_wait(barrier, 19)

    def remote(src, dst, send, recv, device):
        return pltpu.make_async_remote_copy(
            src_ref=src, dst_ref=dst, send_sem=send, recv_sem=recv, device_id=device, device_id_type=MESH
        )

    swap = remote(bank.at[:, :, :, other], everything.at[pl.ds(grp * 8, 8)], swap_send, swap_recv, peer)
    swap.start()

    def columns(portion, core):
        first, width = PORTIONS[portion]
        return pl.ds(pl.multiple_of(core * HALF + first, LANES), width)

    def region(portion, stage, place, core, part=None):
        done = ORDERS[portion][:stage]
        cut = "x" if ORDERS[portion][2] == "y" else "y"

        def every(axis, value, size):
            if axis not in done:
                return value
            if part is not None and axis == cut:
                return pl.ds(2 * part, 2)
            return pl.ds(0, size)

        return signal.at[
            every("z", split_z[place[1]][0], 2), every("y", at_y(place), 4), every("z", split_z[place[1]][1], 2),
            every("x", at_x(place), 4), :, columns(portion, core),
        ]

    def wide(portion, stage, d):
        dst = region(portion, stage, HERE, grp)
        src = packed.at[:, columns(portion, grp)] if stage == 0 else dst
        at = (portion, stage, d - 1)
        return remote(src, dst, wide_send.at[at], wide_recv.at[at], ident(moved(ORDERS[portion][stage], d)))

    def relay(portion, part):
        axis = ORDERS[portion][2]
        got = region(portion, 2, moved(axis, -1 if part == 0 else 1), grp, part)
        at = (portion, 2 + part, 1)
        return remote(got, got, wide_send.at[at], wide_recv.at[at], ident(moved(axis, 1 if part == 0 else -1)))

    def incoming(portion, stage, d, core):
        axis = ORDERS[portion][min(stage, 2)]
        if stage < 2 or d != 2:
            part = None
        else:
            part = stage - 2
        return region(portion, min(stage, 2), moved(axis, -d), core, part), (portion, stage, d - 1)

    def arrived(portion, stage, d):
        got, at = incoming(portion, stage, d, grp)
        remote(got, got, wide_send.at[at], wide_recv.at[at], peer).wait_recv()
        remote(got, got, pass_send.at[at], pass_recv.at[at], peer).start()

    def pass_on(portions):
        for portion in portions:
            for d, part in ((1, 0), (3, 1)):
                arrived(portion, 2, d)
                relay(portion, part).start()

    def pass_last(portions):
        for portion in portions:
            for part in range(2):
                arrived(portion, 2 + part, 2)

    def pass_first(portions):
        for portion in portions:
            for d in (1, 3, 2):
                arrived(portion, 0, d)
            for d in (1, 3, 2):
                wide(portion, 1, d).start()

    def pass_second(portions):
        for portion in portions:
            for d in (1, 3, 2):
                arrived(portion, 1, d)
            for d in (1, 3):
                wide(portion, 2, d).start()

    own.wait()
    packed[0:4, :] = loaded[0, 0]
    packed[4:8, :] = loaded[0, 1]
    for portion in EARLY + LATE:
        for d in (1, 3, 2):
            wide(portion, 0, d).start()
    mine = pltpu.make_async_copy(packed, signal.at[det, here["y"], low_z, here["x"]], local_sem.at[1])
    mine.start()

    swap.wait_recv()
    keep.wait()
    for slot in range(16):
        wave = everything[assign[slot]]
        staged[slot, 0:4, :] = wave[0]
        staged[slot, 4:8, :] = wave[1]

    def far(d):
        to = shifted(d)
        return remote(
            staged.at[number(to)], tmpl.at[here["y"], low_z, here["x"], :, half],
            far_send.at[d], far_recv.at[d], ident(to),
        )

    def piece(place, plane, columns):
        return tmpl.at[at_y(place), plane, at_x(place), :, columns]

    def deep(place):
        got = piece(place, low_z, half)
        to = moved("z", 1 + 2 * (place[2] % 2))
        at = DEEP(place)
        return remote(got, got, deep_send.at[at], deep_recv.at[at], ident(to))

    def DEEP(place):
        return place[0] * 4 + place[2]

    def near(place, plane, columns):
        got = piece(place, low_z if plane == 0 else 1 - low_z, columns)
        at = (plane, DEEP(place))
        return remote(got, got, near_send.at[at], near_recv.at[at], peer)

    mine.wait()
    pass_first(EARLY)
    for d in FAR:
        far(d).start()
    kept = pltpu.make_async_copy(staged.at[number(HERE)], piece(HERE, low_z, half), local_sem.at[2])
    kept.start()
    prepare(part, det, slides, antenna, bands, net, ramp)
    power[...] = jnp.zeros_like(power)
    kept.wait()
    deep(HERE).start()
    near(HERE, 0, half).start()

    def got_far(order):
        for d in order:
            place = shifted(d, -1)
            got = piece(place, low_z, half)
            remote(got, got, far_send.at[d], far_recv.at[d], peer).wait_recv()
            deep(place).start()
            near(place, 0, half).start()

    def got_deep(order):
        for d in order:
            place = shifted(d, -1)
            got = piece(place, 1 - low_z, half)
            at = DEEP(place)
            remote(got, got, deep_send.at[at], deep_recv.at[at], peer).wait_recv()
            near(place, 1, half).start()

    events = ((0, 1), (0, 2), (0, 3), (1, 1), (1, 2), (1, 3), (2, 1), (2, 3), (2, 2), (3, 2))

    def complete(portions, events):
        for portion in portions:
            for stage, d in events:
                come, at = incoming(portion, stage, d, 1 - grp)
                remote(come, come, pass_send.at[at], pass_recv.at[at], peer).wait_recv()


    def complete_near(plane):
        for place in PLANE:
            near(place, plane, other).wait_recv()

    pass_second(EARLY)
    pass_first(LATE)
    got_far(FAR)
    for copy in tables:
        copy.wait()
    complete(EARLY, events[:6])
    complete_near(0)
    got_deep((0,) + FAR[:8])
    pass_on(EARLY)
    pass_second(LATE)
    got_deep(FAR[8:])
    pass_last(EARLY)

    complete_near(1)
    complete(EARLY, events[6:])

    def build(step, held):
        products(step, det, bounds, tmpl, signal, held, power)

    def pair(p, carry):
        first_stage(2 * p, held_a, bands, net, series)
        build(2 * p + 1, held_b)

        @pl.when(p == 2)
        def _():
            pass_last(LATE)
            complete(LATE, events[6:])

        first_stage(2 * p + 1, held_b, bands, net, series)
        build(2 * p + 2, held_a)
        return carry

    build(0, held_a)
    pass_on(LATE)
    complete(LATE, events[:6])
    lax.fori_loop(0, 3, pair, 0)
    first_stage(6, held_a, bands, net, series)
    build(7, held_b)
    first_stage(7, held_b, bands, net, series)
    total, shares = power_shares(power)
    response = sum(antenna[d, c] * antenna[d, c] for d in range(2) for c in range(2))

    def parts(i):
        return ((rows.at[0, i], chi.at[slot_at]), (rows.at[pl.ds(1, 2), i], net_out.at[slot_at]))

    def give(i, kind):
        src, dst = parts(i)[kind]
        return pltpu.make_async_remote_copy(
            src_ref=src, dst_ref=dst, send_sem=out_send.at[kind, i], recv_sem=out_recv.at[kind, slot_at],
            device_id={"grp": to_grp, "tm": target(i)}, device_id_type=MESH,
        )

    def block(step, carry):
        eb = (2 * lax.rem(here["y"], 2) + lax.div(here["x"], 2)) ^ (3 - step)
        def send(kind):
            for k in range(2):
                i = 2 * eb + k
                is_self = (target(i) == tm) & same_core

                @pl.when(is_self)
                def _():
                    src, dst = parts(i)[kind]
                    pltpu.make_async_copy(src, dst, out_recv.at[kind, slot_at]).start()

                @pl.when(jnp.logical_not(is_self))
                def _():
                    give(i, kind).start()

        second_stage(
            eb, total, shares, response, series, twiddle, turn, inner, last, weave, ramp, zbuf, bbuf, vbuf, rows,
            lambda: send(0),
        )
        send(1)
        return carry

    lax.fori_loop(0, 4, block, 0)

    swap.wait_send()

    for d, place in enumerate(PLANE):
        deep(place).wait_send()
        for plane in range(2):
            near(place, plane, half).wait_send()
        if d > 0:
            far(d).wait_send()
    for portion in EARLY + LATE:
        for stage, d in events:
            if stage < 2 or d != 2:
                wide(portion, stage, d).wait_send()
            else:
                relay(portion, stage - 2).wait_send()
            got, at = incoming(portion, stage, d, grp)
            remote(got, got, pass_send.at[at], pass_recv.at[at], peer).wait_send()

    def finish(i, carry):
        is_self = (target(i) == tm) & same_core
        for kind, dst in ((0, chi), (1, net_out)):
            pltpu.make_async_copy(dst.at[i], dst.at[i], out_recv.at[kind, i]).wait()

            @pl.when(jnp.logical_not(is_self))
            def _():
                give(i, kind).wait_send()
        return carry

    lax.fori_loop(0, 8, finish, 0)


def settle_kernel(chi, net, chi_out, net_out, chi_held, net_held, sem):
    moves = []
    for k in range(4):
        part = pl.ds(2 * k, 2)
        for i, (src, held, dst) in enumerate(((net, net_held, net_out), (chi, chi_held, chi_out))):
            moves.append((
                pltpu.make_async_copy(src.at[part], held.at[part], sem.at[0, i, k]),
                pltpu.make_async_copy(held.at[part], dst.at[part], sem.at[1, i, k]),
            ))
    for come, _ in moves:
        come.start()
    for come, go in moves:
        come.wait()
        go.start()
    for _, go in moves:
        go.wait()


def settle(chi, net):
    hbm = pl.BlockSpec(memory_space=pltpu.HBM)
    chi, net = pl.pallas_call(
        settle_kernel,
        out_shape=(jax.ShapeDtypeStruct(chi.shape, chi.dtype), jax.ShapeDtypeStruct(net.shape, net.dtype)),
        in_specs=[hbm, hbm],
        out_specs=[hbm, hbm],
        scratch_shapes=[
            pltpu.VMEM(chi.shape, chi.dtype), pltpu.VMEM(net.shape, net.dtype), pltpu.SemaphoreType.DMA((2, 2, 4)),
        ],
        compiler_params=pltpu.CompilerParams(vmem_limit_bytes=60 * 2**20),
        cost_estimate=pl.CostEstimate(flops=0, bytes_accessed=3 * 2**20, transcendentals=0),
    )(chi, net)
    return chi[None], net


def on_device(strain, bank, assignment, slides, bounds, antenna):
    dma = pltpu.SemaphoreType.DMA
    smem, hbm = pl.BlockSpec(memory_space=pltpu.SMEM), pl.BlockSpec(memory_space=pltpu.HBM)
    chi, net = pl.pallas_call(
        kernel,
        out_shape=(
            jax.ShapeDtypeStruct((8, 4, COLS), jnp.float32),
            jax.ShapeDtypeStruct((8, 2, 4, COLS), jnp.float32),
        ),
        in_specs=[smem] * 4 + [hbm] * 8,
        out_specs=[hbm, hbm],
        scratch_shapes=[
            pltpu.VMEM((4, 2, 4, 8, COLS), jnp.float32),
            pltpu.VMEM((2, 4, 2, 4, 8, COLS), jnp.float32),
            pltpu.VMEM((16, 2, 4, HALF), jnp.float32),
            pltpu.VMEM((16, 8, HALF), jnp.float32),
            pltpu.VMEM((1, 2, 4, COLS), jnp.float32),
            pltpu.VMEM((8, COLS), jnp.float32),
            pltpu.VMEM((3, 8, 4, COLS), jnp.float32),
            dma((3,)), dma, dma, dma((6, 4, 3)), dma((6, 4, 3)), dma((6, 4, 3)), dma((6, 4, 3)),
            dma((16,)), dma((16,)), dma((16,)), dma((16,)), dma((2, 16)), dma((2, 16)), dma((2, 8)), dma((2, 8)),
            dma((9,)),
        ] + compute_scratch(),
        compiler_params=pltpu.CompilerParams(collective_id=0, has_side_effects=True, vmem_limit_bytes=60 * 2**20),
        cost_estimate=pl.CostEstimate(flops=20 * 10**9, bytes_accessed=20 * 10**6, transcendentals=0),
    )(assignment, bounds, slides, antenna, bank, strain, *[jnp.asarray(table) for table in constant_tables()])
    return settle(chi, net)


def solution(mesh):
    P = jax.sharding.PartitionSpec
    return jax.shard_map(
        on_device,
        mesh=mesh,
        in_specs=(P("det", None, "tm", None), P("grp", None, "tm", None), P(), P(), P(), P()),
        out_specs=(P("det", "grp", "tm", None), P("grp", "det", "tm", None)),
        check_vma=False,
    )
```

```python
import functools
import math

import jax
import jax.numpy as jnp
import numpy as np
from jax import lax
from jax.experimental import pallas as pl
from jax.experimental.pallas import tpu as pltpu

FOLD = 128
COLS = 4096
BINS = FOLD * COLS
BANDS = 8
CHUNK = 512
STEPS = COLS // CHUNK
LANES = 128
OUT_ROWS = 32


def rows_of(part):
    tau = np.arange(OUT_ROWS)
    return 64 * (part % 2) + 32 * (tau // 16) + 16 * (part // 2) + tau % 16


def halves(table):
    high = np.asarray(table, np.float32).astype(jnp.bfloat16)
    low = (np.asarray(table, np.float64) - high.astype(np.float64)).astype(np.float32)
    return high, low.astype(jnp.bfloat16)


def pack_columns(real, imag):
    m = real.shape[0]
    parts = np.stack([real.reshape(m, 32, 4), imag.reshape(m, 32, 4)], axis=2)
    return parts.reshape(m, 256)


def stacked_rows(cos, sin):
    top = pack_columns(cos, -sin)
    bottom = pack_columns(sin, cos)
    return np.concatenate([top, bottom], axis=0)


def constant_tables():
    b = np.arange(FOLD)
    even, odd, twiddle = [], [], []
    for part in range(4):
        e = rows_of(part)
        angle = 2 * np.pi * ((e[:, None] * b[None, :]) % FOLD) / FOLD
        cos, sin = np.cos(angle), np.sin(angle)
        for parity, group in ((0, even), (1, odd)):
            blocks = []
            for band in range(parity, BANDS, 2):
                inside = (b >= 16 * band - 8) & (b < 16 * band + 24)
                blocks.append(stacked_rows(cos * inside, sin * inside))
            group.append(np.concatenate(blocks, axis=0))
        a = np.arange(COLS)
        angle = 2 * np.pi * (e[:, None] * a[None, :]) / BINS
        twiddle.append(np.stack([np.cos(angle), np.sin(angle)]))
    even = halves(np.stack(even))
    odd = halves(np.stack(odd))
    bands = np.stack([np.stack([even[1], even[0]], axis=1), np.stack([odd[1], odd[0]], axis=1)], axis=1)
    twiddle = np.stack(twiddle).astype(np.float32).reshape(4, 2, 4, 8, 32, LANES).swapaxes(3, 4).copy()
    a1 = np.arange(LANES)
    q2 = np.arange(32)
    v, r2 = np.meshgrid(np.arange(8), np.arange(4), indexing="ij")
    angle = (2 * np.pi * v * r2 / 32)[..., None, None] * np.ones((8, LANES))
    turn = np.stack([np.cos(angle), np.sin(angle)]).astype(np.float32)
    angle = 2 * np.pi * (a1[None, :] * q2[:, None]) / COLS
    inner = np.stack([np.cos(angle), np.sin(angle)]).astype(np.float32)
    angle = 2 * np.pi * ((a1[:, None] * a1[None, :]) % LANES) / LANES
    cos, sin = np.cos(angle), np.sin(angle)
    last = np.stack(halves(np.block([[cos, sin], [-sin, cos]])))
    place = np.zeros((512, 512), np.float32)
    u1, u2 = np.meshgrid(np.arange(128), np.arange(4), indexing="ij")
    place[(u2 * 128 + u1).ravel(), (u2 + 4 * u1).ravel()] = 1.0
    return bands, twiddle, turn, inner, last, place.astype(jnp.bfloat16)


def split_two(x):
    high = x.astype(jnp.bfloat16)
    low = (x - high.astype(jnp.float32)).astype(jnp.bfloat16)
    return high, low


def mm(a, b):
    return jnp.dot(a, b, preferred_element_type=jnp.float32)


ROOT = math.sqrt(0.5)


def eight(x):
    def add(p, q):
        return (p[0] + q[0], p[1] + q[1])

    def sub(p, q):
        return (p[0] - q[0], p[1] - q[1])

    def turn(p):
        return (-p[1], p[0])

    def addi(p, q):
        return (p[0] - q[1], p[1] + q[0])

    def subi(p, q):
        return (p[0] + q[1], p[1] - q[0])

    def four(z):
        s02, d02 = add(z[0], z[2]), sub(z[0], z[2])
        s13, d13 = add(z[1], z[3]), sub(z[1], z[3])
        return [add(s02, s13), addi(d02, d13), sub(s02, s13), subi(d02, d13)]

    ev = four([x[0], x[2], x[4], x[6]])
    od = four([x[1], x[3], x[5], x[7]])
    o1 = ((od[1][0] - od[1][1]) * ROOT, (od[1][0] + od[1][1]) * ROOT)
    o3 = ((od[3][0] + od[3][1]) * ROOT, (od[3][1] - od[3][0]) * ROOT)
    return [
        add(ev[0], od[0]),
        add(ev[1], o1),
        addi(ev[2], od[2]),
        sub(ev[3], o3),
        sub(ev[0], od[0]),
        sub(ev[1], o1),
        subi(ev[2], od[2]),
        add(ev[3], o3),
    ]


def four_point(z):
    s0 = (z[0][0] + z[2][0], z[0][1] + z[2][1])
    d0 = (z[0][0] - z[2][0], z[0][1] - z[2][1])
    s1 = (z[1][0] + z[3][0], z[1][1] + z[3][1])
    d1 = (z[1][0] - z[3][0], z[1][1] - z[3][1])
    return [
        (s0[0] + s1[0], s0[1] + s1[1]),
        (d0[0] - d1[1], d0[1] + d1[0]),
        (s0[0] - s1[0], s0[1] - s1[1]),
        (d0[0] + d1[1], d0[1] - d1[0]),
    ]


def times(x, c, s):
    return (x[0] * c - x[1] * s, x[0] * s + x[1] * c)


def prepare(part, det, slides, antenna, bands, net, ramp):
    column = (
        lax.broadcasted_iota(jnp.int32, (32, LANES), 0) * LANES
        + lax.broadcasted_iota(jnp.int32, (32, LANES), 1)
    )
    tau = lax.broadcasted_iota(jnp.int32, (OUT_ROWS, 256), 0)
    row = 64 * (part & 1) + 32 * (tau >> 4) + 16 * (part >> 1) + (tau & 15)
    packed = lax.broadcasted_iota(jnp.int32, (OUT_ROWS, 256), 1)
    bin_row = (packed >> 3) * 4 + (packed & 3)
    quarter = ((packed >> 2) & 1) * (FOLD // 4)
    for side in range(2):
        which = det if side == 0 else 1 - det
        first = which == 0
        weight_re = jnp.where(first, antenna[0, 0], antenna[1, 0])
        weight_im = jnp.where(first, antenna[0, 1], antenna[1, 1])
        for slide in range(2):
            shift = which * jnp.where(det == 0, slides[slide], slides[2 + slide])
            angle = (((row + shift) * bin_row + quarter) & (FOLD - 1)).astype(jnp.float32) * (2.0 * math.pi / FOLD)
            for half, table in ((0, jnp.cos(angle)), (1, jnp.sin(angle))):
                high, low = split_two(table)
                at = 64 * slide + 32 * half
                if side == 0:
                    for parity in range(2):
                        bands[parity, 256 + at : 288 + at, :] = low
                        bands[parity, 640 + at : 672 + at, :] = high
                else:
                    net[at : at + 32, :] = low
                    net[128 + at : 160 + at, :] = high
            angle = ((column * shift) & (BINS - 1)).astype(jnp.float32) * (2.0 * math.pi / BINS)
            cos, sin = jnp.cos(angle), jnp.sin(angle)
            ramp[slide, 2 * side] = weight_re * cos - weight_im * sin
            ramp[slide, 2 * side + 1] = weight_re * sin + weight_im * cos


def column_block(step):
    return jnp.where(step < 6, step % 3 + 4 * (step // 3), 4 * step - 21)


def products(step, det, bounds, tmpl, signal, held, power):
    start = pl.multiple_of(column_block(step) * CHUNK, CHUNK)
    cols = pl.ds(start, CHUNK)
    src = lax.broadcasted_iota(jnp.int32, (2, 8, CHUNK), 0)
    sub = lax.broadcasted_iota(jnp.int32, (2, 8, CHUNK), 1)
    lane = lax.broadcasted_iota(jnp.int32, (2, 8, CHUNK), 2)
    top = sub < 4
    place_in = (src * 4 + (sub & 3)) * COLS + lane + start

    def fold(v):
        v = v[0] + v[1]
        return v[:, 0:128] + v[:, 128:256] + v[:, 256:384] + v[:, 384:512]

    def keep(value):
        return value.reshape(16, CHUNK).astype(jnp.bfloat16)

    for i in range(16):
        y, low_z, x = i // 4, (i // 2) % 2, slice(2 * (i % 2), 2 * (i % 2) + 2)
        rows = slice(16 * i, 16 * i + 16)
        wave = tmpl[y, low_z, x, :, cols]
        rolled = pltpu.roll(wave, 4, 1)
        wave_re = jnp.where(top, wave, rolled)
        wave_im = jnp.where(top, rolled, -wave)
        own = signal[det, y, low_z, x, :, cols]
        own = own * wave_re + pltpu.roll(own, 4, 1) * wave_im
        oth = signal[1 - det, y, low_z, x, :, cols]
        oth = oth * wave_re + pltpu.roll(oth, 4, 1) * wave_im
        bound = (i - 1) // 2
        squares = wave * wave
        high = own.astype(jnp.bfloat16).astype(jnp.float32)
        low = own - high
        if 0 <= bound < BANDS - 1:
            upper = place_in >= bounds[bound] - 8 * i * COLS
            power[i, 0] += fold(jnp.where(upper, 0.0, squares))
            cut = lambda value: jnp.where(upper, 0.0, value)
            high_low, low_low = cut(high), cut(low)
            lower = (keep(high_low), keep(low_low))
            higher = (keep(high - high_low), keep(low - low_low))
            even, odd = (higher, lower) if bound % 2 else (lower, higher)
        else:
            zero = jnp.zeros((16, CHUNK), jnp.bfloat16)
            even, odd = (keep(high), keep(low)), (zero, zero)
            if bound == BANDS - 1:
                even, odd = odd, even
                power[i, 0] += fold(squares)
        power[i, 1] += fold(squares)
        held[0, rows, :], held[1, rows, :] = even
        held[2, rows, :], held[3, rows, :] = odd
        held[4, rows, :], held[5, rows, :] = split_two(oth.reshape(16, CHUNK))


def first_stage(step, held, bands, net, series):
    tiles = CHUNK // LANES
    block = column_block(step) * tiles

    def put(first, value):
        rows = value.shape[0] // 8
        for tile in range(tiles):
            piece = value[:, tile * LANES : (tile + 1) * LANES].reshape(rows, 8, LANES)
            series[pl.ds(first, rows), block + tile] = piece

    net_sum = None
    for parity in range(2):
        both = mm(bands[parity], held[2 * parity])
        fine = mm(bands[parity, 384:768, :], held[2 * parity + 1])
        value = both[0:384] + both[384:768] + fine
        put(32 * parity, value[0:256])
        net_sum = value[256:384] if net_sum is None else net_sum + value[256:384]
    put(64, net_sum)
    both = mm(net[...], held[4])
    fine = mm(net[128:256, :], held[5])
    put(80, both[0:128] + both[128:256] + fine)


def power_shares(power):
    powers = []
    for band in range(BANDS):
        acc = jnp.zeros((8, LANES), jnp.float32)
        for i in range(16):
            bound = (i - 1) // 2
            if bound == band:
                acc += power[i, 0]
            if bound + 1 == band:
                acc += power[i, 1] - power[i, 0]
        powers.append(jnp.sum(jnp.sum(acc, axis=0, keepdims=True), axis=1, keepdims=True))
    total = sum(powers)
    return total, [value / total for value in powers]


def second_stage(eb, total, shares, response, series, twiddle, turn, inner, last, place, ramp, zbuf, bbuf, vbuf, rows, first):
    inverse = [(1.0 / (2 * BANDS - 2)) / (total * share) for share in shares]
    net_scale = 1.0 / (total * response)
    cos, sin = twiddle[0, eb], twiddle[1, eb]
    inner_re, inner_im = inner[0][:, None, :], inner[1][:, None, :]

    def settle_rows(kinds):
        high, low = split_two(vbuf[64 * kinds[0] : 64 * kinds[-1] + 64, :])
        done = mm(high, place[...]) + mm(low, place[...])
        for at, kind in enumerate(kinds):
            for v in range(8):
                both = done[at * 64 + v * 8 : at * 64 + v * 8 + 8, :]
                rows[kind, 2 * eb, :, v * 512 : (v + 1) * 512] = both[0:4]
                rows[kind, 2 * eb + 1, :, v * 512 : (v + 1) * 512] = both[4:8]

    def transform(item, z):
        z = times(z, cos, sin)
        re, im = z[0].reshape(8, 4, 8, LANES), z[1].reshape(8, 4, 8, LANES)
        values = eight([(re[s], im[s]) for s in range(8)])
        turned = [(values[0][0][1:], values[0][1][1:])]
        turned += [times((values[v][0][1:], values[v][1][1:]), turn[0, v, 1:], turn[1, v, 1:]) for v in range(1, 8)]
        first = tuple(jnp.stack([value[c][0] for value in values]) for c in range(2))
        re = jnp.stack([value[0] for value in turned])
        im = jnp.stack([value[1] for value in turned])
        done = four_point([first] + [(re[:, r2], im[:, r2]) for r2 in range(3)])
        re = jnp.concatenate([value[0] for value in done], axis=0)
        im = jnp.concatenate([value[1] for value in done], axis=0)
        z = times((re, im), inner_re, inner_im)
        slot = item % 2
        zbuf[slot, :, 0:LANES] = z[0].reshape(256, LANES)
        zbuf[slot, :, LANES : 2 * LANES] = z[1].reshape(256, LANES)
        high, low = split_two(zbuf[slot])
        bbuf[item] = mm(high, last[0]) + mm(low, last[0]) + mm(high, last[1])

    for item in range(BANDS):
        base = (item // 2) * 8 + (item % 2) * 32 + eb
        transform(item, (series[base], series[base + 4]))
    for u2 in range(4):
        part = slice(64 * u2, 64 * u2 + 64)
        re = [bbuf[band, part, 0:LANES] for band in range(BANDS)]
        im = [bbuf[band, part, LANES : 2 * LANES] for band in range(BANDS)]
        whole_re, whole_im = sum(re), sum(im)
        chi = None
        for band in range(BANDS):
            gap_re = re[band] - shares[band] * whole_re
            gap_im = im[band] - shares[band] * whole_im
            term = (gap_re * gap_re + gap_im * gap_im) * inverse[band]
            chi = term if chi is None else chi + term
        columns = slice(u2 * LANES, (u2 + 1) * LANES)
        vbuf[0:64, columns] = chi
    settle_rows(range(1))
    first()
    for slide in range(2):
        own = (series[64 + 8 * slide + eb], series[64 + 8 * slide + 4 + eb])
        oth = (series[80 + 8 * slide + eb], series[80 + 8 * slide + 4 + eb])
        line = [ramp[slide, k][:, None, :] for k in range(4)]
        own, oth = times(own, line[0], line[1]), times(oth, line[2], line[3])
        transform(BANDS + slide, (own[0] + oth[0], own[1] + oth[1]))

    for u2 in range(4):
        part = slice(64 * u2, 64 * u2 + 64)
        columns = slice(u2 * LANES, (u2 + 1) * LANES)
        for slide in range(2):
            re = bbuf[BANDS + slide, part, 0:LANES]
            im = bbuf[BANDS + slide, part, LANES : 2 * LANES]
            vbuf[64 + 64 * slide : 128 + 64 * slide, columns] = (re * re + im * im) * net_scale
    settle_rows(range(1, 3))


def compute_scratch():
    return [
        pltpu.VMEM((256, 256), jnp.bfloat16),
        pltpu.VMEM((2, 4, 32, LANES), jnp.float32),
        pltpu.VMEM((96, 32, 8, LANES), jnp.float32),
        pltpu.VMEM((6, 256, CHUNK), jnp.bfloat16),
        pltpu.VMEM((6, 256, CHUNK), jnp.bfloat16),
        pltpu.VMEM((16, 2, 8, LANES), jnp.float32),
        pltpu.VMEM((2, 256, 256), jnp.float32),
        pltpu.VMEM((10, 256, 256), jnp.float32),
        pltpu.VMEM((192, 512), jnp.float32),
        pltpu.VMEM((2, 768, 256), jnp.bfloat16),
        pltpu.VMEM((2, 4, 32, 8, LANES), jnp.float32),
        pltpu.VMEM((2, 8, 4, 8, LANES), jnp.float32),
        pltpu.VMEM((2, 32, LANES), jnp.float32),
        pltpu.VMEM((2, 256, 256), jnp.bfloat16),
        pltpu.VMEM((512, 512), jnp.bfloat16),
    ]


MESH = pl.DeviceIdType.MESH
HALF = COLS // 2
PORTIONS = ((0, 512), (512, 512), (1024, 512), (1536, 128), (1664, 128), (1792, 256))
ORDERS = (("x", "y", "z"), ("y", "z", "x"), ("z", "x", "y")) * 2
EARLY, LATE = (0, 1, 2), (3, 4, 5)
FAR = (1, 4, 3, 12, 2, 8, 5, 15, 7, 13, 6, 9, 11, 14, 10)


def kernel(
    assign, bounds, slides, antenna, bank, strain, bands_hbm, twiddle_hbm, turn_hbm, inner_hbm, last_hbm, place_hbm,
    chi, net_out, tmpl, signal, everything, staged, loaded, packed, rows,
    local_sem, swap_send, swap_recv, wide_send, wide_recv, pass_send, pass_recv,
    far_send, far_recv, deep_send, deep_recv, near_send, near_recv, out_send, out_recv, table_sem,
    net, ramp, series, held_a, held_b, power, zbuf, bbuf, vbuf, bands, twiddle, turn, inner, last, weave,
):
    det, grp, tm = lax.axis_index("det"), lax.axis_index("grp"), lax.axis_index("tm")
    low_z = lax.rem(lax.div(tm, 4), 2)
    here = {"y": lax.div(tm, 8), "z": det * 2 + low_z, "x": lax.rem(tm, 4)}
    onward = {axis: [value] + [lax.rem(value + k, 4) for k in (1, 2, 3)] for axis, value in here.items()}
    split_z = [(det, low_z)] + [(lax.div(z, 2), lax.rem(z, 2)) for z in onward["z"][1:]]
    peer = {"grp": 1 - grp}
    half = pl.ds(pl.multiple_of(grp * HALF, HALF), HALF)
    other = pl.ds(pl.multiple_of((1 - grp) * HALF, HALF), HALF)

    AXES = ("y", "z", "x")

    def moved(axis, by):
        return tuple(by % 4 if name == axis else 0 for name in AXES)

    def shifted(d, sign=1):
        return ((sign * (d // 4)) % 4, 0, (sign * (d % 4)) % 4)

    def at_y(place):
        return onward["y"][place[0]]

    def at_x(place):
        return onward["x"][place[2]]

    tm_at = {}

    def ident(place):
        if place not in tm_at:
            tm_at[place] = at_y(place) * 8 + split_z[place[1]][1] * 4 + at_x(place)
        return {"det": split_z[place[1]][0], "tm": tm_at[place]}

    slots = {}

    def number(place):
        if place not in slots:
            slots[place] = at_y(place) * 4 + at_x(place)
        return slots[place]

    HERE = (0, 0, 0)
    PLANE = [shifted(d) for d in range(16)]
    for place in PLANE + [moved("z", d) for d in (1, 2, 3)]:
        ident(place)
        number(place)

    keep = pltpu.make_async_copy(bank.at[:, :, :, half], everything.at[pl.ds(grp * 8, 8)], local_sem.at[0])
    keep.start()
    own = pltpu.make_async_copy(strain, loaded, local_sem.at[1])
    own.start()

    part = 2 * low_z + grp
    tables = [
        pltpu.make_async_copy(src, dst, table_sem.at[i])
        for i, (src, dst) in enumerate((
            (bands_hbm.at[part, 0, 0], bands.at[0, pl.ds(0, 256)]), (bands_hbm.at[part, 0, 1], bands.at[0, pl.ds(384, 256)]),
            (bands_hbm.at[part, 1, 0], bands.at[1, pl.ds(0, 256)]), (bands_hbm.at[part, 1, 1], bands.at[1, pl.ds(384, 256)]),
            (twiddle_hbm.at[part], twiddle), (turn_hbm, turn),
            (inner_hbm, inner), (last_hbm, last), (place_hbm, weave),
        ))
    ]
    for copy in tables:
        copy.start()

    to_grp = lax.div(here["y"], 2)
    same_core = to_grp == grp
    slot_at = 4 * lax.rem(here["y"], 2) + here["x"]

    def target(i):
        return (2 * grp + i // 4) * 8 + low_z * 4 + i % 4

    barrier = pltpu.get_barrier_semaphore()

    hops = lambda place: min(place[0], 4 - place[0]) + min(place[2], 4 - place[2])
    for place in sorted(PLANE[1:], key=hops, reverse=True):
        pl.semaphore_signal(barrier, inc=1, device_id=ident(place), device_id_type=MESH)
    for d in (2, 1, 3):
        pl.semaphore_signal(barrier, inc=1, device_id=ident(moved("z", d)), device_id_type=MESH)
    pl.semaphore_signal(barrier, inc=1, device_id=peer, device_id_type=MESH)

    pl.semaphore_wait(barrier, 19)

    def remote(src, dst, send, recv, device):
        return pltpu.make_async_remote_copy(
            src_ref=src, dst_ref=dst, send_sem=send, recv_sem=recv, device_id=device, device_id_type=MESH
        )

    swap = remote(bank.at[:, :, :, other], everything.at[pl.ds(grp * 8, 8)], swap_send, swap_recv, peer)
    swap.start()

    def columns(portion, core):
        first, width = PORTIONS[portion]
        return pl.ds(pl.multiple_of(core * HALF + first, LANES), width)

    def region(portion, stage, place, core, part=None):
        done = ORDERS[portion][:stage]
        cut = "x" if ORDERS[portion][2] == "y" else "y"

        def every(axis, value, size):
            if axis not in done:
                return value
            if part is not None and axis == cut:
                return pl.ds(2 * part, 2)
            return pl.ds(0, size)

        return signal.at[
            every("z", split_z[place[1]][0], 2), every("y", at_y(place), 4), every("z", split_z[place[1]][1], 2),
            every("x", at_x(place), 4), :, columns(portion, core),
        ]

    def wide(portion, stage, d):
        dst = region(portion, stage, HERE, grp)
        src = packed.at[:, columns(portion, grp)] if stage == 0 else dst
        at = (portion, stage, d - 1)
        return remote(src, dst, wide_send.at[at], wide_recv.at[at], ident(moved(ORDERS[portion][stage], d)))

    def relay(portion, part):
        axis = ORDERS[portion][2]
        got = region(portion, 2, moved(axis, -1 if part == 0 else 1), grp, part)
        at = (portion, 2 + part, 1)
        return remote(got, got, wide_send.at[at], wide_recv.at[at], ident(moved(axis, 1 if part == 0 else -1)))

    def incoming(portion, stage, d, core):
        axis = ORDERS[portion][min(stage, 2)]
        if stage < 2 or d != 2:
            part = None
        else:
            part = stage - 2
        return region(portion, min(stage, 2), moved(axis, -d), core, part), (portion, stage, d - 1)

    def arrived(portion, stage, d):
        got, at = incoming(portion, stage, d, grp)
        remote(got, got, wide_send.at[at], wide_recv.at[at], peer).wait_recv()
        remote(got, got, pass_send.at[at], pass_recv.at[at], peer).start()

    def pass_on(portions):
        for portion in portions:
            for d, part in ((1, 0), (3, 1)):
                arrived(portion, 2, d)
                relay(portion, part).start()

    def pass_last(portions):
        for portion in portions:
            for part in range(2):
                arrived(portion, 2 + part, 2)

    def pass_first(portions):
        for portion in portions:
            for d in (1, 3, 2):
                arrived(portion, 0, d)
            for d in (1, 3, 2):
                wide(portion, 1, d).start()

    def pass_second(portions):
        for portion in portions:
            for d in (1, 3, 2):
                arrived(portion, 1, d)
            for d in (1, 3):
                wide(portion, 2, d).start()

    own.wait()
    packed[0:4, :] = loaded[0, 0]
    packed[4:8, :] = loaded[0, 1]
    for portion in EARLY + LATE:
        for d in (1, 3, 2):
            wide(portion, 0, d).start()
    mine = pltpu.make_async_copy(packed, signal.at[det, here["y"], low_z, here["x"]], local_sem.at[1])
    mine.start()

    swap.wait_recv()
    keep.wait()
    for slot in range(16):
        wave = everything[assign[slot]]
        staged[slot, 0:4, :] = wave[0]
        staged[slot, 4:8, :] = wave[1]

    def far(d):
        to = shifted(d)
        return remote(
            staged.at[number(to)], tmpl.at[here["y"], low_z, here["x"], :, half],
            far_send.at[d], far_recv.at[d], ident(to),
        )

    def piece(place, plane, columns):
        return tmpl.at[at_y(place), plane, at_x(place), :, columns]

    def deep(place):
        got = piece(place, low_z, half)
        to = moved("z", 1 + 2 * (place[2] % 2))
        at = DEEP(place)
        return remote(got, got, deep_send.at[at], deep_recv.at[at], ident(to))

    def DEEP(place):
        return place[0] * 4 + place[2]

    def near(place, plane, columns):
        got = piece(place, low_z if plane == 0 else 1 - low_z, columns)
        at = (plane, DEEP(place))
        return remote(got, got, near_send.at[at], near_recv.at[at], peer)

    mine.wait()
    pass_first(EARLY)
    for d in FAR:
        far(d).start()
    kept = pltpu.make_async_copy(staged.at[number(HERE)], piece(HERE, low_z, half), local_sem.at[2])
    kept.start()
    prepare(part, det, slides, antenna, bands, net, ramp)
    power[...] = jnp.zeros_like(power)
    kept.wait()
    deep(HERE).start()
    near(HERE, 0, half).start()

    def got_far(order):
        for d in order:
            place = shifted(d, -1)
            got = piece(place, low_z, half)
            remote(got, got, far_send.at[d], far_recv.at[d], peer).wait_recv()
            deep(place).start()
            near(place, 0, half).start()

    def got_deep(order):
        for d in order:
            place = shifted(d, -1)
            got = piece(place, 1 - low_z, half)
            at = DEEP(place)
            remote(got, got, deep_send.at[at], deep_recv.at[at], peer).wait_recv()
            near(place, 1, half).start()

    events = ((0, 1), (0, 2), (0, 3), (1, 1), (1, 2), (1, 3), (2, 1), (2, 3), (2, 2), (3, 2))

    def complete(portions, events):
        for portion in portions:
            for stage, d in events:
                come, at = incoming(portion, stage, d, 1 - grp)
                remote(come, come, pass_send.at[at], pass_recv.at[at], peer).wait_recv()


    def complete_near(plane):
        for place in PLANE:
            near(place, plane, other).wait_recv()

    pass_second(EARLY)
    pass_first(LATE)
    got_far(FAR)
    for copy in tables:
        copy.wait()
    complete(EARLY, events[:6])
    complete_near(0)
    got_deep((0,) + FAR[:8])
    pass_on(EARLY)
    pass_second(LATE)
    got_deep(FAR[8:])
    pass_last(EARLY)

    complete_near(1)
    complete(EARLY, events[6:])

    def build(step, held):
        products(step, det, bounds, tmpl, signal, held, power)

    def pair(p, carry):
        first_stage(2 * p, held_a, bands, net, series)
        build(2 * p + 1, held_b)

        @pl.when(p == 2)
        def _():
            pass_last(LATE)
            complete(LATE, events[6:])

        first_stage(2 * p + 1, held_b, bands, net, series)
        build(2 * p + 2, held_a)
        return carry

    build(0, held_a)
    pass_on(LATE)
    complete(LATE, events[:6])
    lax.fori_loop(0, 3, pair, 0)
    first_stage(6, held_a, bands, net, series)
    build(7, held_b)
    first_stage(7, held_b, bands, net, series)
    total, shares = power_shares(power)
    response = sum(antenna[d, c] * antenna[d, c] for d in range(2) for c in range(2))

    def parts(i):
        return ((rows.at[0, i], chi.at[slot_at]), (rows.at[pl.ds(1, 2), i], net_out.at[slot_at]))

    def give(i, kind):
        src, dst = parts(i)[kind]
        return pltpu.make_async_remote_copy(
            src_ref=src, dst_ref=dst, send_sem=out_send.at[kind, i], recv_sem=out_recv.at[kind, slot_at],
            device_id={"grp": to_grp, "tm": target(i)}, device_id_type=MESH,
        )

    def block(step, carry):
        eb = (2 * lax.rem(here["y"], 2) + lax.div(here["x"], 2)) ^ (3 - step)
        def send(kind):
            for k in range(2):
                i = 2 * eb + k
                is_self = (target(i) == tm) & same_core

                @pl.when(is_self)
                def _():
                    src, dst = parts(i)[kind]
                    pltpu.make_async_copy(src, dst, out_recv.at[kind, slot_at]).start()

                @pl.when(jnp.logical_not(is_self))
                def _():
                    give(i, kind).start()

        second_stage(
            eb, total, shares, response, series, twiddle, turn, inner, last, weave, ramp, zbuf, bbuf, vbuf, rows,
            lambda: send(0),
        )
        send(1)
        return carry

    lax.fori_loop(0, 4, block, 0)

    swap.wait_send()

    for d, place in enumerate(PLANE):
        deep(place).wait_send()
        for plane in range(2):
            near(place, plane, half).wait_send()
        if d > 0:
            far(d).wait_send()
    for portion in EARLY + LATE:
        for stage, d in events:
            if stage < 2 or d != 2:
                wide(portion, stage, d).wait_send()
            else:
                relay(portion, stage - 2).wait_send()
            got, at = incoming(portion, stage, d, grp)
            remote(got, got, pass_send.at[at], pass_recv.at[at], peer).wait_send()

    def finish(i, carry):
        is_self = (target(i) == tm) & same_core
        for kind, dst in ((0, chi), (1, net_out)):
            pltpu.make_async_copy(dst.at[i], dst.at[i], out_recv.at[kind, i]).wait()

            @pl.when(jnp.logical_not(is_self))
            def _():
                give(i, kind).wait_send()
        return carry

    lax.fori_loop(0, 8, finish, 0)


def settle_kernel(chi, net, chi_out, net_out, chi_held, net_held, sem):
    moves = []
    for k in range(4):
        part = pl.ds(2 * k, 2)
        for i, (src, held, dst) in enumerate(((net, net_held, net_out), (chi, chi_held, chi_out))):
            moves.append((
                pltpu.make_async_copy(src.at[part], held.at[part], sem.at[0, i, k]),
                pltpu.make_async_copy(held.at[part], dst.at[part], sem.at[1, i, k]),
            ))
    for come, _ in moves:
        come.start()
    for come, go in moves:
        come.wait()
        go.start()
    for _, go in moves:
        go.wait()


def settle(chi, net):
    hbm = pl.BlockSpec(memory_space=pltpu.HBM)
    chi, net = pl.pallas_call(
        settle_kernel,
        out_shape=(jax.ShapeDtypeStruct(chi.shape, chi.dtype), jax.ShapeDtypeStruct(net.shape, net.dtype)),
        in_specs=[hbm, hbm],
        out_specs=[hbm, hbm],
        scratch_shapes=[
            pltpu.VMEM(chi.shape, chi.dtype), pltpu.VMEM(net.shape, net.dtype), pltpu.SemaphoreType.DMA((2, 2, 4)),
        ],
        compiler_params=pltpu.CompilerParams(vmem_limit_bytes=60 * 2**20),
        cost_estimate=pl.CostEstimate(flops=0, bytes_accessed=3 * 2**20, transcendentals=0),
    )(chi, net)
    return chi[None], net


def on_device(strain, bank, assignment, slides, bounds, antenna):
    dma = pltpu.SemaphoreType.DMA
    smem, hbm = pl.BlockSpec(memory_space=pltpu.SMEM), pl.BlockSpec(memory_space=pltpu.HBM)
    chi, net = pl.pallas_call(
        kernel,
        out_shape=(
            jax.ShapeDtypeStruct((8, 4, COLS), jnp.float32),
            jax.ShapeDtypeStruct((8, 2, 4, COLS), jnp.float32),
        ),
        in_specs=[smem] * 4 + [hbm] * 8,
        out_specs=[hbm, hbm],
        scratch_shapes=[
            pltpu.VMEM((4, 2, 4, 8, COLS), jnp.float32),
            pltpu.VMEM((2, 4, 2, 4, 8, COLS), jnp.float32),
            pltpu.VMEM((16, 2, 4, HALF), jnp.float32),
            pltpu.VMEM((16, 8, HALF), jnp.float32),
            pltpu.VMEM((1, 2, 4, COLS), jnp.float32),
            pltpu.VMEM((8, COLS), jnp.float32),
            pltpu.VMEM((3, 8, 4, COLS), jnp.float32),
            dma((3,)), dma, dma, dma((6, 4, 3)), dma((6, 4, 3)), dma((6, 4, 3)), dma((6, 4, 3)),
            dma((16,)), dma((16,)), dma((16,)), dma((16,)), dma((2, 16)), dma((2, 16)), dma((2, 8)), dma((2, 8)),
            dma((9,)),
        ] + compute_scratch(),
        compiler_params=pltpu.CompilerParams(collective_id=0, has_side_effects=True, vmem_limit_bytes=60 * 2**20),
        cost_estimate=pl.CostEstimate(flops=20 * 10**9, bytes_accessed=20 * 10**6, transcendentals=0),
    )(assignment, bounds, slides, antenna, bank, strain, *[jnp.asarray(table) for table in constant_tables()])
    return settle(chi, net)


def solution(mesh):
    P = jax.sharding.PartitionSpec
    return jax.shard_map(
        on_device,
        mesh=mesh,
        in_specs=(P("det", None, "tm", None), P("grp", None, "tm", None), P(), P(), P(), P()),
        out_specs=(P("det", "grp", "tm", None), P("grp", "det", "tm", None)),
        check_vma=False,
    )
```
